32 devices in a mesh: section: 2 (over core), dp: 16 (over z, y, x).
Axes of the slice: x: 2, y: 2, z: 4, core: 2. Of those that a mesh axis runs over, the one named last changes fastest.
Arguments:
- hidden_in: bfloat16 [16384, 768], P('dp')
- segment_ids: int32 [32, 512], P('dp'), may hold values from 0 to 8, as said below
- cls_positions: int32 [32, 8], P('dp'), may hold values from 0 to 361, as said below
- valid_counts: int32 [32], P('dp'), may hold values from 224 to 512, as said below
- proj_in: bfloat16 [2, 768, 2304], P('section'), may hold values from -0.21875 to 0.21875
- proj_bias: float32 [2, 2, 768], P('section'), may hold values from -1.2 to 1.2
- proj_out: bfloat16 [2, 768, 768], P('section'), may hold values from -1.25 to 1.25
- out_shift: float32 [2, 768], P('section'), may hold values from -1.2 to 1.2
- norm_gains: float32 [2, 2, 768], P('section'), may hold values from 0.25 to 1.75
- norm_shifts: float32 [2, 2, 768], P('section'), may hold values from -1.2 to 1.2
- widen: bfloat16 [2, 768, 3072], P('section'), may hold values from -0.21875 to 0.21875
- widen_bias: float32 [2, 3072], P('section'), may hold values from -1.2 to 1.2
- narrow: bfloat16 [2, 3072, 768], P('section'), may hold values from -0.109375 to 0.109375
- narrow_bias: float32 [2, 768], P('section'), may hold values from -1.2 to 1.2
- cotangent: bfloat16 [16384, 768], P('dp'), may hold values from -6 to 6
Outputs:
- section_cls: float32 [2, 32, 8, 768], P('section', 'dp')
- section_input_grads: float32 [2, 16384, 768], P('section', 'dp')
- proj_in_grad: float32 [2, 768, 2304], P('section')
- proj_bias_grad: float32 [2, 2, 768], P('section')
- proj_out_grad: float32 [2, 768, 768], P('section')
- out_shift_grad: float32 [2, 768], P('section')
- norm_gain_grad: float32 [2, 2, 768], P('section')
- norm_shift_grad: float32 [2, 2, 768], P('section')
- widen_grad: float32 [2, 768, 3072], P('section')
- widen_bias_grad: float32 [2, 3072], P('section')
- narrow_grad: float32 [2, 3072, 768], P('section')
- narrow_bias_grad: float32 [2, 768], P('section')
- stream_rms: float32 [2, 3], P('section')
The draws below stay inside these ranges and needn't reach their ends.
Inputs may be any that keep to these rules, and one draw needn't show every extreme that they name: `segment_ids`: each row holds 8 segments in order, numbered 0 up, a query then a passage in turn, followed by padding numbered 8 up to the row's end. `cls_positions`: the first position of each segment of the row, rising. `valid_counts`: the sum of the row's segment lengths; the positions from it on are padding. Some row has no padding.
All inputs are finite; a program needn't handle non-finite values.
Results may differ from the reference program's by a relative error of at most 0.019.
The reference program's roundings to bfloat16 on the way count: a program that leaves them out, or rounds other values in their place, can miss the bound.
Values may be sent and summed in bfloat16 or wider, within the bound.
A program may use at most 320 MiB of HBM per device.

```python
import jax
import jax.numpy as jnp
from jax import lax

D = 768
HEADS = 12
HEAD_DIM = 64
FF = 3072
ROW_LEN = 512
NSEG = 8
ROWS_ALL = 32
TOKENS = 16384
N_SECTION = 2


def segment_plan(key):
    queries = jax.random.randint(jax.random.fold_in(key, 11), (ROWS_ALL, NSEG // 2), ROW_LEN // 64, ROW_LEN // 16)
    passages = jax.random.randint(jax.random.fold_in(key, 12), (ROWS_ALL, NSEG // 2), ROW_LEN * 3 // 32, ROW_LEN * 5 // 32)
    lengths = jnp.stack([queries, passages], -1).reshape(ROWS_ALL, NSEG).astype(jnp.int32)
    longest = jnp.stack([jnp.full((NSEG // 2,), ROW_LEN // 16 - 1, jnp.int32), jnp.full((NSEG // 2,), ROW_LEN * 5 // 32 - 1, jnp.int32)], -1).reshape(NSEG).astype(jnp.int32)
    full_row = jax.random.randint(jax.random.fold_in(key, 13), (), 0, ROWS_ALL).astype(jnp.int32)
    row_numbers = jnp.arange(ROWS_ALL).astype(jnp.int32)
    is_full = (row_numbers == full_row)[:, None]
    lengths = jnp.where(is_full, longest[None, :], lengths).astype(jnp.int32)
    earlier = jnp.sum(lengths[:, :-1], -1).astype(jnp.int32)
    last_len = jnp.where(row_numbers == full_row, ROW_LEN - earlier, lengths[:, -1]).astype(jnp.int32)
    lengths = jnp.concatenate([lengths[:, :-1], last_len[:, None]], -1).astype(jnp.int32)
    ends = jnp.cumsum(lengths, -1).astype(jnp.int32)
    return ((ends - lengths).astype(jnp.int32), ends[:, -1].astype(jnp.int32))


def draw_segment_ids(key, part):
    starts, totals = segment_plan(key)
    positions = jnp.arange(ROW_LEN).astype(jnp.int32)
    numbers = jnp.sum((positions[None, None, :] >= starts[:, :, None]).astype(jnp.int32), axis=1) - 1
    return jnp.where(positions[None, :] < totals[:, None], numbers, NSEG).astype(jnp.int32)


def draw_cls_positions(key, part):
    starts, totals = segment_plan(key)
    return starts.astype(jnp.int32)


def draw_valid_counts(key, part):
    starts, totals = segment_plan(key)
    return totals.astype(jnp.int32)


def draw_hidden_in(key, part):
    starts, totals = segment_plan(key)
    key = jax.random.fold_in(key, 5)
    token_rows = (jnp.arange(TOKENS) // ROW_LEN).astype(jnp.int32)
    token_places = (jnp.arange(TOKENS) % ROW_LEN).astype(jnp.int32)
    row_totals = jnp.take(totals, token_rows)
    padding = jnp.where(token_places >= row_totals, 3.0, 1.0).astype(jnp.float32)
    rank = token_rows.astype(jnp.float32) / ROWS_ALL
    values = jax.random.normal(key, (TOKENS, D), jnp.float32)
    scales = 0.6 * 3.0 ** rank
    return (values * (scales * padding)[:, None]).astype(jnp.bfloat16)


def level_of(stream_key, extent, cuts, low, high):
    def one(position, parts):
        heights = jax.random.uniform(jax.random.fold_in(jax.random.fold_in(stream_key, 6), position), (parts,), jnp.float32, low / len(cuts), high / len(cuts))
        return jnp.repeat(jnp.exp(heights), extent[position] // parts).reshape((-1,) + (1,) * (len(extent) - position - 1))

    level = one(*cuts[0])
    for cut in cuts[1:]:
        level = level * one(*cut)
    return level


def gaussian(rng, shape, spread, bound, pieces=(), dtype=jnp.bfloat16):
    level = level_of(rng, shape, pieces, -0.22, 0.18) if pieces else 1.0
    entries = jax.random.normal(rng, shape, jnp.float32) * spread * level
    return jnp.minimum(jnp.maximum(entries, -bound), bound).astype(dtype)


def setup_inputs(seed: int = 0) -> dict:
    splits = jax.random.split(jax.random.key(seed), 16)
    return {
        "hidden_in": draw_hidden_in(jax.random.fold_in(splits[15], 71), 0),
        "segment_ids": draw_segment_ids(jax.random.fold_in(splits[15], 71), 0),
        "cls_positions": draw_cls_positions(jax.random.fold_in(splits[15], 71), 0),
        "valid_counts": draw_valid_counts(jax.random.fold_in(splits[15], 71), 0),
        "proj_in": gaussian(splits[4], (N_SECTION, D, 3 * D), D ** -0.5, 0.21875, ((0, 2),)),
        "proj_bias": gaussian(splits[5], (N_SECTION, 2, D), 0.3, 1.2, ((0, 2),), jnp.float32),
        "proj_out": gaussian(splits[6], (N_SECTION, D, D), (D // 32) ** -0.5, 1.25, ((0, 2),)),
        "out_shift": gaussian(splits[7], (N_SECTION, D), 0.3, 1.2, ((0, 2),), jnp.float32),
        "norm_gains": jnp.clip(1.0 + 0.15 * jax.random.normal(splits[8], (N_SECTION, 2, D), jnp.float32), 0.25, 1.75),
        "norm_shifts": gaussian(splits[9], (N_SECTION, 2, D), 0.3, 1.2, ((0, 2),), jnp.float32),
        "widen": gaussian(splits[10], (N_SECTION, D, FF), D ** -0.5, 0.21875, ((0, 2),)),
        "widen_bias": gaussian(splits[11], (N_SECTION, FF), 0.3, 1.2, ((0, 2),), jnp.float32),
        "narrow": gaussian(splits[12], (N_SECTION, FF, D), FF ** -0.5, 0.109375, ((0, 2),)),
        "narrow_bias": gaussian(splits[13], (N_SECTION, D), 0.3, 1.2, ((0, 2),), jnp.float32),
        "cotangent": gaussian(splits[14], (TOKENS, D), 1.0, 6.0, ((0, 16),)),
    }


@jax.custom_vjp
def low(v):
    return lax.optimization_barrier(v.astype(jnp.bfloat16)).astype(jnp.float32)

@jax.custom_vjp
def low_back(v):
    return v

def low_keep(v):
    return (low(v), None)

def low_pass(kept, grad):
    return (grad,)

def back_keep(v):
    return (v, None)

def back_low(kept, grad):
    return (low(grad),)
low.defvjp(low_keep, low_pass)
low_back.defvjp(back_keep, back_low)
EPSILON = 1e-12
MASKED = -1e+30
HIGHEST = lax.Precision.HIGHEST

def product(left, right):
    return jnp.dot(left, right, precision=HIGHEST)

def layer_norm(signal, gain, shift):
    centred = signal - lax.optimization_barrier(jnp.mean(signal, -1, keepdims=True))
    factor = lax.rsqrt(lax.optimization_barrier(jnp.mean(centred * centred, -1, keepdims=True)) + EPSILON)
    return centred * factor * gain + shift

def attend_row(block):
    queries, keys, values, segments = block
    scores = jnp.einsum('qhd,khd->hqk', queries, keys, precision=HIGHEST) * HEAD_DIM ** (-0.5)
    scores = low_back(scores)
    same_doc = segments[:, None] == segments[None, :]
    weights = jax.nn.softmax(jnp.where(same_doc[None], scores, MASKED), axis=-1)
    weights = low(weights)
    return jnp.einsum('hqk,khd->qhd', weights, values, precision=HIGHEST)

def layer(layer_in, segments, params):
    proj_in, proj_bias, proj_out, out_shift, norm_gains, norm_shifts, widen, widen_bias, narrow, narrow_bias = params
    group_rows = segments.shape[0]
    filler = jnp.zeros_like(proj_bias[0])
    qkv_all = product(layer_in, proj_in) + jnp.concatenate([proj_bias[0], filler, proj_bias[1]])
    qkv_all = low_back(low(qkv_all))
    qkv_parts = qkv_all.reshape(group_rows, ROW_LEN, 3, HEADS, HEAD_DIM)
    mixed_heads = lax.map(jax.checkpoint(attend_row), (qkv_parts[:, :, 0], qkv_parts[:, :, 1], qkv_parts[:, :, 2], segments))
    mixed_heads = low_back(low(mixed_heads.reshape(-1, D)))
    branch = low_back(product(mixed_heads, proj_out) + out_shift)
    first_out = layer_norm(layer_in + branch, norm_gains[0], norm_shifts[0])
    hidden = low_back(product(low(first_out), widen) + widen_bias)
    activated = low(jax.nn.gelu(hidden, approximate=False))
    feed_out = low_back(product(activated, narrow) + narrow_bias)
    stream = first_out + feed_out
    return (layer_norm(stream, norm_gains[1], norm_shifts[1]), (stream, branch, feed_out))

def network(taps, params, inputs, segments):
    layer_in = inputs + taps[0]
    outputs = []
    statistics = []
    for section_no in range(N_SECTION):
        if section_no > 0:
            layer_in = low_back(low(layer_in)) + taps[section_no]
        layer_out, stats = layer(layer_in, segments, tuple((weight_set[section_no] for weight_set in params)))
        outputs.append(layer_out)
        statistics.append(stats)
        layer_in = layer_out
    return (layer_in, (jnp.stack(outputs), statistics))

def reference(hidden_in, segment_ids, cls_positions, valid_counts, proj_in, proj_bias, proj_out, out_shift, norm_gains, norm_shifts, widen, widen_bias, narrow, narrow_bias, cotangent):
    params = tuple((array.astype(jnp.float32) for array in (proj_in, proj_bias, proj_out, out_shift, norm_gains, norm_shifts, widen, widen_bias, narrow, narrow_bias)))
    group = 8 if ROWS_ALL % 8 == 0 else 1
    steps_count = ROWS_ALL // group
    inputs = hidden_in.astype(jnp.float32).reshape(steps_count, group * ROW_LEN, D)
    upstreams = cotangent.astype(jnp.float32).reshape(steps_count, group * ROW_LEN, D)
    segments = segment_ids.reshape(steps_count, group, ROW_LEN)
    starts = cls_positions.reshape(steps_count, group, NSEG)
    counts = valid_counts.reshape(steps_count, group)

    def one_group(carry, item):
        grad_sums, square_sums, token_sum = carry
        group_in, group_seg, group_cls, group_count, group_up = item
        taps = jnp.zeros((N_SECTION, group * ROW_LEN, D), jnp.float32)
        last_out, backward, aux = jax.vjp(lambda tap_set, weight_sets: network(tap_set, weight_sets, group_in, group_seg), taps, params, has_aux=True)
        tap_grads, param_grads = backward(group_up)
        outputs, statistics = aux
        valid = (jnp.arange(ROW_LEN)[None, :] < group_count[:, None]).reshape(-1).astype(jnp.float32)[:, None]
        squares = jnp.stack([jnp.stack([jnp.sum(valid * summand * summand) for summand in stats]) for stats in statistics])
        picks = jnp.broadcast_to(group_cls[None, :, :, None], (N_SECTION, group, NSEG, D))
        cls_rows = jnp.take_along_axis(outputs.reshape(N_SECTION, group, ROW_LEN, D), picks, axis=2)
        grad_sums = jax.tree.map(lambda total, term: total + term, grad_sums, param_grads)
        token_sum = token_sum + jnp.sum(group_count.astype(jnp.float32))
        return ((grad_sums, square_sums + squares, token_sum), (cls_rows, tap_grads))
    start = (jax.tree.map(jnp.zeros_like, params), jnp.zeros((N_SECTION, 3), jnp.float32), jnp.zeros((), jnp.float32))
    final, stacked = lax.scan(one_group, start, (inputs, segments, starts, counts, upstreams))
    grad_sums, square_sums, token_sum = final
    cls_rows, tap_grads = stacked
    section_cls = jnp.transpose(cls_rows, (1, 0, 2, 3, 4)).reshape(N_SECTION, ROWS_ALL, NSEG, D)
    section_input_grads = jnp.transpose(tap_grads, (1, 0, 2, 3)).reshape(N_SECTION, TOKENS, D)
    stream_rms = jnp.sqrt(square_sums / (token_sum * D))
    return (section_cls, section_input_grads, grad_sums[0], grad_sums[1], grad_sums[2], grad_sums[3], grad_sums[4], grad_sums[5], grad_sums[6], grad_sums[7], grad_sums[8], grad_sums[9], stream_rms)
```

```python
import functools

import jax
import jax.numpy as jnp
from jax import lax
from jax.experimental import pallas as pl
from jax.experimental.pallas import tpu as pltpu
from jax.sharding import PartitionSpec as P

HEADS = 12
HEAD_DIM = 64
EPSILON = 1e-12
MASKED = -1e30
F32 = jnp.float32
BF16 = jnp.bfloat16
MIB = 2**20
SAVED = ("qkv", "e", "rinv", "mixed", "xhat1", "r", "firstb", "act", "slope", "xhat2")
ANY = pl.BlockSpec(memory_space=pl.ANY)
VMEM = pl.BlockSpec(memory_space=pltpu.VMEM)
SMEM = pl.BlockSpec(memory_space=pltpu.SMEM)


def mm(left, right):
    return jnp.dot(left, right, preferred_element_type=F32)


def mm_left_t(left, right):
    return lax.dot_general(left, right, (((0,), (0,)), ((), ())), preferred_element_type=F32)


def mm_right_t(left, right):
    return lax.dot_general(left, right, (((1,), (1,)), ((), ())), preferred_element_type=F32)


def lanes(start, size):
    return pl.ds(pl.multiple_of(start, size), size)


def gelu_and_slope(v):
    z = jnp.abs(v) * 0.7071067811865476
    t = 1.0 / (1.0 + 0.3275911 * z)
    e = jnp.exp(-0.5 * v * v)
    poly = t * (
        0.127414796 + t * (-0.142248368 + t * (0.7107068705 + t * (-0.7265760135 + t * 0.5307027145)))
    )
    tail = poly * e
    cdf = jnp.where(v >= 0, 1.0 - tail, tail)
    return v * cdf, cdf + v * e * 0.3989422804014327


def start_from(flag, pairs):
    for own, peer, target, sem in pairs:

        @pl.when(flag == 1)
        def _(own=own, target=target, sem=sem):
            pltpu.make_async_copy(own, target, sem).start()

        @pl.when(flag == 0)
        def _(peer=peer, target=target, sem=sem):
            pltpu.make_async_copy(peer, target, sem).start()


def forward_kernel(
    flags, cls_at, vec_own, vec_peer, seg_cols, seg_rows, h_any,
    win_own, wout_own, wid_own, nar_own, win_peer, wout_peer, wid_peer, nar_peer,
    qkv_o, e_o, rinv_o, mixed_o, xhat1_o, r_o, firstb_o, act_o, slope_o, xhat2_o, xb_o, small_o,
    h, win, wout, wid, nar, bias, qkv, e_v, rinv, mixed, xhat1, rr, first, firstb, act, slope, xhat2, xb, feed, vec,
    sems, out_sems,
):
    flag, row, valid, h_row = flags[0], flags[1], flags[2], flags[3]
    length, width = h.shape
    ff = wid.shape[1]
    start_from(flag, [
        (win_own, win_peer, win, sems.at[0]),
        (wout_own, wout_peer, wout, sems.at[1]),
        (wid_own, wid_peer, wid, sems.at[2]),
        (nar_own, nar_peer, nar, sems.at[3]),
    ])
    load_h = pltpu.make_async_copy(h_any.at[h_row], h, sems.at[4])
    load_h.start()
    stores = []

    def put(source, target):
        copy = pltpu.make_async_copy(source, target, out_sems.at[len(stores)])
        copy.start()
        stores.append(copy)

    vec[...] = jnp.where(flag == 1, vec_own[...], vec_peer[...])
    bias[...] = jnp.where(seg_cols[row][:, :1] == seg_rows[pl.ds(row, 1), :], 0.0, MASKED)
    load_h.wait()
    pltpu.make_async_copy(win_own, win, sems.at[0]).wait()

    tile = 256
    for part in range(3):
        shift = [vec[0:1, :], None, vec[1:2, :]][part]
        for j in range(width // tile):
            at = part * width + j * tile
            got = mm(h[...], win[:, at : at + tile])
            if shift is not None:
                got = got + shift[:, j * tile : (j + 1) * tile]
            got = got.astype(BF16)
            if part == 0:
                got = got * BF16(HEAD_DIM**-0.5)
            qkv[:, at : at + tile] = got
    put(qkv, qkv_o)

    low = lax.broadcasted_iota(jnp.int32, (length, 128), 1) < HEAD_DIM
    ones = jnp.ones((length, 128), BF16)

    def pair(p, carry):
        q = qkv[:, lanes(p * 128, 128)]
        k = qkv[:, lanes(width + p * 128, 128)]
        v = qkv[:, lanes(2 * width + p * 128, 128)]
        v1 = jnp.concatenate([v, ones], axis=1)
        outs = []
        for i in range(2):
            qm = jnp.where(low if i == 0 else ~low, q, BF16(0))
            s = mm_right_t(qm, k) + bias[...]
            top = jnp.max(s, axis=1, keepdims=True)
            e = jnp.exp(s - top).astype(BF16)
            e_v[2 * p + i] = e
            outs.append(mm(e, v1))
        r0 = 1.0 / outs[0][:, 128:]
        r1 = 1.0 / outs[1][:, 128:]
        m = jnp.where(low, outs[0][:, :128] * r0, outs[1][:, :128] * r1)
        mixed[:, lanes(p * 128, 128)] = m.astype(BF16)
        rinv[:, lanes(p * 128, 128)] = jnp.where(low, r0, r1)
        return carry

    lax.fori_loop(0, HEADS // 2, pair, 0)
    put(e_v, e_o)
    put(rinv, rinv_o)
    put(mixed, mixed_o)

    pltpu.make_async_copy(wout_own, wout, sems.at[1]).wait()
    block = 128
    sums = jnp.zeros((3, width), F32)

    def norm_first(b, total):
        rows = pl.ds(pl.multiple_of(b * block, block), block)
        ok = (lax.broadcasted_iota(jnp.int32, (block, 1), 0) + b * block < valid).astype(F32)
        branch = mm(mixed[rows, :], wout[...]) + vec[2:3, :]
        u = h[rows, :].astype(F32) + branch
        c = u - jnp.mean(u, axis=1, keepdims=True)
        f = lax.rsqrt(jnp.mean(c * c, axis=1, keepdims=True) + EPSILON)
        x = c * f
        xhat1[rows, :] = x
        rr[0, rows, :] = jnp.broadcast_to(f, (block, 128))
        y = x * vec[3:4, :] + vec[5:6, :]
        first[rows, :] = y
        firstb[rows, :] = y.astype(BF16)
        return total + jnp.sum(ok * branch * branch, axis=0, keepdims=True)

    branch_sum = lax.fori_loop(0, length // block, norm_first, jnp.zeros((1, width), F32))
    put(xhat1, xhat1_o)
    put(firstb, firstb_o)

    pltpu.make_async_copy(wid_own, wid, sems.at[2]).wait()
    pltpu.make_async_copy(nar_own, nar, sems.at[3]).wait()
    feed[...] = jnp.broadcast_to(vec[11:12, :], feed.shape)

    def widen(j):
        at = j * tile
        hid = mm(firstb[...], wid[:, lanes(at, tile)]) + vec[pl.ds(12 + j, 1), 0:tile]
        a, d = gelu_and_slope(hid)
        act[:, lanes(at, tile)] = a.astype(BF16)
        slope[:, lanes(at, tile)] = d.astype(BF16)

    def narrow(j):
        feed[...] += mm(act[:, lanes(j * tile, tile)], nar[lanes(j * tile, tile), :])

    widen(0)

    def ffn(j, carry):
        narrow(j - 1)
        widen(j)
        return carry

    lax.fori_loop(1, ff // tile, ffn, 0)
    put(act, act_o)
    put(slope, slope_o)
    narrow(ff // tile - 1)

    def norm_second(b, totals):
        rows = pl.ds(pl.multiple_of(b * block, block), block)
        ok = (lax.broadcasted_iota(jnp.int32, (block, 1), 0) + b * block < valid).astype(F32)
        fd = feed[rows, :]
        u = first[rows, :] + fd
        c = u - jnp.mean(u, axis=1, keepdims=True)
        f = lax.rsqrt(jnp.mean(c * c, axis=1, keepdims=True) + EPSILON)
        x = c * f
        xhat2[rows, :] = x
        rr[1, rows, :] = jnp.broadcast_to(f, (block, 128))
        y = x * vec[4:5, :] + vec[6:7, :]
        first[rows, :] = y
        xb[rows, :] = y.astype(BF16)
        return (
            totals[0] + jnp.sum(ok * u * u, axis=0, keepdims=True),
            totals[1] + jnp.sum(ok * fd * fd, axis=0, keepdims=True),
        )

    zero = jnp.zeros((1, width), F32)
    stream_sum, feed_sum = lax.fori_loop(0, length // block, norm_second, (zero, zero))
    put(xhat2, xhat2_o)
    put(rr, r_o)
    put(xb, xb_o)
    for i in range(8):
        small_o[i : i + 1, :] = first[pl.ds(cls_at[i], 1), :]
    small_o[8:9, :] = stream_sum
    small_o[9:10, :] = branch_sum
    small_o[10:11, :] = feed_sum
    small_o[11:16, :] = jnp.zeros((5, width), F32)
    for copy in stores:
        copy.wait()


def forward(flags, cls_at, vecs, seg_cols, seg_rows, h, own, peer):
    length = seg_rows.shape[1]
    width = h.shape[-1]
    ff = own[2].shape[1]
    saved = [
        ((length, 3 * width), BF16), ((HEADS, length, length), BF16), ((length, width), F32), ((length, width), BF16),
        ((length, width), F32), ((2, length, 128), F32), ((length, width), BF16), ((length, ff), BF16),
        ((length, ff), BF16), ((length, width), F32), ((length, width), BF16),
    ]
    names = (*SAVED, "xb")
    out = pl.pallas_call(
        forward_kernel,
        out_shape=[jax.ShapeDtypeStruct(s, d) for s, d in saved] + [jax.ShapeDtypeStruct((16, width), F32)],
        in_specs=[SMEM, SMEM, VMEM, VMEM, VMEM, VMEM] + [ANY] * 9,
        out_specs=[ANY] * len(saved) + [VMEM],
        scratch_shapes=[
            pltpu.VMEM((length, width), BF16),
            *[pltpu.VMEM(w.shape, BF16) for w in own],
            pltpu.VMEM((length, length), F32),
            pltpu.VMEM((length, 3 * width), BF16),
            pltpu.VMEM((HEADS, length, length), BF16),
            pltpu.VMEM((length, width), F32),
            pltpu.VMEM((length, width), BF16),
            pltpu.VMEM((length, width), F32),
            pltpu.VMEM((2, length, 128), F32),
            pltpu.VMEM((length, width), F32),
            pltpu.VMEM((length, width), BF16),
            pltpu.VMEM((length, ff), BF16),
            pltpu.VMEM((length, ff), BF16),
            pltpu.VMEM((length, width), F32),
            pltpu.VMEM((length, width), BF16),
            pltpu.VMEM((length, width), F32),
            pltpu.VMEM(vecs[0].shape, F32),
            pltpu.SemaphoreType.DMA((5,)),
            pltpu.SemaphoreType.DMA((11,)),
        ],
        compiler_params=pltpu.CompilerParams(vmem_limit_bytes=60 * MIB),
        cost_estimate=pl.CostEstimate(flops=9 * 10**9, bytes_accessed=40 * 10**6, transcendentals=5 * 10**6),
        name="forward_layer",
    )(flags, cls_at, vecs[0], vecs[1], seg_cols, seg_rows, h, *own, *peer)
    return dict(zip(names, out[:-1])), out[-1]


def backward_kernel(
    flags, vec_own, vec_peer, g_any, h_any, qkv_a, e_a, rinv_a, mixed_a, xhat1_a, r_a, firstb_a, act_a, slope_a, xhat2_a,
    win_own, wout_own, wid_own, nar_own, win_peer, wout_peer, wid_peer, nar_peer,
    grad_o, din_o, dinb_o, small_o,
    g, h, win, wout, wid, nar, qkv, e_v, rinv, mixed, xhat1, rr, firstb, act, slope, xhat2,
    vec, ds, dfeed, dh, dres, dbr, dm, dqkv, dinb, row_stage, col_stage, wbias,
    sems, e_sems, stage_sems, out_sems,
):
    flag, g_row, h_row = flags[0], flags[1], flags[2]
    length, width = h.shape
    ff = wid.shape[1]
    tile = 256
    block = 128
    loads = {}

    def load(name, source, target, i):
        loads[name] = pltpu.make_async_copy(source, target, sems.at[i])
        loads[name].start()

    load("g", g_any.at[g_row], g, 4)
    load("xhat2", xhat2_a, xhat2, 5)
    load("r", r_a, rr, 6)
    start_from(flag, [(nar_own, nar_peer, nar, sems.at[3])])
    load("act", act_a, act, 7)
    load("slope", slope_a, slope, 8)
    load("firstb", firstb_a, firstb, 9)
    start_from(flag, [(wid_own, wid_peer, wid, sems.at[2])])
    load("xhat1", xhat1_a, xhat1, 10)
    load("mixed", mixed_a, mixed, 11)
    start_from(flag, [(wout_own, wout_peer, wout, sems.at[1])])
    load("rinv", rinv_a, rinv, 12)
    load("qkv", qkv_a, qkv, 13)

    def load_e(p, slot):
        return pltpu.make_async_copy(e_a.at[pl.ds(2 * p, 2)], e_v.at[slot], e_sems.at[slot])

    load_e(0, 0).start()
    load("h", h_any.at[h_row], h, 14)
    start_from(flag, [(win_own, win_peer, win, sems.at[0])])

    vec[...] = jnp.where(flag == 1, vec_own[...], vec_peer[...])
    zero = jnp.zeros((1, width), F32)

    def norm_back(up, x, f):
        return f * (up - jnp.mean(up, axis=1, keepdims=True) - x * jnp.mean(up * x, axis=1, keepdims=True))

    loads["g"].wait()
    loads["xhat2"].wait()
    loads["r"].wait()

    def second(b, sums):
        rows = pl.ds(pl.multiple_of(b * block, block), block)
        up = g[rows, :].astype(F32)
        x = xhat2[rows, :]
        d = norm_back(up * vec[4:5, :], x, rr[1, rows, 0:1])
        ds[rows, :] = d
        db = d.astype(BF16)
        dfeed[rows, :] = db
        return (
            sums[0] + jnp.sum(up * x, axis=0, keepdims=True),
            sums[1] + jnp.sum(up, axis=0, keepdims=True),
            sums[2] + jnp.sum(db.astype(F32), axis=0, keepdims=True),
        )

    gain2, shift2, narrow_bias = lax.fori_loop(0, length // block, second, (zero, zero, zero))

    def stage_rows(n, value, target, first):
        slot = n % 2
        @pl.when(jnp.logical_not(first))
        def _():
            pltpu.make_async_copy(row_stage.at[slot], target, stage_sems.at[slot]).wait()
        row_stage[slot] = value.astype(BF16)
        pltpu.make_async_copy(row_stage.at[slot], target, stage_sems.at[slot]).start()

    def stage_cols(n, value, target, first):
        slot = n % 2
        @pl.when(jnp.logical_not(first))
        def _():
            pltpu.make_async_copy(col_stage.at[slot], target, stage_sems.at[2 + slot]).wait()
        col_stage[slot] = value.astype(BF16)
        pltpu.make_async_copy(col_stage.at[slot], target, stage_sems.at[2 + slot]).start()

    pltpu.make_async_copy(nar_own, nar, sems.at[3]).wait()
    loads["act"].wait()
    loads["slope"].wait()
    loads["firstb"].wait()

    def ffn(j, carry):
        at = lanes(j * tile, tile)
        da = mm_right_t(dfeed[...], nar[at, :])
        d = (slope[:, at].astype(F32) * da).astype(BF16)
        dh[:, at] = d
        wbias[pl.ds(j, 1), :] = jnp.sum(d.astype(F32), axis=0, keepdims=True)
        stage_rows(j, mm_left_t(act[:, at], dfeed[...]), grad_o.at[8 + j // 3, lanes((j % 3) * tile, tile), :], j < 2)
        stage_cols(j, mm_left_t(firstb[...], d), grad_o.at[4 + j // 3, :, lanes((j % 3) * tile, tile)], j < 2)
        return carry

    lax.fori_loop(0, ff // tile, ffn, 0)
    pltpu.make_async_copy(wid_own, wid, sems.at[2]).wait()

    def first_grad(j, carry):
        at = lanes(j * tile, tile)
        ds[:, at] = ds[:, at] + mm_right_t(dh[...], wid[at, :])
        return carry

    lax.fori_loop(0, width // tile, first_grad, 0)

    loads["xhat1"].wait()

    def first(b, sums):
        rows = pl.ds(pl.multiple_of(b * block, block), block)
        up = ds[rows, :]
        x = xhat1[rows, :]
        d = norm_back(up * vec[3:4, :], x, rr[0, rows, 0:1])
        dres[rows, :] = d
        db = d.astype(BF16)
        dbr[rows, :] = db
        return (
            sums[0] + jnp.sum(up * x, axis=0, keepdims=True),
            sums[1] + jnp.sum(up, axis=0, keepdims=True),
            sums[2] + jnp.sum(db.astype(F32), axis=0, keepdims=True),
        )

    gain1, shift1, out_shift = lax.fori_loop(0, length // block, first, (zero, zero, zero))

    loads["mixed"].wait()
    pltpu.make_async_copy(wout_own, wout, sems.at[1]).wait()
    loads["rinv"].wait()
    loads["qkv"].wait()

    def out_grad(j, carry):
        at = lanes(j * tile, tile)
        stage_cols(j, mm_left_t(mixed[...], dbr[:, at]), grad_o.at[3, :, at], j < 0)
        d = mm_right_t(dbr[...], wout[at, :]).astype(BF16).astype(F32)
        dm[:, at] = (d * rinv[:, at]).astype(BF16)
        return carry

    lax.fori_loop(0, width // tile, out_grad, 0)

    low = lax.broadcasted_iota(jnp.int32, (length, 128), 1) < HEAD_DIM

    def pair(p, carry):
        slot = p % 2
        @pl.when(p + 1 < HEADS // 2)
        def _():
            load_e(p + 1, 1 - slot).start()
        at_q, at_k, at_v = lanes(p * 128, 128), lanes(width + p * 128, 128), lanes(2 * width + p * 128, 128)
        q, k, v = qkv[:, at_q], qkv[:, at_k], qkv[:, at_v]
        d = dm[:, at_q]
        prod = d.astype(F32) * mixed[:, at_q].astype(F32)
        load_e(p, slot).wait()
        dq, dk, dv = [], [], []
        for i in range(2):
            mine = low if i == 0 else ~low
            delta = jnp.sum(jnp.where(mine, prod, 0.0), axis=1, keepdims=True)
            dp = mm_right_t(jnp.where(mine, d, BF16(0)), v)
            e = e_v[slot, i]
            s = (e.astype(F32) * (dp - delta)).astype(BF16)
            dq.append(mm(s, k))
            dk.append(mm_left_t(s, q))
            dv.append(mm_left_t(e, d))
        dqkv[:, at_q] = (jnp.where(low, dq[0], dq[1]) * HEAD_DIM**-0.5).astype(BF16)
        dqkv[:, at_k] = jnp.where(low, dk[0], dk[1]).astype(BF16)
        dqkv[:, at_v] = jnp.where(low, dv[0], dv[1]).astype(BF16)
        return carry

    lax.fori_loop(0, HEADS // 2, pair, 0)

    loads["h"].wait()

    def in_grad(j, carry):
        at = lanes(j * tile, tile)
        stage_cols(j + 1, mm_left_t(h[...], dqkv[:, at]), grad_o.at[j // 3, :, lanes((j % 3) * tile, tile)], j < 0)
        return carry

    lax.fori_loop(0, 3 * width // tile, in_grad, 0)
    pltpu.make_async_copy(win_own, win, sems.at[0]).wait()

    def input_grad(j, carry):
        at = lanes(j * tile, tile)
        d = dres[:, at] + mm_right_t(dqkv[...], win[at, :])
        dres[:, at] = d
        dinb[:, at] = d.astype(BF16)
        return carry

    lax.fori_loop(0, width // tile, input_grad, 0)
    out_f = pltpu.make_async_copy(dres, din_o, out_sems.at[0])
    out_b = pltpu.make_async_copy(dinb, dinb_o.at[0], out_sems.at[1])
    out_f.start()
    out_b.start()
    small_o[0:1, :] = jnp.sum(dqkv[:, 0:width].astype(F32), axis=0, keepdims=True)
    small_o[1:2, :] = jnp.sum(dqkv[:, 2 * width :].astype(F32), axis=0, keepdims=True)
    small_o[2:3, :] = out_shift
    small_o[3:4, :] = gain1
    small_o[4:5, :] = gain2
    small_o[5:6, :] = shift1
    small_o[6:7, :] = shift2
    for i in range(ff // tile):
        small_o[7 + i // 3 : 8 + i // 3, (i % 3) * tile : (i % 3 + 1) * tile] = wbias[i : i + 1, :]
    small_o[11:12, :] = narrow_bias
    small_o[12:16, :] = jnp.zeros((4, width), F32)
    for slot in range(2):
        pltpu.make_async_copy(row_stage.at[slot], grad_o.at[8, 0:tile, :], stage_sems.at[slot]).wait()
        pltpu.make_async_copy(col_stage.at[slot], grad_o.at[0, :, 0:tile], stage_sems.at[2 + slot]).wait()
    out_f.wait()
    out_b.wait()


def backward(flags, vecs, g, h, saved, own, peer):
    length, width = saved["xhat1"].shape
    ff = own[2].shape[1]
    return pl.pallas_call(
        backward_kernel,
        out_shape=[
            jax.ShapeDtypeStruct((12, width, width), BF16),
            jax.ShapeDtypeStruct((length, width), F32),
            jax.ShapeDtypeStruct((1, length, width), BF16),
            jax.ShapeDtypeStruct((16, width), F32),
        ],
        in_specs=[SMEM, VMEM, VMEM] + [ANY] * 20,
        out_specs=[ANY, ANY, ANY, VMEM],
        scratch_shapes=[
            pltpu.VMEM((length, width), BF16),
            pltpu.VMEM((length, width), BF16),
            *[pltpu.VMEM(w.shape, BF16) for w in own],
            pltpu.VMEM((length, 3 * width), BF16),
            pltpu.VMEM((2, 2, length, length), BF16),
            pltpu.VMEM((length, width), F32),
            pltpu.VMEM((length, width), BF16),
            pltpu.VMEM((length, width), F32),
            pltpu.VMEM((2, length, 128), F32),
            pltpu.VMEM((length, width), BF16),
            pltpu.VMEM((length, ff), BF16),
            pltpu.VMEM((length, ff), BF16),
            pltpu.VMEM((length, width), F32),
            pltpu.VMEM(vecs[0].shape, F32),
            pltpu.VMEM((length, width), F32),
            pltpu.VMEM((length, width), BF16),
            pltpu.VMEM((length, ff), BF16),
            pltpu.VMEM((length, width), F32),
            pltpu.VMEM((length, width), BF16),
            pltpu.VMEM((length, width), BF16),
            pltpu.VMEM((length, 3 * width), BF16),
            pltpu.VMEM((length, width), BF16),
            pltpu.VMEM((2, 256, width), BF16),
            pltpu.VMEM((2, width, 256), BF16),
            pltpu.VMEM((16, 256), F32),
            pltpu.SemaphoreType.DMA((15,)),
            pltpu.SemaphoreType.DMA((2,)),
            pltpu.SemaphoreType.DMA((4,)),
            pltpu.SemaphoreType.DMA((2,)),
        ],
        compiler_params=pltpu.CompilerParams(vmem_limit_bytes=60 * MIB),
        cost_estimate=pl.CostEstimate(flops=18 * 10**9, bytes_accessed=60 * 10**6, transcendentals=0),
        name="backward_layer",
    )(flags, vecs[0], vecs[1], g, h, *[saved[n] for n in SAVED], *own, *peer)


def swap_sections(array):
    return lax.ppermute(array, "section", [(0, 1), (1, 0)])


MESH = pl.DeviceIdType.MESH


def sum_plan(devices, rows):
    side = round((devices / 2) ** (1 / 3))
    extents = [side, side, devices // (side * side)]
    axes, stride = [], 1
    for extent in extents:
        steps, step = [], 1
        while step < extent:
            steps.append(stride * step)
            step *= 2
        axes.append(steps)
        stride *= extent
    x, y, z = axes
    unit = 16 * devices if rows % (16 * devices) == 0 else 8 * devices
    units = rows // unit
    last = round(units * 2 / 9)
    head = (units - last + 1) // 2
    counts = [head, units - last - head, last]
    plan, base = [], 0
    for count, order in zip(counts, (x + y + z, y + x + z, z + x + y)):
        plan.append((base, unit, count, order))
        base += unit * count
    return plan


def halves(rows, cols, stages):
    shapes = []
    for _ in range(stages):
        by_rows = rows >= 32
        rows, cols = (rows // 2, cols) if by_rows else (rows, cols // 2)
        shapes.append((rows, cols, by_rows))
    return shapes


def sum_kernel(plan, grad0, grad1, small_in, out, small_out, total, other, small_recv, small_acc, *rest):
    stages = len(plan[0][3])
    recvs = rest[: len(plan) * stages]
    load_sems, pair_sems, rs_sems, ag_sems, out_sems, small_sems = rest[len(plan) * stages :]
    section, me = lax.axis_index("section"), lax.axis_index("dp")
    width = total.shape[1]

    def bit_of(distance):
        return lax.rem(me // distance, 2)

    def partner(distance):
        return (section, me + distance * (1 - 2 * bit_of(distance)))

    peer = (1 - section, me)

    barrier = pltpu.get_barrier_semaphore()
    pl.semaphore_signal(barrier, inc=1, device_id=peer, device_id_type=MESH)
    for distance in plan[0][3]:
        pl.semaphore_signal(barrier, inc=1, device_id=partner(distance), device_id_type=MESH)
    pl.semaphore_wait(barrier, stages + 1)

    steps = max(count for _, _, count, _ in plan)

    def rows_at(part, k):
        base, unit, _, _ = plan[part]
        return pl.ds(pl.multiple_of(base + k * unit, 16), unit)

    def load(part, k, source):
        return pltpu.make_async_copy(source.at[rows_at(part, k)], total.at[rows_at(part, k)], load_sems.at[part, k])

    def trade(part, k, source):
        return pltpu.make_async_remote_copy(
            src_ref=source.at[rows_at(part, k)], dst_ref=other.at[rows_at(part, k)],
            send_sem=pair_sems.at[0, part, k], recv_sem=pair_sems.at[1, part, k],
            device_id=peer, device_id_type=MESH,
        )

    def each(count, k, body):
        pl.when((k >= 0) & (k < count))(body)

    def begin(k, carry):
        for part, (_, _, count, _) in enumerate(plan):

            def go(part=part):
                @pl.when(section == 0)
                def _():
                    load(part, k, grad0).start()
                    trade(part, k, grad1).start()

                @pl.when(section == 1)
                def _():
                    load(part, k, grad1).start()
                    trade(part, k, grad0).start()

            each(count, k, go)
        return carry

    lax.fori_loop(0, steps, begin, 0)

    def regions(part, k, stage):
        base, unit, _, order = plan[part]
        row, col = base + k * unit, 0
        for s, (rows, cols, by_rows) in enumerate(halves(unit, width, stages)):
            bit = bit_of(order[s])
            keep, send = bit, 1 - bit
            if by_rows:
                kept, sent = (row + keep * rows, rows, col, cols), (row + send * rows, rows, col, cols)
            else:
                kept, sent = (row, rows, col + keep * cols, cols), (row, rows, col + send * cols, cols)
            if s == stage:
                return kept, sent
            row, col = kept[0], kept[2]

    def view(ref, region):
        row, rows, col, cols = region
        if cols == width:
            return ref.at[pl.ds(pl.multiple_of(row, 16), rows)]
        return ref.at[pl.ds(pl.multiple_of(row, 16), rows), pl.ds(pl.multiple_of(col, 128), cols)]

    def reduce_copy(part, k, stage):
        _, sent = regions(part, k, stage)
        return pltpu.make_async_remote_copy(
            src_ref=view(total, sent), dst_ref=recvs[part * stages + stage].at[k],
            send_sem=rs_sems.at[0, part, stage, k], recv_sem=rs_sems.at[1, part, stage, k],
            device_id=partner(plan[part][3][stage]), device_id_type=MESH,
        )

    def gather_copy(part, k, stage):
        kept, _ = regions(part, k, stage)
        return pltpu.make_async_remote_copy(
            src_ref=view(other, kept), dst_ref=view(other, kept),
            send_sem=ag_sems.at[0, part, stage, k], recv_sem=ag_sems.at[1, part, stage, k],
            device_id=partner(plan[part][3][stage]), device_id_type=MESH,
        )

    def store(part, k):
        return pltpu.make_async_copy(other.at[rows_at(part, k)], out.at[rows_at(part, k)], out_sems.at[part, k])

    def add(region, source, target=total):
        row, rows, col, cols = region
        block = min(rows, 32)

        def body(i, carry):
            at = (pl.ds(pl.multiple_of(row + i * block, 16), block), pl.ds(pl.multiple_of(col, 128), cols))
            target[at] = total[at] + source[pl.ds(pl.multiple_of(i * block, 16), block), :]
            return carry

        lax.fori_loop(0, rows // block, body, 0)

    def task(part, k, stage):
        if stage == 0:
            load(part, k, grad0).wait()
            trade(part, k, grad0).wait_recv()
            base, unit, _, _ = plan[part]
            add((base + k * unit, unit, 0, width), other.at[rows_at(part, k)])
            reduce_copy(part, k, 0).start()
        elif stage <= stages:
            reduce_copy(part, k, stage - 1).wait_recv()
            kept, _ = regions(part, k, stage - 1)
            add(kept, recvs[part * stages + stage - 1].at[k], total if stage < stages else other)
            if stage < stages:
                reduce_copy(part, k, stage).start()
            else:
                gather_copy(part, k, stages - 1).start()
        else:
            past = 2 * stages - stage
            gather_copy(part, k, past).wait_recv()
            if past > 0:
                gather_copy(part, k, past - 1).start()
            else:
                store(part, k).start()

    small_acc[0] = small_in[...]

    def small_copy(stage):
        return pltpu.make_async_remote_copy(
            src_ref=small_acc.at[stage], dst_ref=small_recv.at[stage],
            send_sem=small_sems.at[0, stage], recv_sem=small_sems.at[1, stage],
            device_id=partner(plan[0][3][stage]), device_id_type=MESH,
        )

    def small_step(stage):
        if stage > 0:
            small_copy(stage - 1).wait_recv()
            small_acc[stage] = small_acc[stage - 1] + small_recv[stage - 1]
        if stage < stages:
            small_copy(stage).start()
        else:
            small_out[...] = small_acc[stages]

    def step(t, carry):
        for stage in range(2 * stages + 1):
            for part, (_, _, count, _) in enumerate(plan):
                each(count, t - stage, lambda part=part, stage=stage: task(part, t - stage, stage))
        for stage in range(stages + 1):
            pl.when(t == stage)(lambda stage=stage: small_step(stage))
        return carry

    lax.fori_loop(0, steps + 2 * stages, step, 0)

    def finish(k, carry):
        for part, (_, _, count, _) in enumerate(plan):

            def go(part=part):
                trade(part, k, grad0).wait_send()
                for stage in range(stages):
                    reduce_copy(part, k, stage).wait_send()
                    gather_copy(part, k, stage).wait_send()
                store(part, k).wait()

            each(count, k, go)
        return carry

    lax.fori_loop(0, steps, finish, 0)
    for stage in range(stages):
        small_copy(stage).wait_send()


def sum_gradients(grad0, grad1, small):
    devices = lax.axis_size("dp")
    shape = grad0.shape
    rows, width = shape[0] * shape[1], shape[2]
    plan = sum_plan(devices, rows)
    stages = len(plan[0][3])
    steps = max(count for _, _, count, _ in plan)
    recvs = [
        pltpu.VMEM((count, r, c), BF16)
        for _, unit, count, _ in plan
        for r, c, _ in halves(unit, width, stages)
    ]
    parts = len(plan)
    blocks, small = pl.pallas_call(
        functools.partial(sum_kernel, plan),
        out_shape=[jax.ShapeDtypeStruct((rows, width), BF16), jax.ShapeDtypeStruct(small.shape, F32)],
        in_specs=[ANY, ANY, VMEM],
        out_specs=[ANY, VMEM],
        scratch_shapes=[
            pltpu.VMEM((rows, width), BF16),
            pltpu.VMEM((rows, width), BF16),
            pltpu.VMEM((stages, *small.shape), F32),
            pltpu.VMEM((stages + 1, *small.shape), F32),
            *recvs,
            pltpu.SemaphoreType.DMA((parts, steps)),
            pltpu.SemaphoreType.DMA((2, parts, steps)),
            pltpu.SemaphoreType.DMA((2, parts, stages, steps)),
            pltpu.SemaphoreType.DMA((2, parts, stages, steps)),
            pltpu.SemaphoreType.DMA((parts, steps)),
            pltpu.SemaphoreType.DMA((2, stages)),
        ],
        compiler_params=pltpu.CompilerParams(collective_id=0, has_side_effects=True, vmem_limit_bytes=60 * MIB),
        cost_estimate=pl.CostEstimate(flops=10**7, bytes_accessed=60 * 10**6, transcendentals=0),
        name="sum_gradients",
    )(grad0.reshape(rows, width), grad1.reshape(rows, width), small)
    return blocks.reshape(shape), small


def local(
    hidden_in, segment_ids, cls_positions, valid_counts, proj_in, proj_bias, proj_out, out_shift, norm_gains,
    norm_shifts, widen, widen_bias, narrow, narrow_bias, cotangent,
):
    section = lax.axis_index("section")
    row_count, length = segment_ids.shape
    width = hidden_in.shape[1]
    own = (proj_in[0], proj_out[0], widen[0], narrow[0])
    tiles = widen_bias[0].reshape(-1, 256)
    vec_own = jnp.concatenate([
        proj_bias[0], out_shift, norm_gains[0], norm_shifts[0], jnp.zeros((4, width), F32), narrow_bias,
        jnp.pad(tiles, ((0, 0), (0, width - 256))),
    ])
    peer = tuple(swap_sections(w) for w in own)
    vecs = (vec_own, swap_sections(vec_own))
    row = section
    valid = valid_counts[row]
    cls_at = cls_positions[row]
    seg_cols = jnp.broadcast_to(segment_ids[:, :, None], (row_count, length, 128))
    h0 = hidden_in.reshape(row_count, length, width)
    g1 = cotangent.reshape(row_count, length, width)
    mine = [(section == layer).astype(jnp.int32) for layer in range(2)]
    none = jnp.zeros((), jnp.int32)

    saved0, small0 = forward(
        jnp.stack([mine[0], row, valid, row]), cls_at, vecs, seg_cols, segment_ids, h0, own, peer
    )
    h1 = saved0["xb"][None]
    saved1, small1 = forward(
        jnp.stack([mine[1], row, valid, none]), cls_at, vecs, seg_cols, segment_ids, h1, own, peer
    )
    grad1, din1, dinb1, back1 = backward(jnp.stack([mine[1], row, none]), vecs, g1, h1, saved1, own, peer)
    grad0, din0, _, back0 = backward(jnp.stack([mine[0], none, row]), vecs, dinb1, h0, saved0, own, peer)

    first = section == 0
    all0 = jnp.concatenate([small0, back0])
    all1 = jnp.concatenate([small1, back1])
    kept = jnp.where(first, all0, all1)
    got = swap_sections(jnp.where(first, all1, all0))
    section_cls = jnp.where(first, jnp.stack([kept[:8], got[:8]]), jnp.stack([got[:8], kept[:8]]))
    din_kept = jnp.where(first, din0, din1)
    din_got = swap_sections(jnp.where(first, din1, din0))
    input_grads = jnp.where(first, jnp.concatenate([din_kept, din_got]), jnp.concatenate([din_got, din_kept]))

    count = jnp.broadcast_to(jnp.sum(valid_counts.astype(F32)), (1, width))
    sums = jnp.concatenate([(kept + got)[8:], count, jnp.zeros((7, width), F32)])
    blocks, sums = sum_gradients(grad0, grad1, sums)
    d_in = jnp.concatenate([blocks[0], blocks[1], blocks[2]], axis=1).astype(F32)
    d_out = blocks[3].astype(F32)
    d_widen = jnp.concatenate([blocks[4], blocks[5], blocks[6], blocks[7]], axis=1).astype(F32)
    d_narrow = blocks[8:12].reshape(-1, width).astype(F32)
    squares, back, total = jnp.sum(sums[0:3], axis=1), sums[8:20], sums[24, 0]
    stream_rms = jnp.sqrt(squares / (total * width))
    return (
        section_cls[None],
        input_grads[None],
        d_in[None],
        back[0:2][None],
        d_out[None],
        back[2:3],
        back[3:5][None],
        back[5:7][None],
        d_widen[None],
        back[7:11].reshape(1, -1),
        d_narrow[None],
        back[11:12],
        stream_rms[None],
    )


def solution(mesh):
    placed = (
        P("dp", None),
        P("dp", None),
        P("dp", None),
        P("dp"),
        P("section", None, None),
        P("section", None, None),
        P("section", None, None),
        P("section", None),
        P("section", None, None),
        P("section", None, None),
        P("section", None, None),
        P("section", None),
        P("section", None, None),
        P("section", None),
        P("dp", None),
    )
    return jax.shard_map(
        local,
        mesh=mesh,
        in_specs=placed,
        out_specs=(
            P("section", "dp", None, None),
            P("section", "dp", None),
            P("section", None, None),
            P("section", None, None),
            P("section", None, None),
            P("section", None),
            P("section", None, None),
            P("section", None, None),
            P("section", None, None),
            P("section", None),
            P("section", None, None),
            P("section", None),
            P("section", None),
        ),
        check_vma=False,
    )
```

```python
import functools

import jax
import jax.numpy as jnp
from jax import lax
from jax.experimental import pallas as pl
from jax.experimental.pallas import tpu as pltpu
from jax.sharding import PartitionSpec as P

HEADS = 12
HEAD_DIM = 64
EPSILON = 1e-12
MASKED = -1e30
F32 = jnp.float32
BF16 = jnp.bfloat16
MIB = 2**20
SAVED = ("qkv", "e", "rinv", "mixed", "xhat1", "r", "firstb", "act", "slope", "xhat2")
ANY = pl.BlockSpec(memory_space=pl.ANY)
VMEM = pl.BlockSpec(memory_space=pltpu.VMEM)
SMEM = pl.BlockSpec(memory_space=pltpu.SMEM)


def mm(left, right):
    return jnp.dot(left, right, preferred_element_type=F32)


def mm_left_t(left, right):
    return lax.dot_general(left, right, (((0,), (0,)), ((), ())), preferred_element_type=F32)


def mm_right_t(left, right):
    return lax.dot_general(left, right, (((1,), (1,)), ((), ())), preferred_element_type=F32)


def lanes(start, size):
    return pl.ds(pl.multiple_of(start, size), size)


def gelu_and_slope(v):
    z = jnp.abs(v) * 0.7071067811865476
    t = 1.0 / (1.0 + 0.3275911 * z)
    e = jnp.exp(-0.5 * v * v)
    poly = t * (
        0.127414796 + t * (-0.142248368 + t * (0.7107068705 + t * (-0.7265760135 + t * 0.5307027145)))
    )
    tail = poly * e
    cdf = jnp.where(v >= 0, 1.0 - tail, tail)
    return v * cdf, cdf + v * e * 0.3989422804014327


def start_from(flag, pairs):
    for own, peer, target, sem in pairs:

        @pl.when(flag == 1)
        def _(own=own, target=target, sem=sem):
            pltpu.make_async_copy(own, target, sem).start()

        @pl.when(flag == 0)
        def _(peer=peer, target=target, sem=sem):
            pltpu.make_async_copy(peer, target, sem).start()


def forward_kernel(
    flags, cls_at, vec_own, vec_peer, seg_cols, seg_rows, h_any,
    win_own, wout_own, wid_own, nar_own, win_peer, wout_peer, wid_peer, nar_peer,
    qkv_o, e_o, rinv_o, mixed_o, xhat1_o, r_o, firstb_o, act_o, slope_o, xhat2_o, xb_o, small_o,
    h, win, wout, wid, nar, bias, qkv, e_v, rinv, mixed, xhat1, rr, first, firstb, act, slope, xhat2, xb, feed, vec,
    sems, out_sems,
):
    flag, row, valid, h_row = flags[0], flags[1], flags[2], flags[3]
    length, width = h.shape
    ff = wid.shape[1]
    start_from(flag, [
        (win_own, win_peer, win, sems.at[0]),
        (wout_own, wout_peer, wout, sems.at[1]),
        (wid_own, wid_peer, wid, sems.at[2]),
        (nar_own, nar_peer, nar, sems.at[3]),
    ])
    load_h = pltpu.make_async_copy(h_any.at[h_row], h, sems.at[4])
    load_h.start()
    stores = []

    def put(source, target):
        copy = pltpu.make_async_copy(source, target, out_sems.at[len(stores)])
        copy.start()
        stores.append(copy)

    vec[...] = jnp.where(flag == 1, vec_own[...], vec_peer[...])
    bias[...] = jnp.where(seg_cols[row][:, :1] == seg_rows[pl.ds(row, 1), :], 0.0, MASKED)
    load_h.wait()
    pltpu.make_async_copy(win_own, win, sems.at[0]).wait()

    tile = 256
    for part in range(3):
        shift = [vec[0:1, :], None, vec[1:2, :]][part]
        for j in range(width // tile):
            at = part * width + j * tile
            got = mm(h[...], win[:, at : at + tile])
            if shift is not None:
                got = got + shift[:, j * tile : (j + 1) * tile]
            got = got.astype(BF16)
            if part == 0:
                got = got * BF16(HEAD_DIM**-0.5)
            qkv[:, at : at + tile] = got
    put(qkv, qkv_o)

    low = lax.broadcasted_iota(jnp.int32, (length, 128), 1) < HEAD_DIM
    ones = jnp.ones((length, 128), BF16)

    def pair(p, carry):
        q = qkv[:, lanes(p * 128, 128)]
        k = qkv[:, lanes(width + p * 128, 128)]
        v = qkv[:, lanes(2 * width + p * 128, 128)]
        v1 = jnp.concatenate([v, ones], axis=1)
        outs = []
        for i in range(2):
            qm = jnp.where(low if i == 0 else ~low, q, BF16(0))
            s = mm_right_t(qm, k) + bias[...]
            top = jnp.max(s, axis=1, keepdims=True)
            e = jnp.exp(s - top).astype(BF16)
            e_v[2 * p + i] = e
            outs.append(mm(e, v1))
        r0 = 1.0 / outs[0][:, 128:]
        r1 = 1.0 / outs[1][:, 128:]
        m = jnp.where(low, outs[0][:, :128] * r0, outs[1][:, :128] * r1)
        mixed[:, lanes(p * 128, 128)] = m.astype(BF16)
        rinv[:, lanes(p * 128, 128)] = jnp.where(low, r0, r1)
        return carry

    lax.fori_loop(0, HEADS // 2, pair, 0)
    put(e_v, e_o)
    put(rinv, rinv_o)
    put(mixed, mixed_o)

    pltpu.make_async_copy(wout_own, wout, sems.at[1]).wait()
    block = 128
    sums = jnp.zeros((3, width), F32)

    def norm_first(b, total):
        rows = pl.ds(pl.multiple_of(b * block, block), block)
        ok = (lax.broadcasted_iota(jnp.int32, (block, 1), 0) + b * block < valid).astype(F32)
        branch = mm(mixed[rows, :], wout[...]) + vec[2:3, :]
        u = h[rows, :].astype(F32) + branch
        c = u - jnp.mean(u, axis=1, keepdims=True)
        f = lax.rsqrt(jnp.mean(c * c, axis=1, keepdims=True) + EPSILON)
        x = c * f
        xhat1[rows, :] = x
        rr[0, rows, :] = jnp.broadcast_to(f, (block, 128))
        y = x * vec[3:4, :] + vec[5:6, :]
        first[rows, :] = y
        firstb[rows, :] = y.astype(BF16)
        return total + jnp.sum(ok * branch * branch, axis=0, keepdims=True)

    branch_sum = lax.fori_loop(0, length // block, norm_first, jnp.zeros((1, width), F32))
    put(xhat1, xhat1_o)
    put(firstb, firstb_o)

    pltpu.make_async_copy(wid_own, wid, sems.at[2]).wait()
    pltpu.make_async_copy(nar_own, nar, sems.at[3]).wait()
    feed[...] = jnp.broadcast_to(vec[11:12, :], feed.shape)

    def widen(j):
        at = j * tile
        hid = mm(firstb[...], wid[:, lanes(at, tile)]) + vec[pl.ds(12 + j, 1), 0:tile]
        a, d = gelu_and_slope(hid)
        act[:, lanes(at, tile)] = a.astype(BF16)
        slope[:, lanes(at, tile)] = d.astype(BF16)

    def narrow(j):
        feed[...] += mm(act[:, lanes(j * tile, tile)], nar[lanes(j * tile, tile), :])

    widen(0)

    def ffn(j, carry):
        narrow(j - 1)
        widen(j)
        return carry

    lax.fori_loop(1, ff // tile, ffn, 0)
    put(act, act_o)
    put(slope, slope_o)
    narrow(ff // tile - 1)

    def norm_second(b, totals):
        rows = pl.ds(pl.multiple_of(b * block, block), block)
        ok = (lax.broadcasted_iota(jnp.int32, (block, 1), 0) + b * block < valid).astype(F32)
        fd = feed[rows, :]
        u = first[rows, :] + fd
        c = u - jnp.mean(u, axis=1, keepdims=True)
        f = lax.rsqrt(jnp.mean(c * c, axis=1, keepdims=True) + EPSILON)
        x = c * f
        xhat2[rows, :] = x
        rr[1, rows, :] = jnp.broadcast_to(f, (block, 128))
        y = x * vec[4:5, :] + vec[6:7, :]
        first[rows, :] = y
        xb[rows, :] = y.astype(BF16)
        return (
            totals[0] + jnp.sum(ok * u * u, axis=0, keepdims=True),
            totals[1] + jnp.sum(ok * fd * fd, axis=0, keepdims=True),
        )

    zero = jnp.zeros((1, width), F32)
    stream_sum, feed_sum = lax.fori_loop(0, length // block, norm_second, (zero, zero))
    put(xhat2, xhat2_o)
    put(rr, r_o)
    put(xb, xb_o)
    for i in range(8):
        small_o[i : i + 1, :] = first[pl.ds(cls_at[i], 1), :]
    small_o[8:9, :] = stream_sum
    small_o[9:10, :] = branch_sum
    small_o[10:11, :] = feed_sum
    small_o[11:12, :] = jnp.full((1, width), valid.astype(F32))
    small_o[12:16, :] = jnp.zeros((4, width), F32)
    for copy in stores:
        copy.wait()


def forward(flags, cls_at, vecs, seg_cols, seg_rows, h, own, peer):
    length = seg_rows.shape[1]
    width = h.shape[-1]
    ff = own[2].shape[1]
    saved = [
        ((length, 3 * width), BF16), ((HEADS, length, length), BF16), ((length, width), F32), ((length, width), BF16),
        ((length, width), F32), ((2, length, 128), F32), ((length, width), BF16), ((length, ff), BF16),
        ((length, ff), BF16), ((length, width), F32), ((length, width), BF16),
    ]
    names = (*SAVED, "xb")
    out = pl.pallas_call(
        forward_kernel,
        out_shape=[jax.ShapeDtypeStruct(s, d) for s, d in saved] + [jax.ShapeDtypeStruct((16, width), F32)],
        in_specs=[SMEM, SMEM, VMEM, VMEM, VMEM, VMEM] + [ANY] * 9,
        out_specs=[ANY] * len(saved) + [VMEM],
        scratch_shapes=[
            pltpu.VMEM((length, width), BF16),
            *[pltpu.VMEM(w.shape, BF16) for w in own],
            pltpu.VMEM((length, length), F32),
            pltpu.VMEM((length, 3 * width), BF16),
            pltpu.VMEM((HEADS, length, length), BF16),
            pltpu.VMEM((length, width), F32),
            pltpu.VMEM((length, width), BF16),
            pltpu.VMEM((length, width), F32),
            pltpu.VMEM((2, length, 128), F32),
            pltpu.VMEM((length, width), F32),
            pltpu.VMEM((length, width), BF16),
            pltpu.VMEM((length, ff), BF16),
            pltpu.VMEM((length, ff), BF16),
            pltpu.VMEM((length, width), F32),
            pltpu.VMEM((length, width), BF16),
            pltpu.VMEM((length, width), F32),
            pltpu.VMEM(vecs[0].shape, F32),
            pltpu.SemaphoreType.DMA((5,)),
            pltpu.SemaphoreType.DMA((11,)),
        ],
        compiler_params=pltpu.CompilerParams(vmem_limit_bytes=60 * MIB),
        cost_estimate=pl.CostEstimate(flops=9 * 10**9, bytes_accessed=40 * 10**6, transcendentals=5 * 10**6),
        name="forward_layer",
    )(flags, cls_at, vecs[0], vecs[1], seg_cols, seg_rows, h, *own, *peer)
    return dict(zip(names, out[:-1])), out[-1]


def backward_pieces(flag, g_at, h_at, ins, outs, scratch):
    (vec_own, vec_peer, qkv_a, e_a, rinv_a, mixed_a, xhat1_a, r_a, firstb_a, act_a, slope_a, xhat2_a,
     win_own, wout_own, wid_own, nar_own, win_peer, wout_peer, wid_peer, nar_peer) = ins
    grad_o, din_o, dinb_o, small_o = outs
    (g, h, win, wout, wid, nar, qkv, e_v, rinv, mixed, xhat1, rr, firstb, act, slope, xhat2,
     vec, ds, dfeed, dm, row_stage, col_stage, wbias, sums, sems, e_sems, stage_sems, out_sems) = scratch
    dh, dqkv, dbr, dres, dinb = slope, qkv, g, xhat2, dfeed
    length, width = h.shape
    ff = wid.shape[1]
    tile = 256
    block = 128

    def copy(source, target, i):
        return pltpu.make_async_copy(source, target, sems.at[i])

    plain = dict(
        g=(g_at, g, 4), xhat2=(xhat2_a, xhat2, 5), r=(r_a, rr, 6), act=(act_a, act, 7), slope=(slope_a, slope, 8),
        firstb=(firstb_a, firstb, 9), xhat1=(xhat1_a, xhat1, 10), mixed=(mixed_a, mixed, 11), rinv=(rinv_a, rinv, 12),
        qkv=(qkv_a, qkv, 13), h=(h_at, h, 14),
    )
    weights = dict(
        win=(win_own, win_peer, win, 0), wout=(wout_own, wout_peer, wout, 1), wid=(wid_own, wid_peer, wid, 2),
        nar=(nar_own, nar_peer, nar, 3),
    )

    def start(*names):
        for name in names:
            if name in plain:
                copy(*plain[name]).start()
            else:
                own, peer, target, i = weights[name]
                start_from(flag, [(own, peer, target, sems.at[i])])

    def wait(*names):
        for name in names:
            if name in plain:
                copy(*plain[name]).wait()
            else:
                own, _, target, i = weights[name]
                copy(own, target, i).wait()

    def load_e(p, slot):
        return pltpu.make_async_copy(e_a.at[pl.ds(2 * p, 2)], e_v.at[slot], e_sems.at[slot])

    def norm_back(up, x, f):
        return f * (up - jnp.mean(up, axis=1, keepdims=True) - x * jnp.mean(up * x, axis=1, keepdims=True))

    def prepare():
        start("g", "xhat2", "r", "nar", "act", "slope", "firstb", "wid", "xhat1", "mixed", "wout", "rinv", "qkv")
        load_e(0, 0).start()
        start("h", "win")
        vec[...] = jnp.where(flag == 1, vec_own[...], vec_peer[...])

    def send_out(stage, shift, n, value, target, first):
        slot = n % 2

        @pl.when(jnp.logical_not(first))
        def _():
            pltpu.make_async_copy(stage.at[slot], target, stage_sems.at[shift + slot]).wait()

        stage[slot] = value.astype(BF16)
        pltpu.make_async_copy(stage.at[slot], target, stage_sems.at[shift + slot]).start()

    def put_rows(n, value, target, first):
        send_out(row_stage, 0, n, value, target, first)

    def put_cols(n, value, target, first):
        send_out(col_stage, 2, n, value, target, first)

    def norms(source, x_ref, f_at, gain, target, target_b, where):
        zero = jnp.zeros((1, width), F32)

        def body(b, total):
            rows = pl.ds(pl.multiple_of(b * block, block), block)
            up = source[rows, :].astype(F32)
            x = x_ref[rows, :]
            d = norm_back(up * vec[gain : gain + 1, :], x, rr[f_at, rows, 0:1])
            target[rows, :] = d
            db = d.astype(BF16)
            target_b[rows, :] = db
            return (
                total[0] + jnp.sum(up * x, axis=0, keepdims=True),
                total[1] + jnp.sum(up, axis=0, keepdims=True),
                total[2] + jnp.sum(db.astype(F32), axis=0, keepdims=True),
            )

        got = lax.fori_loop(0, length // block, body, (zero, zero, zero))
        for i in range(3):
            sums[where + i : where + i + 1, :] = got[i]

    def second():
        wait("g", "xhat2", "r")
        norms(g, xhat2, 1, 4, ds, dfeed, 0)
        wait("nar", "act", "slope", "firstb")

    def ffn(j, carry):
        at = lanes(j * tile, tile)
        da = mm_right_t(dfeed[...], nar[at, :])
        d = (slope[:, at].astype(F32) * da).astype(BF16)
        dh[:, at] = d
        wbias[pl.ds(j, 1), :] = jnp.sum(d.astype(F32), axis=0, keepdims=True)
        put_rows(j, mm_left_t(act[:, at], dfeed[...]), grad_o.at[8 + j // 3, lanes((j % 3) * tile, tile), :], j < 2)
        put_cols(j, mm_left_t(firstb[...], d), grad_o.at[4 + j // 3, :, lanes((j % 3) * tile, tile)], j < 2)
        return carry

    def first():
        wait("wid")

        def body(j, carry):
            at = lanes(j * tile, tile)
            ds[:, at] = ds[:, at] + mm_right_t(dh[...], wid[at, :])
            return carry

        lax.fori_loop(0, width // tile, body, 0)
        wait("xhat1")
        norms(ds, xhat1, 0, 3, dres, dbr, 3)
        wait("mixed", "wout", "rinv", "qkv")

    def out_grad():
        def body(j, carry):
            at = lanes(j * tile, tile)
            put_cols(j, mm_left_t(mixed[...], dbr[:, at]), grad_o.at[3, :, at], j < 0)
            d = mm_right_t(dbr[...], wout[at, :]).astype(BF16).astype(F32)
            dm[:, at] = (d * rinv[:, at]).astype(BF16)
            return carry

        lax.fori_loop(0, width // tile, body, 0)

    def pair(p, carry):
        low = lax.broadcasted_iota(jnp.int32, (length, 128), 1) < HEAD_DIM
        slot = p % 2

        @pl.when(p + 1 < HEADS // 2)
        def _():
            load_e(p + 1, 1 - slot).start()

        at_q, at_k, at_v = lanes(p * 128, 128), lanes(width + p * 128, 128), lanes(2 * width + p * 128, 128)
        q, k, v = qkv[:, at_q], qkv[:, at_k], qkv[:, at_v]
        d = dm[:, at_q]
        prod = d.astype(F32) * mixed[:, at_q].astype(F32)
        load_e(p, slot).wait()
        dq, dk, dv = [], [], []
        for i in range(2):
            mine = low if i == 0 else ~low
            delta = jnp.sum(jnp.where(mine, prod, 0.0), axis=1, keepdims=True)
            dp = mm_right_t(jnp.where(mine, d, BF16(0)), v)
            e = e_v[slot, i]
            s = (e.astype(F32) * (dp - delta)).astype(BF16)
            dq.append(mm(s, k))
            dk.append(mm_left_t(s, q))
            dv.append(mm_left_t(e, d))
        dqkv[:, at_q] = (jnp.where(low, dq[0], dq[1]) * HEAD_DIM**-0.5).astype(BF16)
        dqkv[:, at_k] = jnp.where(low, dk[0], dk[1]).astype(BF16)
        dqkv[:, at_v] = jnp.where(low, dv[0], dv[1]).astype(BF16)
        return carry

    def in_grad():
        wait("h")

        def body(j, carry):
            at = lanes(j * tile, tile)
            put_cols(j + 1, mm_left_t(h[...], dqkv[:, at]), grad_o.at[j // 3, :, lanes((j % 3) * tile, tile)], j < 0)
            return carry

        lax.fori_loop(0, 3 * width // tile, body, 0)

    def input_grad():
        wait("win")

        def body(j, carry):
            at = lanes(j * tile, tile)
            d = dres[:, at] + mm_right_t(dqkv[...], win[at, :])
            dres[:, at] = d
            dinb[:, at] = d.astype(BF16)
            return carry

        lax.fori_loop(0, width // tile, body, 0)
        stores = [pltpu.make_async_copy(dres, din_o, out_sems.at[0])]
        if dinb_o is not None:
            stores.append(pltpu.make_async_copy(dinb, dinb_o.at[0], out_sems.at[1]))
        for store in stores:
            store.start()
        small_o[0:1, :] = jnp.sum(dqkv[:, 0:width].astype(F32), axis=0, keepdims=True)
        small_o[1:2, :] = jnp.sum(dqkv[:, 2 * width :].astype(F32), axis=0, keepdims=True)
        small_o[2:3, :] = sums[5:6, :]
        small_o[3:4, :] = sums[3:4, :]
        small_o[4:5, :] = sums[0:1, :]
        small_o[5:6, :] = sums[4:5, :]
        small_o[6:7, :] = sums[1:2, :]
        for i in range(ff // tile):
            small_o[7 + i // 3 : 8 + i // 3, (i % 3) * tile : (i % 3 + 1) * tile] = wbias[i : i + 1, :]
        small_o[11:12, :] = sums[2:3, :]
        small_o[12:16, :] = jnp.zeros((4, width), F32)
        for slot in range(2):
            pltpu.make_async_copy(row_stage.at[slot], grad_o.at[8, 0:tile, :], stage_sems.at[slot]).wait()
            pltpu.make_async_copy(col_stage.at[slot], grad_o.at[0, :, 0:tile], stage_sems.at[2 + slot]).wait()
        for store in stores:
            store.wait()

    def tiles(low, high):
        lax.fori_loop(low, high, ffn, 0)

    def pairs(low, high):
        lax.fori_loop(low, high, pair, 0)

    third, half = ff // tile // 3, HEADS // 6
    return prepare, [
        lambda: (second(), tiles(0, third)),
        lambda: tiles(third, 2 * third),
        lambda: tiles(2 * third, 3 * third),
        first,
        lambda: (out_grad(), pairs(0, half)),
        lambda: pairs(half, 2 * half),
        lambda: pairs(2 * half, 3 * half),
        in_grad,
        input_grad,
    ]


def backward_scratch(length, width, weights, vec):
    ff = weights[2].shape[1]
    return [
        pltpu.VMEM((length, width), BF16),
        pltpu.VMEM((length, width), BF16),
        *[pltpu.VMEM(w.shape, BF16) for w in weights],
        pltpu.VMEM((length, 3 * width), BF16),
        pltpu.VMEM((2, 2, length, length), BF16),
        pltpu.VMEM((length, width), F32),
        pltpu.VMEM((length, width), BF16),
        pltpu.VMEM((length, width), F32),
        pltpu.VMEM((2, length, 128), F32),
        pltpu.VMEM((length, width), BF16),
        pltpu.VMEM((length, ff), BF16),
        pltpu.VMEM((length, ff), BF16),
        pltpu.VMEM((length, width), F32),
        pltpu.VMEM(vec.shape, F32),
        pltpu.VMEM((length, width), F32),
        pltpu.VMEM((length, width), BF16),
        pltpu.VMEM((length, width), BF16),
        pltpu.VMEM((2, 256, width), BF16),
        pltpu.VMEM((2, width, 256), BF16),
        pltpu.VMEM((16, 256), F32),
        pltpu.VMEM((8, width), F32),
        pltpu.SemaphoreType.DMA((15,)),
        pltpu.SemaphoreType.DMA((2,)),
        pltpu.SemaphoreType.DMA((4,)),
        pltpu.SemaphoreType.DMA((2,)),
    ]


BACKWARD_SCRATCH = 28


def backward_kernel(flags, vec_own, vec_peer, g_any, h_any, *rest):
    ins = (vec_own, vec_peer, *rest[:18])
    prepare, pieces = backward_pieces(
        flags[0], g_any.at[flags[1]], h_any.at[flags[2]], ins, rest[18:22], rest[22:]
    )
    prepare()
    for piece in pieces:
        piece()


def backward(flags, vecs, g, h, saved, own, peer):
    length, width = saved["xhat1"].shape
    return pl.pallas_call(
        backward_kernel,
        out_shape=[
            jax.ShapeDtypeStruct((12, width, width), BF16),
            jax.ShapeDtypeStruct((length, width), F32),
            jax.ShapeDtypeStruct((1, length, width), BF16),
            jax.ShapeDtypeStruct((16, width), F32),
        ],
        in_specs=[SMEM, VMEM, VMEM] + [ANY] * 20,
        out_specs=[ANY, ANY, ANY, VMEM],
        scratch_shapes=backward_scratch(length, width, own, vecs[0]),
        compiler_params=pltpu.CompilerParams(vmem_limit_bytes=60 * MIB),
        cost_estimate=pl.CostEstimate(flops=18 * 10**9, bytes_accessed=60 * 10**6, transcendentals=0),
        name="backward_layer",
    )(flags, vecs[0], vecs[1], g, h, *[saved[n] for n in SAVED], *own, *peer)


def swap_sections(array):
    return lax.ppermute(array, "section", [(0, 1), (1, 0)])


MESH = pl.DeviceIdType.MESH


def sum_plan(devices, rows):
    side = round((devices / 2) ** (1 / 3))
    extents = [side, side, devices // (side * side)]
    axes, stride = [], 1
    for extent in extents:
        steps, step = [], 1
        while step < extent:
            steps.append(stride * step)
            step *= 2
        axes.append(steps)
        stride *= extent
    x, y, z = axes
    unit = 256 if devices <= 16 else 128
    halves = rows // (unit // 2)
    last = 2 * round(halves * 0.194 / 2)
    head = (halves - last) // 4
    shapes = [(unit, head, x + y + z), (unit, (halves - last) // 2 - head, y + x + z), (unit // 2, last, z + x + y)]
    plan, base = [], 0
    for rows_of, count, order in shapes:
        plan.append((base, rows_of, count, order))
        base += rows_of * count
    return plan


def halvings(unit, width, stages):
    rows, cols, steps = unit // 2, width, []
    for _ in range(stages):
        if rows >= 32:
            kind, rows = "rows", rows // 2
        elif cols == width:
            kind, cols = "cols", cols // 2
        else:
            kind = "full"
        steps.append((kind, rows, cols))
    return steps


class GradientSum:
    def __init__(self, plan, slots, width, grads, out, buffers, sems):
        self.plan, self.slots, self.width, self.grads, self.out = plan, slots, width, grads, out
        self.stages = len(plan[0][3])
        self.steps = [halvings(unit, width, self.stages) for _, unit, _, _ in plan]
        self.total, self.other, self.recvs, self.fulls = buffers
        self.load_sems, self.pair_sems, self.rs_sems, self.ag_sems, self.end_sems, self.free, self.full_free = sems
        self.section, self.me = lax.axis_index("section"), lax.axis_index("dp")
        self.peer = (1 - self.section, self.me)
        self.length = max(2 * count for _, _, count, _ in plan) + 2 * self.stages + 3

    def bit(self, part, stage):
        return lax.rem(self.me // self.plan[part][3][stage], 2)

    def partner(self, part, stage):
        return (self.section, self.me + self.plan[part][3][stage] * (1 - 2 * self.bit(part, stage)))

    def barrier(self):
        barrier = pltpu.get_barrier_semaphore()
        for device in [self.peer] + [self.partner(0, stage) for stage in range(self.stages)]:
            pl.semaphore_signal(barrier, inc=1, device_id=device, device_id_type=MESH)
        pl.semaphore_wait(barrier, self.stages + 1)

    def slot(self, k):
        return lax.rem(k, self.slots)

    def half(self, ref, part, k, which):
        base, unit, count, _ = self.plan[part]
        row = base + lax.rem(k, count) * unit + which * (unit // 2)
        return ref.at[row // self.width, pl.ds(pl.multiple_of(lax.rem(row, self.width), 16), unit // 2)]

    def load(self, part, k, source):
        slot = self.slot(k)
        return pltpu.make_async_copy(
            self.half(source, part, k, self.section), self.total[part].at[slot], self.load_sems.at[part, slot]
        )

    def trade(self, part, k, source):
        slot = self.slot(k)
        return pltpu.make_async_remote_copy(
            src_ref=self.half(source, part, k, 1 - self.section), dst_ref=self.other[part].at[slot],
            send_sem=self.pair_sems.at[0, part, slot], recv_sem=self.pair_sems.at[1, part, slot],
            device_id=self.peer, device_id_type=MESH,
        )

    def regions(self, part, stage):
        row, col = 0, 0
        rows, cols = self.plan[part][1] // 2, self.width
        if stage < 0:
            return (row, rows, col, cols), None
        for s in range(stage + 1):
            kind, rows, cols = self.steps[part][s]
            keep = self.bit(part, s)
            sent_row, sent_col = row, col
            if kind == "rows":
                row, sent_row = row + keep * rows, row + (1 - keep) * rows
            elif kind == "cols":
                col, sent_col = col + keep * cols, col + (1 - keep) * cols
        return (row, rows, col, cols), (sent_row, rows, sent_col, cols)

    def view(self, ref, slot, region):
        row, rows, col, cols = region
        at = pl.ds(pl.multiple_of(row, 16), rows)
        if cols == self.width:
            return ref.at[slot, at]
        return ref.at[slot, at, pl.ds(pl.multiple_of(col, 128), cols)]

    def held(self, part, stage, slot):
        fulls = [s for s in range(stage + 1) if self.steps[part][s][0] == "full"]
        if fulls:
            return self.fulls[part][fulls[-1]].at[slot]
        return self.view(self.total[part], slot, self.regions(part, stage)[0])

    def reduce_copy(self, part, k, stage):
        slot = self.slot(k)
        if self.steps[part][stage][0] == "full":
            source = self.held(part, stage - 1, slot)
        else:
            source = self.view(self.total[part], slot, self.regions(part, stage)[1])
        return pltpu.make_async_remote_copy(
            src_ref=source, dst_ref=self.recvs[part][stage].at[slot],
            send_sem=self.rs_sems.at[0, part, stage, slot], recv_sem=self.rs_sems.at[1, part, stage, slot],
            device_id=self.partner(part, stage), device_id_type=MESH,
        )

    def start_reduce(self, part, k, stage):
        if self.steps[part][stage][0] == "full":

            @pl.when(k >= self.slots)
            def _():
                pl.semaphore_wait(self.full_free.at[part, stage], 1)

        self.reduce_copy(part, k, stage).start()

    def gather_copy(self, part, k, stage):
        slot = self.slot(k)
        place = self.view(self.other[part], slot, self.regions(part, stage)[0])
        return pltpu.make_async_remote_copy(
            src_ref=place, dst_ref=place,
            send_sem=self.ag_sems.at[0, part, stage, slot], recv_sem=self.ag_sems.at[1, part, stage, slot],
            device_id=self.partner(part, stage), device_id_type=MESH,
        )

    def gathers(self, part, stage):
        return stage >= 0 and self.steps[part][stage][0] != "full"

    def keep(self, part, k):
        slot = self.slot(k)
        return pltpu.make_async_copy(
            self.other[part].at[slot], self.half(self.out, part, k, self.section), self.end_sems.at[0, part, slot]
        )

    def hand_over(self, part, k):
        slot = self.slot(k)
        place = self.half(self.out, part, k, self.section)
        return pltpu.make_async_remote_copy(
            src_ref=self.other[part].at[slot], dst_ref=place,
            send_sem=self.end_sems.at[0, part, slot], recv_sem=self.end_sems.at[1, part, slot],
            device_id=self.peer, device_id_type=MESH,
        )

    def owned(self, part, k):
        return (k < self.plan[part][2]) == (self.section == 1)

    def add(self, target, left, right, rows):
        block = min(rows, 64)

        def body(i, carry):
            at = pl.ds(pl.multiple_of(i * block, 16), block)
            target[at, :] = left[at, :] + right[at, :]
            return carry

        lax.fori_loop(0, rows // block, body, 0)

    def retire(self, part, k):
        self.trade(part, k, self.grads[0]).wait_send()
        for stage in range(self.stages):
            self.reduce_copy(part, k, stage).wait_send()
            if self.gathers(part, stage):
                self.gather_copy(part, k, stage).wait_send()
        mine = self.owned(part, k)
        pl.when(mine)(lambda: self.keep(part, k).wait())
        pl.when(jnp.logical_not(mine))(lambda: self.hand_over(part, k).wait_send())

    def task(self, part, k, stage):
        last = self.stages - 1
        slot = self.slot(k)
        if stage == 0:

            @pl.when(k >= self.slots)
            def _():
                self.retire(part, k - self.slots)
                pl.semaphore_signal(self.free.at[part], inc=1, device_id=self.peer, device_id_type=MESH)
                pl.semaphore_wait(self.free.at[part], 1)

            first = k < self.plan[part][2]

            @pl.when(first)
            def _():
                self.load(part, k, self.grads[1]).start()
                self.trade(part, k, self.grads[1]).start()

            @pl.when(jnp.logical_not(first))
            def _():
                self.load(part, k, self.grads[0]).start()
                self.trade(part, k, self.grads[0]).start()

        elif stage == 1:
            self.load(part, k, self.grads[0]).wait()
            self.trade(part, k, self.grads[0]).wait_recv()
            rows = self.plan[part][1] // 2
            total = self.total[part].at[slot]
            self.add(total, total, self.other[part].at[slot], rows)
            self.start_reduce(part, k, 0)
        elif stage <= last + 2:
            s = stage - 2
            self.reduce_copy(part, k, s).wait_recv()
            kind, rows, _ = self.steps[part][s]
            kept, _ = self.regions(part, s)
            left = self.held(part, s - 1, slot) if kind == "full" else self.view(self.total[part], slot, kept)
            if s == last:
                target = self.view(self.other[part], slot, kept)
            else:
                target = self.held(part, s, slot)
            self.add(target, left, self.recvs[part][s].at[slot], rows)
            if kind == "full":

                @pl.when(k + self.slots < 2 * self.plan[part][2])
                def _():
                    pl.semaphore_signal(
                        self.full_free.at[part, s], inc=1, device_id=self.partner(part, s), device_id_type=MESH
                    )

            if s < last:
                self.start_reduce(part, k, s + 1)
            elif self.gathers(part, last):
                self.gather_copy(part, k, last).start()
        elif stage <= 2 * last + 3:
            s = 2 * last + 3 - stage
            if self.gathers(part, s):
                self.gather_copy(part, k, s).wait_recv()
            if s == 0:
                mine = self.owned(part, k)
                pl.when(mine)(lambda: self.keep(part, k).start())
                pl.when(jnp.logical_not(mine))(lambda: self.hand_over(part, k).start())
            elif self.gathers(part, s - 1):
                self.gather_copy(part, k, s - 1).start()
        else:
            pl.when(self.owned(part, k))(lambda: self.hand_over(part, k).wait_recv())

    def step(self, t):
        for stage in range(2 * self.stages + 3):
            for part, (_, _, count, _) in enumerate(self.plan):
                k = t - stage
                pl.when((k >= 0) & (k < 2 * count))(lambda part=part, stage=stage, k=k: self.task(part, k, stage))

    def finish(self):
        for part, (_, _, count, _) in enumerate(self.plan):

            def body(k, carry, part=part):
                self.retire(part, k)
                return carry

            lax.fori_loop(max(2 * count - self.slots, 0), 2 * count, body, 0)


def sum_scratch(plan, slots, width):
    stages = len(plan[0][3])
    steps = [halvings(unit, width, stages) for _, unit, _, _ in plan]
    parts = len(plan)
    shapes = []
    for _, unit, _, _ in plan:
        shapes += [pltpu.VMEM((slots, unit // 2, width), BF16)] * 2
    for step in steps:
        shapes += [pltpu.VMEM((slots, rows, cols), BF16) for _, rows, cols in step]
        shapes += [pltpu.VMEM((slots, rows, cols), BF16) for kind, rows, cols in step[:-1] if kind == "full"]
    shapes += [
        pltpu.SemaphoreType.DMA((parts, slots)),
        pltpu.SemaphoreType.DMA((2, parts, slots)),
        pltpu.SemaphoreType.DMA((2, parts, stages, slots)),
        pltpu.SemaphoreType.DMA((2, parts, stages, slots)),
        pltpu.SemaphoreType.DMA((2, parts, slots)),
        pltpu.SemaphoreType.REGULAR((parts,)),
        pltpu.SemaphoreType.REGULAR((parts, stages)),
    ]

    def split(refs):
        refs = list(refs)
        total, other = [], []
        for _ in plan:
            total.append(refs.pop(0))
            other.append(refs.pop(0))
        recvs, fulls = [], []
        for step in steps:
            recvs.append([refs.pop(0) for _ in step])
            fulls.append({s: refs.pop(0) for s in range(stages - 1) if step[s][0] == "full"})
        return (total, other, recvs, fulls), refs

    return shapes, split


def backward_sum_kernel(plan, slots, split, *refs):
    refs = list(refs)
    take = lambda n: [refs.pop(0) for _ in range(n)]
    vec_own, vec_peer, small0, all1, g_any, h_any = take(6)
    ins = (vec_own, vec_peer, *take(18))
    grad1, din1 = take(2)
    out, grad0, din0, din_got, small_got, small_sum, small_mine = take(7)
    back = take(BACKWARD_SCRATCH)
    back_small, small_send, small_acc, small_recv, small_sems, din_sems = take(6)
    section = lax.axis_index("section")
    width = din0.shape[1]
    total = GradientSum(plan, slots, width, (grad0, grad1), out, *split(refs))
    flag = (section == 0).astype(jnp.int32)
    prepare, pieces = backward_pieces(
        flag, g_any.at[0], h_any.at[section], ins, (grad0, din0, None, back_small), back
    )

    def din_copy(source):
        return pltpu.make_async_remote_copy(
            src_ref=source, dst_ref=din_got, send_sem=din_sems.at[0], recv_sem=din_sems.at[1],
            device_id=total.peer, device_id_type=MESH,
        )

    def small_trade():
        return pltpu.make_async_remote_copy(
            src_ref=small_send, dst_ref=small_got, send_sem=small_sems.at[0, total.stages],
            recv_sem=small_sems.at[1, total.stages], device_id=total.peer, device_id_type=MESH,
        )

    def small_copy(stage):
        return pltpu.make_async_remote_copy(
            src_ref=small_acc.at[stage], dst_ref=small_recv.at[stage], send_sem=small_sems.at[0, stage],
            recv_sem=small_sems.at[1, stage], device_id=total.partner(0, stage), device_id_type=MESH,
        )

    def small_start():
        pl.when(section == 1)(lambda: din_copy(din0).start())
        all0 = jnp.concatenate([small0[...], back_small[...]])
        one = all1[...]
        small_mine[...] = jnp.where(section == 0, all0, one)
        small_send[...] = jnp.where(section == 0, one, all0)
        small_trade().start()

    def small_step(stage):
        if stage == 0:
            small_trade().wait_recv()
            small_acc[0] = small_mine[8:, :] + small_got[8:, :]
        else:
            small_copy(stage - 1).wait_recv()
            small_acc[stage] = small_acc[stage - 1] + small_recv[stage - 1]
        if stage < total.stages:
            small_copy(stage).start()
        else:
            small_sum[...] = small_acc[stage]

    total.barrier()
    prepare()
    pl.when(section == 0)(lambda: din_copy(din1).start())

    events = list(pieces) + [small_start] + [functools.partial(small_step, s) for s in range(total.stages + 1)]

    def body(t, carry):
        total.step(t)
        for i, event in enumerate(events):
            pl.when(t == i)(lambda event=event: event() and None)
        return carry

    lax.fori_loop(0, total.length, body, 0)
    total.finish()
    small_trade().wait_send()
    for stage in range(total.stages):
        small_copy(stage).wait_send()
    din_copy(din0).wait_send()
    din_copy(din0).wait_recv()


def backward_sum(vecs, g, h, saved, own, peer, grad1, din1, small0, all1):
    length, width = saved["xhat1"].shape
    devices = lax.axis_size("dp")
    plan = sum_plan(devices, grad1.shape[0] * width)
    stages = len(plan[0][3])
    slots = 2 * stages + 4
    shapes, split = sum_scratch(plan, slots, width)
    sums = (24, width)
    return pl.pallas_call(
        functools.partial(backward_sum_kernel, plan, slots, split),
        out_shape=[
            jax.ShapeDtypeStruct(grad1.shape, BF16),
            jax.ShapeDtypeStruct(grad1.shape, BF16),
            jax.ShapeDtypeStruct((length, width), F32),
            jax.ShapeDtypeStruct((length, width), F32),
            jax.ShapeDtypeStruct((32, width), F32),
            jax.ShapeDtypeStruct(sums, F32),
            jax.ShapeDtypeStruct((32, width), F32),
        ],
        in_specs=[VMEM] * 4 + [ANY] * 22,
        out_specs=[ANY] * 4 + [VMEM] * 3,
        scratch_shapes=[
            *backward_scratch(length, width, own, vecs[0]),
            pltpu.VMEM((16, width), F32),
            pltpu.VMEM((32, width), F32),
            pltpu.VMEM((stages + 1, *sums), F32),
            pltpu.VMEM((stages, *sums), F32),
            pltpu.SemaphoreType.DMA((2, stages + 1)),
            pltpu.SemaphoreType.DMA((2,)),
            *shapes,
        ],
        compiler_params=pltpu.CompilerParams(collective_id=0, has_side_effects=True, vmem_limit_bytes=63 * MIB),
        cost_estimate=pl.CostEstimate(flops=18 * 10**9, bytes_accessed=120 * 10**6, transcendentals=0),
        name="backward_and_sum",
    )(vecs[0], vecs[1], small0, all1, g, h, *[saved[n] for n in SAVED], *own, *peer, grad1, din1)


def finish_kernel(
    flags, blocks, din0, din1, din_got, small_mine, small_got, small_sum,
    cls_o, input_o, in_o, bias_o, out_o, out_shift_o, gain_o, shift_o, widen_o, widen_bias_o, narrow_o, narrow_bias_o, rms_o,
    dins, wide, sems,
):
    block = pl.program_id(0)
    section = flags[0]
    length, width = din_got.shape
    got_row = 1 - section

    def rows(row):
        return input_o.at[0, pl.ds(pl.multiple_of(row * length, 16), length)]

    got_copy = pltpu.make_async_copy(din_got, rows(got_row), sems.at[0])
    own_copies = [pltpu.make_async_copy(din, rows(section), sems.at[1]) for din in (din0, din1)]

    @pl.when(block == 0)
    def _():
        got_copy.start()
        for layer in range(2):
            pl.when(section == layer)(own_copies[layer].start)
        cls_o[0, section] = small_mine[0:8, :]
        cls_o[0, got_row] = small_got[0:8, :]
        bias_o[0] = small_sum[8:10, :]
        out_shift_o[...] = small_sum[10:11, :]
        gain_o[0] = small_sum[11:13, :]
        shift_o[0] = small_sum[13:15, :]
        for i in range(4):
            widen_bias_o[0:1, i * width : (i + 1) * width] = small_sum[15 + i : 16 + i, :]
        narrow_bias_o[...] = small_sum[19:20, :]
        squares = jnp.sum(small_sum[0:3, :], axis=1, keepdims=True)
        rms_o[...] = jnp.sqrt(squares / (small_sum[3:4, 0:1] * width))

    def target(index):
        if index < 3:
            return in_o.at[0, :, index * width : (index + 1) * width]
        if index == 3:
            return out_o.at[0]
        if index < 8:
            return widen_o.at[0, :, (index - 4) * width : (index - 3) * width]
        return narrow_o.at[0, (index - 8) * width : (index - 7) * width, :]

    slot = lax.rem(block, 2)
    for index in range(12):

        @pl.when(block == index)
        def _(index=index):
            if index >= 2:
                pltpu.make_async_copy(wide.at[slot], target(index - 2), sems.at[2 + index % 2]).wait()
            wide[slot] = blocks[0].astype(F32)
            pltpu.make_async_copy(wide.at[slot], target(index), sems.at[2 + index % 2]).start()
            if index == 11:
                for i in (10, 11):
                    pltpu.make_async_copy(wide.at[i % 2], target(i), sems.at[2 + i % 2]).wait()
                got_copy.wait()
                own_copies[0].wait()


def finish(section, blocks, din0, din1, din_got, small_mine, small_got, small_sum):
    length, width = din_got.shape
    shapes = [
        (1, 2, 8, width), (1, 2 * length, width), (1, width, 3 * width), (1, 2, width), (1, width, width), (1, width),
        (1, 2, width), (1, 2, width), (1, width, 4 * width), (1, 4 * width), (1, 4 * width, width), (1, width), (3, 1),
    ]
    big = (1, 2, 4, 8, 10)
    whole = lambda shape: pl.BlockSpec(shape, lambda i: (0,) * len(shape))
    return pl.pallas_call(
        finish_kernel,
        grid=(12,),
        out_shape=[jax.ShapeDtypeStruct(s, F32) for s in shapes],
        in_specs=[SMEM, pl.BlockSpec((1, width, width), lambda i: (i, 0, 0)), ANY, ANY, ANY]
        + [whole(a.shape) for a in (small_mine, small_got, small_sum)],
        out_specs=[ANY if i in big else whole(s) for i, s in enumerate(shapes)],
        scratch_shapes=[
            pltpu.VMEM((8, 128), F32),
            pltpu.VMEM((2, width, width), F32),
            pltpu.SemaphoreType.DMA((4,)),
        ],
        compiler_params=pltpu.CompilerParams(vmem_limit_bytes=32 * MIB),
        cost_estimate=pl.CostEstimate(flops=10**7, bytes_accessed=46 * 10**6, transcendentals=0),
        name="finish",
    )(section[None], blocks, din0, din1, din_got, small_mine, small_got, small_sum)


def local(
    hidden_in, segment_ids, cls_positions, valid_counts, proj_in, proj_bias, proj_out, out_shift, norm_gains,
    norm_shifts, widen, widen_bias, narrow, narrow_bias, cotangent,
):
    section = lax.axis_index("section")
    row_count, length = segment_ids.shape
    width = hidden_in.shape[1]
    own = (proj_in[0], proj_out[0], widen[0], narrow[0])
    tiles = widen_bias[0].reshape(-1, 256)
    vec_own = jnp.concatenate([
        proj_bias[0], out_shift, norm_gains[0], norm_shifts[0], jnp.zeros((4, width), F32), narrow_bias,
        jnp.pad(tiles, ((0, 0), (0, width - 256))),
    ])
    peer = tuple(swap_sections(w) for w in own)
    vecs = (vec_own, swap_sections(vec_own))
    row = section
    valid = valid_counts[row]
    cls_at = cls_positions[row]
    seg_cols = jnp.broadcast_to(segment_ids[:, :, None], (row_count, length, 128))
    h0 = hidden_in.reshape(row_count, length, width)
    g1 = cotangent.reshape(row_count, length, width)
    mine = [(section == layer).astype(jnp.int32) for layer in range(2)]
    none = jnp.zeros((), jnp.int32)

    saved0, small0 = forward(
        jnp.stack([mine[0], row, valid, row]), cls_at, vecs, seg_cols, segment_ids, h0, own, peer
    )
    h1 = saved0["xb"][None]
    saved1, small1 = forward(
        jnp.stack([mine[1], row, valid, none]), cls_at, vecs, seg_cols, segment_ids, h1, own, peer
    )
    grad1, din1, dinb1, back1 = backward(jnp.stack([mine[1], row, none]), vecs, g1, h1, saved1, own, peer)
    blocks, _, din0, din_got, small_got, small_sum, small_mine = backward_sum(
        vecs, dinb1, h0, saved0, own, peer, grad1, din1, small0, jnp.concatenate([small1, back1])
    )
    outs = finish(section, blocks, din0, din1, din_got, small_mine, small_got, small_sum)
    return (*outs[:-1], outs[-1].reshape(1, 3))


def solution(mesh):
    placed = (
        P("dp", None),
        P("dp", None),
        P("dp", None),
        P("dp"),
        P("section", None, None),
        P("section", None, None),
        P("section", None, None),
        P("section", None),
        P("section", None, None),
        P("section", None, None),
        P("section", None, None),
        P("section", None),
        P("section", None, None),
        P("section", None),
        P("dp", None),
    )
    return jax.shard_map(
        local,
        mesh=mesh,
        in_specs=placed,
        out_specs=(
            P("section", "dp", None, None),
            P("section", "dp", None),
            P("section", None, None),
            P("section", None, None),
            P("section", None, None),
            P("section", None),
            P("section", None, None),
            P("section", None, None),
            P("section", None, None),
            P("section", None),
            P("section", None, None),
            P("section", None),
            P("section", None),
        ),
        check_vma=False,
    )
```

```python
import functools

import jax
import jax.numpy as jnp
from jax import lax
from jax.experimental import pallas as pl
from jax.experimental.pallas import tpu as pltpu
from jax.sharding import PartitionSpec as P

HEADS = 12
HEAD_DIM = 64
EPSILON = 1e-12
MASKED = -1e30
F32 = jnp.float32
BF16 = jnp.bfloat16
MIB = 2**20
TILE = 256
BLOCK = 128
ANY = pl.BlockSpec(memory_space=pl.ANY)
VMEM = pl.BlockSpec(memory_space=pltpu.VMEM)
SMEM = pl.BlockSpec(memory_space=pltpu.SMEM)
MESH = pl.DeviceIdType.MESH
OUT, IN = 8, 9


def mm(left, right):
    return jnp.dot(left, right, preferred_element_type=F32)


def mm_left_t(left, right):
    return lax.dot_general(left, right, (((0,), (0,)), ((), ())), preferred_element_type=F32)


def mm_right_t(left, right):
    return lax.dot_general(left, right, (((1,), (1,)), ((), ())), preferred_element_type=F32)


def lanes(start, size):
    return pl.ds(pl.multiple_of(start, size), size)


def rows_of(b, size):
    return pl.ds(pl.multiple_of(b * size, size), size)


def gelu_and_slope(v):
    z = jnp.abs(v) * 0.7071067811865476
    t = 1.0 / (1.0 + 0.3275911 * z)
    e = jnp.exp(-0.5 * v * v)
    poly = t * (
        0.127414796 + t * (-0.142248368 + t * (0.7107068705 + t * (-0.7265760135 + t * 0.5307027145)))
    )
    tail = poly * e
    cdf = jnp.where(v >= 0, 1.0 - tail, tail)
    return v * cdf, cdf + v * e * 0.3989422804014327


def norm_back(up, x, f):
    return f * (up - jnp.mean(up, axis=1, keepdims=True) - x * jnp.mean(up * x, axis=1, keepdims=True))


class Refs:
    def __init__(self, **refs):
        self.__dict__.update(refs)


SAVED = ("qkv", "rinv", "mixed", "xhat1", "rr", "firstb", "act", "slope", "xhat2")
WEIGHTS = ("win", "wout", "wid", "nar")


class Compute:
    def __init__(self, v, a, sems, section, valid, cls_at):
        self.v, self.a, self.sems = v, a, sems
        self.section, self.valid, self.cls_at = section, valid, cls_at
        self.length, self.width = v.h.shape
        self.ff = v.wid.shape[1]

    def weight_copy(self, i):
        return pltpu.make_async_copy(self.a.own[i].at[0], getattr(self.v, WEIGHTS[i]), self.sems.weights.at[i])

    def weight_sent(self, i):
        return pltpu.make_async_remote_copy(
            src_ref=self.a.own[i].at[0], dst_ref=getattr(self.v, WEIGHTS[i]), send_sem=self.sems.sent.at[i],
            recv_sem=self.sems.arrived.at[i], device_id=self.a.other, device_id_type=MESH,
        )

    def start_weight(self, layer, name, use):
        i = WEIGHTS.index(name)

        @pl.when(self.section == layer)
        def _():
            self.weight_copy(i).start()
            if use == 2:
                self.weight_sent(i).wait_send()
            if use > 0:
                pl.semaphore_wait(self.sems.free.at[i], 1)
            self.weight_sent(i).start()

        if use > 0:

            @pl.when(self.section != layer)
            def _():
                pl.semaphore_signal(self.sems.free.at[i], inc=1, device_id=self.a.other, device_id_type=MESH)

    def wait_weight(self, layer, name):
        i = WEIGHTS.index(name)
        pl.when(self.section == layer)(lambda: self.weight_copy(i).wait())
        pl.when(self.section != layer)(lambda: self.weight_sent(i).wait_recv())

    def saving(self, name):
        i = SAVED.index(name)
        return pltpu.make_async_copy(getattr(self.v, name), self.a.saved[i], self.sems.saved.at[i])

    def restoring(self, name):
        i = SAVED.index(name)
        return pltpu.make_async_copy(self.a.saved[i], getattr(self.v, name), self.sems.saved.at[i])

    def load_input(self, layer_input):
        return pltpu.make_async_copy(layer_input.at[self.rows()], self.v.h, self.sems.h.at[0])

    def load_cotangent(self, cotangent):
        return pltpu.make_async_copy(cotangent.at[self.rows()], self.v.g, self.sems.h.at[1])

    def rows(self):
        return pl.ds(pl.multiple_of(self.section * self.length, self.length), self.length)

    def e_store(self, layer, p, slot):
        return pltpu.make_async_copy(
            self.v.e.at[slot], self.a.e.at[layer, pl.ds(2 * p, 2)], self.sems.e.at[slot]
        )

    def e_load(self, layer, p, slot):
        return pltpu.make_async_copy(
            self.a.e.at[layer, pl.ds(2 * p, 2)], self.v.e.at[slot], self.sems.e.at[slot]
        )

    def e_drain(self, layer):
        for slot in range(2):
            self.e_store(layer, 0, slot).wait()

    def forward(self, layer, small):
        v, width = self.v, self.width
        vec = v.vec.at[layer]
        again = layer == 1

        def before(*names):
            if again:
                for name in names:
                    self.saving(name).wait()

        def done(*names):
            if not again:
                for name in names:
                    self.saving(name).start()

        self.wait_weight(layer, "win")
        before("qkv")
        for part in range(3):
            shift = [vec[0:1, :], None, vec[1:2, :]][part]
            for j in range(width // TILE):
                at = part * width + j * TILE
                got = mm(v.h[...], v.win[:, at : at + TILE])
                if shift is not None:
                    got = got + shift[:, j * TILE : (j + 1) * TILE]
                got = got.astype(BF16)
                if part == 0:
                    got = got * BF16(HEAD_DIM**-0.5)
                v.qkv[:, at : at + TILE] = got
        done("qkv")
        if again:
            self.e_drain(0)
        else:
            self.start_weight(1, "win", 1)
        before("rinv", "mixed")
        low = lax.broadcasted_iota(jnp.int32, (self.length, 128), 1) < HEAD_DIM
        ones = jnp.ones((self.length, 128), BF16)

        def pair(p, carry):
            slot = lax.rem(p, 2)

            @pl.when(p >= 2)
            def _():
                self.e_store(layer, p, slot).wait()

            q = v.qkv[:, lanes(p * 128, 128)]
            k = v.qkv[:, lanes(width + p * 128, 128)]
            values = jnp.concatenate([v.qkv[:, lanes(2 * width + p * 128, 128)], ones], axis=1)
            outs = []
            for i in range(2):
                qm = jnp.where(low if i == 0 else ~low, q, BF16(0))
                s = mm_right_t(qm, k) + v.bias[...]
                top = jnp.max(s, axis=1, keepdims=True)
                e = jnp.exp(s - top).astype(BF16)
                v.e[slot, i] = e
                outs.append(mm(e, values))
            self.e_store(layer, p, slot).start()
            r0 = 1.0 / outs[0][:, 128:]
            r1 = 1.0 / outs[1][:, 128:]
            m = jnp.where(low, outs[0][:, :128] * r0, outs[1][:, :128] * r1)
            v.mixed[:, lanes(p * 128, 128)] = m.astype(BF16)
            v.rinv[:, lanes(p * 128, 128)] = jnp.where(low, r0, r1)
            return carry

        lax.fori_loop(0, HEADS // 2, pair, 0)
        done("rinv", "mixed")

        self.wait_weight(layer, "wout")
        before("xhat1", "rr", "firstb")

        def mask(b):
            place = lax.broadcasted_iota(jnp.int32, (BLOCK, 1), 0) + b * BLOCK
            return (place < self.valid).astype(F32)

        def norm_first(b, total):
            rows = rows_of(b, BLOCK)
            branch = mm(v.mixed[rows, :], v.wout[...]) + vec[2:3, :]
            u = v.h[rows, :].astype(F32) + branch
            c = u - jnp.mean(u, axis=1, keepdims=True)
            f = lax.rsqrt(jnp.mean(c * c, axis=1, keepdims=True) + EPSILON)
            x = c * f
            v.xhat1[rows, :] = x
            v.rr[0, rows, :] = jnp.broadcast_to(f, (BLOCK, 128))
            y = x * vec[3:4, :] + vec[5:6, :]
            v.first[rows, :] = y
            v.firstb[rows, :] = y.astype(BF16)
            return total + jnp.sum(mask(b) * branch * branch, axis=0, keepdims=True)

        zero = jnp.zeros((1, width), F32)
        blocks = self.length // BLOCK
        branch_sum = lax.fori_loop(0, blocks, norm_first, zero)
        done("xhat1", "firstb")
        if not again:
            self.start_weight(1, "wout", 1)

        self.wait_weight(layer, "wid")
        self.wait_weight(layer, "nar")
        before("act", "slope")
        v.feed[...] = jnp.broadcast_to(vec[11:12, :], v.feed.shape)

        def widen(j):
            at = lanes(j * TILE, TILE)
            hid = mm(v.firstb[...], v.wid[:, at]) + vec[pl.ds(12 + j, 1), 0:TILE]
            a, d = gelu_and_slope(hid)
            v.act[:, at] = a.astype(BF16)
            v.slope[:, at] = d.astype(BF16)

        def narrow(j):
            v.feed[...] += mm(v.act[:, lanes(j * TILE, TILE)], v.nar[rows_of(j, TILE), :])

        widen(0)

        def ffn(j, carry):
            narrow(j - 1)
            widen(j)
            return carry

        lax.fori_loop(1, self.ff // TILE, ffn, 0)
        done("act", "slope")
        narrow(self.ff // TILE - 1)
        if not again:
            self.start_weight(1, "wid", 1)
            self.start_weight(1, "nar", 1)
        before("xhat2")

        def norm_second(b, totals):
            rows = rows_of(b, BLOCK)
            fd = v.feed[rows, :]
            u = v.first[rows, :] + fd
            c = u - jnp.mean(u, axis=1, keepdims=True)
            f = lax.rsqrt(jnp.mean(c * c, axis=1, keepdims=True) + EPSILON)
            x = c * f
            v.xhat2[rows, :] = x
            v.rr[1, rows, :] = jnp.broadcast_to(f, (BLOCK, 128))
            y = x * vec[4:5, :] + vec[6:7, :]
            v.first[rows, :] = y
            if not again:
                v.h[rows, :] = y.astype(BF16)
            ok = mask(b)
            return (
                totals[0] + jnp.sum(ok * u * u, axis=0, keepdims=True),
                totals[1] + jnp.sum(ok * fd * fd, axis=0, keepdims=True),
            )

        stream_sum, feed_sum = lax.fori_loop(0, blocks, norm_second, (zero, zero))
        done("xhat2", "rr")
        for i in range(8):
            small[i : i + 1, :] = v.first[pl.ds(self.cls_at[i], 1), :]
        small[8:9, :] = stream_sum
        small[9:10, :] = branch_sum
        small[10:11, :] = feed_sum
        small[11:12, :] = jnp.full((1, width), self.valid.astype(F32))
        small[12:16, :] = jnp.zeros((4, width), F32)

    def wait_saved(self, restored, *names):
        if restored:
            for name in names:
                if name in WEIGHTS:
                    self.wait_weight(0, name)
                else:
                    self.restoring(name).wait()

    def restore(self, *names):
        for name in names:
            if name in WEIGHTS:
                self.start_weight(0, name, 2)
            else:
                self.restoring(name).start()

    def send_out(self, stage, shift, n, value, target):
        slot = lax.rem(n, 2)

        @pl.when(n >= 2)
        def _():
            pltpu.make_async_copy(stage.at[slot], target, self.sems.stage.at[shift + slot]).wait()

        stage[slot] = value.astype(BF16)
        pltpu.make_async_copy(stage.at[slot], target, self.sems.stage.at[shift + slot]).start()

    def put_rows(self, n, value, target):
        self.send_out(self.v.row_stage, 0, n, value, target)

    def put_cols(self, n, value, target):
        self.send_out(self.v.col_stage, 2, n, value, target)

    def drain_rows(self, grad):
        for slot in range(2):
            pltpu.make_async_copy(self.v.row_stage.at[slot], grad.at[0, 0:TILE, :], self.sems.stage.at[slot]).wait()

    def drain_cols(self, grad):
        for slot in range(2):
            pltpu.make_async_copy(
                self.v.col_stage.at[slot], grad.at[0, :, 0:TILE], self.sems.stage.at[2 + slot]
            ).wait()

    def norms(self, vec, source, x_ref, f_at, gain, target, target_b, where):
        v = self.v
        zero = jnp.zeros((1, self.width), F32)

        def body(b, total):
            rows = rows_of(b, BLOCK)
            up = source[rows, :].astype(F32)
            x = x_ref[rows, :]
            d = norm_back(up * vec[gain : gain + 1, :], x, v.rr[f_at, rows, 0:1])
            target[rows, :] = d
            db = d.astype(BF16)
            target_b[rows, :] = db
            return (
                total[0] + jnp.sum(up * x, axis=0, keepdims=True),
                total[1] + jnp.sum(up, axis=0, keepdims=True),
                total[2] + jnp.sum(db.astype(F32), axis=0, keepdims=True),
            )

        got = lax.fori_loop(0, self.length // BLOCK, body, (zero, zero, zero))
        for i in range(3):
            v.sums[where + i : where + i + 1, :] = got[i]

    def din_kept(self, source):
        return pltpu.make_async_copy(source, self.a.din_kept, self.sems.h.at[2])

    def din_sent(self, source):
        return pltpu.make_async_remote_copy(
            src_ref=source, dst_ref=self.a.din_got, send_sem=self.sems.din.at[0], recv_sem=self.sems.din.at[1],
            device_id=self.a.other, device_id_type=MESH,
        )

    def backward(self, layer, grad, small):
        v, width, restored = self.v, self.width, layer == 0
        vec = v.vec.at[layer]
        dh, dqkv, dbr, dres, ds = v.slope, v.qkv, v.g, v.feed, v.first

        def second():
            self.wait_saved(restored, "xhat2", "rr")
            self.norms(vec, v.g, v.xhat2, 1, 4, ds, v.dfeed, 0)
            self.wait_saved(restored, "nar", "act", "slope", "firstb")

        def ffn(low, j, carry):
            at = lanes(j * TILE, TILE)
            da = mm_right_t(v.dfeed[...], v.nar[at, :])
            d = (v.slope[:, at].astype(F32) * da).astype(BF16)
            dh[:, at] = d
            v.wbias[pl.ds(j, 1), :] = jnp.sum(d.astype(F32), axis=0, keepdims=True)
            place = lanes(lax.rem(j, 3) * TILE, TILE)
            self.put_rows(j - low, mm_left_t(v.act[:, at], v.dfeed[...]), grad.at[2 * (j // 3), place, :])
            self.put_cols(j - low, mm_left_t(v.firstb[...], d), grad.at[2 * (j // 3) + 1, :, place])
            return carry

        def tiles(low, high):
            lax.fori_loop(low, high, functools.partial(ffn, low), 0)
            self.drain_rows(grad)
            self.drain_cols(grad)

        def first():
            self.wait_saved(restored, "wid")

            def body(j, carry):
                at = lanes(j * TILE, TILE)
                ds[:, at] = ds[:, at] + mm_right_t(dh[...], v.wid[at, :])
                return carry

            lax.fori_loop(0, width // TILE, body, 0)
            self.wait_saved(restored, "xhat1")
            self.norms(vec, ds, v.xhat1, 0, 3, dres, dbr, 3)

        def out_grad():
            self.wait_saved(restored, "mixed", "wout", "rinv")

            def body(j, carry):
                at = lanes(j * TILE, TILE)
                self.put_cols(j, mm_left_t(v.mixed[...], dbr[:, at]), grad.at[OUT, :, at])
                d = mm_right_t(dbr[...], v.wout[at, :]).astype(BF16).astype(F32)
                v.dm[:, at] = (d * v.rinv[:, at]).astype(BF16)
                return carry

            lax.fori_loop(0, width // TILE, body, 0)
            self.drain_cols(grad)

        def pair(p, carry):
            low = lax.broadcasted_iota(jnp.int32, (self.length, 128), 1) < HEAD_DIM
            slot = lax.rem(p, 2)

            @pl.when(p + 1 < HEADS // 2)
            def _():
                self.e_load(layer, p + 1, 1 - slot).start()

            at_q, at_k, at_v = lanes(p * 128, 128), lanes(width + p * 128, 128), lanes(2 * width + p * 128, 128)
            q, k, values = v.qkv[:, at_q], v.qkv[:, at_k], v.qkv[:, at_v]
            d = v.dm[:, at_q]
            prod = d.astype(F32) * v.mixed[:, at_q].astype(F32)
            self.e_load(layer, p, slot).wait()
            dq, dk, dv = [], [], []
            for i in range(2):
                mine = low if i == 0 else ~low
                delta = jnp.sum(jnp.where(mine, prod, 0.0), axis=1, keepdims=True)
                dp = mm_right_t(jnp.where(mine, d, BF16(0)), values)
                e = v.e[slot, i]
                s = (e.astype(F32) * (dp - delta)).astype(BF16)
                dq.append(mm(s, k))
                dk.append(mm_left_t(s, q))
                dv.append(mm_left_t(e, d))
            dqkv[:, at_q] = (jnp.where(low, dq[0], dq[1]) * HEAD_DIM**-0.5).astype(BF16)
            dqkv[:, at_k] = jnp.where(low, dk[0], dk[1]).astype(BF16)
            dqkv[:, at_v] = jnp.where(low, dv[0], dv[1]).astype(BF16)
            return carry

        def pairs(low, high):
            if low == 0:
                self.wait_saved(restored, "qkv")
            lax.fori_loop(low, high, pair, 0)

        def in_grad():
            if restored:
                self.load_input(self.a.hidden).wait()

            def body(j, carry):
                at = lanes(j * TILE, TILE)
                place = lanes(lax.rem(j, 3) * TILE, TILE)
                self.put_cols(j, mm_left_t(v.h[...], dqkv[:, at]), grad.at[IN + j // 3, :, place])
                return carry

            lax.fori_loop(0, 3 * width // TILE, body, 0)
            self.drain_cols(grad)

        def input_grad():
            self.wait_saved(restored, "win")

            def body(j, carry):
                at = lanes(j * TILE, TILE)
                d = dres[:, at] + mm_right_t(dqkv[...], v.win[at, :])
                dres[:, at] = d
                if layer == 1:
                    v.g[:, at] = d.astype(BF16)
                return carry

            lax.fori_loop(0, width // TILE, body, 0)
            pl.when(self.section == layer)(lambda: self.din_kept(dres).start())
            pl.when(self.section != layer)(lambda: self.din_sent(dres).start())
            small[16:17, :] = jnp.sum(dqkv[:, 0:width].astype(F32), axis=0, keepdims=True)
            small[17:18, :] = jnp.sum(dqkv[:, 2 * width :].astype(F32), axis=0, keepdims=True)
            for i, source in enumerate((5, 3, 0, 4, 1)):
                small[18 + i : 19 + i, :] = v.sums[source : source + 1, :]
            for i in range(self.ff // TILE):
                small[23 + i // 3 : 24 + i // 3, (i % 3) * TILE : (i % 3 + 1) * TILE] = v.wbias[i : i + 1, :]
            small[27:28, :] = v.sums[2:3, :]
            small[28:32, :] = jnp.zeros((4, width), F32)
            pl.when(self.section == layer)(lambda: self.din_kept(dres).wait())
            pl.when(self.section != layer)(lambda: self.din_sent(dres).wait_send())

        return Refs(
            second=second, tiles=tiles, first=first, out_grad=out_grad, pairs=pairs, in_grad=in_grad,
            input_grad=input_grad,
        )


def sum_plan(devices, rows):
    side = round((devices / 2) ** (1 / 3))
    extents = [side, side, devices // (side * side)]
    axes, stride = [], 1
    for extent in extents:
        steps, step = [], 1
        while step < extent:
            steps.append(stride * step)
            step *= 2
        axes.append(steps)
        stride *= extent
    x, y, z = axes
    unit = 256 if devices <= 16 else 128
    run = 5 * unit // 2
    count = rows // run
    over = rows % run
    return [
        (0, unit, count + (over >= unit), y + x + z),
        (unit, unit, count + (over >= 2 * unit), x + y + z),
        (2 * unit, unit // 2, count, z + x + y),
    ]


def halvings(unit, width, stages):
    rows, cols, steps = unit // 2, width, []
    for _ in range(stages):
        if rows >= 32:
            kind, rows = "rows", rows // 2
        elif cols == width:
            kind, cols = "cols", cols // 2
        else:
            kind = "full"
        steps.append((kind, rows, cols))
    return steps


class GradientSum:
    def __init__(self, plan, slots, width, grads, out, buffers, sems):
        self.plan, self.slots, self.width, self.grads, self.out = plan, slots, width, grads, out
        self.stages = len(plan[0][3])
        self.run = sum(unit for _, unit, _, _ in plan)
        self.steps = [halvings(unit, width, self.stages) for _, unit, _, _ in plan]
        self.total, self.other, self.recvs, self.fulls = buffers
        self.load_sems, self.pair_sems, self.rs_sems, self.ag_sems, self.end_sems, self.free, self.full_free = sems
        self.section, self.me = lax.axis_index("section"), lax.axis_index("dp")
        self.peer = (1 - self.section, self.me)
        self.length = max(2 * count for _, _, count, _ in plan) + 2 * self.stages + 3

    def bit(self, part, stage):
        return lax.rem(self.me // self.plan[part][3][stage], 2)

    def partner(self, part, stage):
        return (self.section, self.me + self.plan[part][3][stage] * (1 - 2 * self.bit(part, stage)))

    def barrier(self):
        barrier = pltpu.get_barrier_semaphore()
        for device in [self.peer] + [self.partner(0, stage) for stage in range(self.stages)]:
            pl.semaphore_signal(barrier, inc=1, device_id=device, device_id_type=MESH)
        pl.semaphore_wait(barrier, self.stages + 1)

    def slot(self, k):
        return lax.rem(k, self.slots)

    def half(self, ref, part, k, which):
        base, unit, count, _ = self.plan[part]
        row = base + lax.rem(k, count) * self.run + which * (unit // 2)
        return ref.at[row // self.width, pl.ds(pl.multiple_of(lax.rem(row, self.width), 16), unit // 2)]

    def load(self, part, k, source):
        slot = self.slot(k)
        return pltpu.make_async_copy(
            self.half(source, part, k, self.section), self.total[part].at[slot], self.load_sems.at[part, slot]
        )

    def trade(self, part, k, source):
        slot = self.slot(k)
        return pltpu.make_async_remote_copy(
            src_ref=self.half(source, part, k, 1 - self.section), dst_ref=self.other[part].at[slot],
            send_sem=self.pair_sems.at[0, part, slot], recv_sem=self.pair_sems.at[1, part, slot],
            device_id=self.peer, device_id_type=MESH,
        )

    def regions(self, part, stage):
        row, col = 0, 0
        rows, cols = self.plan[part][1] // 2, self.width
        if stage < 0:
            return (row, rows, col, cols), None
        for s in range(stage + 1):
            kind, rows, cols = self.steps[part][s]
            keep = self.bit(part, s)
            sent_row, sent_col = row, col
            if kind == "rows":
                row, sent_row = row + keep * rows, row + (1 - keep) * rows
            elif kind == "cols":
                col, sent_col = col + keep * cols, col + (1 - keep) * cols
        return (row, rows, col, cols), (sent_row, rows, sent_col, cols)

    def view(self, ref, slot, region):
        row, rows, col, cols = region
        at = pl.ds(pl.multiple_of(row, 16), rows)
        if cols == self.width:
            return ref.at[slot, at]
        return ref.at[slot, at, pl.ds(pl.multiple_of(col, 128), cols)]

    def held(self, part, stage, slot):
        fulls = [s for s in range(stage + 1) if self.steps[part][s][0] == "full"]
        if fulls:
            return self.fulls[part][fulls[-1]].at[slot]
        return self.view(self.total[part], slot, self.regions(part, stage)[0])

    def reduce_copy(self, part, k, stage):
        slot = self.slot(k)
        if self.steps[part][stage][0] == "full":
            source = self.held(part, stage - 1, slot)
        else:
            source = self.view(self.total[part], slot, self.regions(part, stage)[1])
        return pltpu.make_async_remote_copy(
            src_ref=source, dst_ref=self.recvs[part][stage].at[slot],
            send_sem=self.rs_sems.at[0, part, stage, slot], recv_sem=self.rs_sems.at[1, part, stage, slot],
            device_id=self.partner(part, stage), device_id_type=MESH,
        )

    def start_reduce(self, part, k, stage):
        if self.steps[part][stage][0] == "full":

            @pl.when(k >= self.slots)
            def _():
                pl.semaphore_wait(self.full_free.at[part, stage], 1)

        self.reduce_copy(part, k, stage).start()

    def gather_copy(self, part, k, stage):
        slot = self.slot(k)
        place = self.view(self.other[part], slot, self.regions(part, stage)[0])
        return pltpu.make_async_remote_copy(
            src_ref=place, dst_ref=place,
            send_sem=self.ag_sems.at[0, part, stage, slot], recv_sem=self.ag_sems.at[1, part, stage, slot],
            device_id=self.partner(part, stage), device_id_type=MESH,
        )

    def gathers(self, part, stage):
        return stage >= 0 and self.steps[part][stage][0] != "full"

    def keep(self, part, k):
        slot = self.slot(k)
        return pltpu.make_async_copy(
            self.other[part].at[slot], self.half(self.out, part, k, self.section), self.end_sems.at[0, part, slot]
        )

    def hand_over(self, part, k):
        slot = self.slot(k)
        place = self.half(self.out, part, k, self.section)
        return pltpu.make_async_remote_copy(
            src_ref=self.other[part].at[slot], dst_ref=place,
            send_sem=self.end_sems.at[0, part, slot], recv_sem=self.end_sems.at[1, part, slot],
            device_id=self.peer, device_id_type=MESH,
        )

    def owned(self, part, k):
        return (k < self.plan[part][2]) == (self.section == 1)

    def add(self, target, left, right, rows):
        block = min(rows, 64)

        def body(i, carry):
            at = pl.ds(pl.multiple_of(i * block, 16), block)
            target[at, :] = left[at, :] + right[at, :]
            return carry

        lax.fori_loop(0, rows // block, body, 0)

    def retire(self, part, k):
        self.trade(part, k, self.grads[0]).wait_send()
        for stage in range(self.stages):
            self.reduce_copy(part, k, stage).wait_send()
            if self.gathers(part, stage):
                self.gather_copy(part, k, stage).wait_send()
        mine = self.owned(part, k)
        pl.when(mine)(lambda: self.keep(part, k).wait())
        pl.when(jnp.logical_not(mine))(lambda: self.hand_over(part, k).wait_send())

    def task(self, part, k, stage):
        last = self.stages - 1
        slot = self.slot(k)
        if stage == 0:

            @pl.when(k >= self.slots)
            def _():
                self.retire(part, k - self.slots)
                pl.semaphore_signal(self.free.at[part], inc=1, device_id=self.peer, device_id_type=MESH)
                pl.semaphore_wait(self.free.at[part], 1)

            first = k < self.plan[part][2]

            @pl.when(first)
            def _():
                self.load(part, k, self.grads[1]).start()
                self.trade(part, k, self.grads[1]).start()

            @pl.when(jnp.logical_not(first))
            def _():
                self.load(part, k, self.grads[0]).start()
                self.trade(part, k, self.grads[0]).start()

        elif stage == 1:
            self.load(part, k, self.grads[0]).wait()
            self.trade(part, k, self.grads[0]).wait_recv()
            rows = self.plan[part][1] // 2
            total = self.total[part].at[slot]
            self.add(total, total, self.other[part].at[slot], rows)
            self.start_reduce(part, k, 0)
        elif stage <= last + 2:
            s = stage - 2
            self.reduce_copy(part, k, s).wait_recv()
            kind, rows, _ = self.steps[part][s]
            kept, _ = self.regions(part, s)
            left = self.held(part, s - 1, slot) if kind == "full" else self.view(self.total[part], slot, kept)
            if s == last:
                target = self.view(self.other[part], slot, kept)
            else:
                target = self.held(part, s, slot)
            self.add(target, left, self.recvs[part][s].at[slot], rows)
            if kind == "full":

                @pl.when(k + self.slots < 2 * self.plan[part][2])
                def _():
                    pl.semaphore_signal(
                        self.full_free.at[part, s], inc=1, device_id=self.partner(part, s), device_id_type=MESH
                    )

            if s < last:
                self.start_reduce(part, k, s + 1)
            elif self.gathers(part, last):
                self.gather_copy(part, k, last).start()
        elif stage <= 2 * last + 3:
            s = 2 * last + 3 - stage
            if self.gathers(part, s):
                self.gather_copy(part, k, s).wait_recv()
            if s == 0:
                mine = self.owned(part, k)
                pl.when(mine)(lambda: self.keep(part, k).start())
                pl.when(jnp.logical_not(mine))(lambda: self.hand_over(part, k).start())
            elif self.gathers(part, s - 1):
                self.gather_copy(part, k, s - 1).start()
        else:
            pl.when(self.owned(part, k))(lambda: self.hand_over(part, k).wait_recv())

    def step(self, t):
        for stage in range(2 * self.stages + 3):
            for part, (_, _, count, _) in enumerate(self.plan):
                k = t - stage
                pl.when((k >= 0) & (k < 2 * count))(lambda part=part, stage=stage, k=k: self.task(part, k, stage))

    def finish(self):
        for part, (_, _, count, _) in enumerate(self.plan):

            def body(k, carry, part=part):
                self.retire(part, k)
                return carry

            lax.fori_loop(max(2 * count - self.slots, 0), 2 * count, body, 0)


def sum_scratch(plan, slots, width):
    stages = len(plan[0][3])
    steps = [halvings(unit, width, stages) for _, unit, _, _ in plan]
    parts = len(plan)
    shapes = []
    for _, unit, _, _ in plan:
        shapes += [pltpu.VMEM((slots, unit // 2, width), BF16)] * 2
    for step in steps:
        shapes += [pltpu.VMEM((slots, rows, cols), BF16) for _, rows, cols in step]
        shapes += [pltpu.VMEM((slots, rows, cols), BF16) for kind, rows, cols in step[:-1] if kind == "full"]
    shapes += [
        pltpu.SemaphoreType.DMA((parts, slots)),
        pltpu.SemaphoreType.DMA((2, parts, slots)),
        pltpu.SemaphoreType.DMA((2, parts, stages, slots)),
        pltpu.SemaphoreType.DMA((2, parts, stages, slots)),
        pltpu.SemaphoreType.DMA((2, parts, slots)),
        pltpu.SemaphoreType.REGULAR((parts,)),
        pltpu.SemaphoreType.REGULAR((parts, stages)),
    ]

    def split(refs):
        refs = list(refs)
        total, other = [], []
        for _ in plan:
            total.append(refs.pop(0))
            other.append(refs.pop(0))
        recvs, fulls = [], []
        for step in steps:
            recvs.append([refs.pop(0) for _ in step])
            fulls.append({s: refs.pop(0) for s in range(stages - 1) if step[s][0] == "full"})
        return (total, other, recvs, fulls), refs

    return shapes, split


def layers_kernel(plan, slots, split, *refs):
    refs = list(refs)
    take = lambda n: [refs.pop(0) for _ in range(n)]
    valid_ref, cls_ref, seg_ref, proj_bias, out_shift, gains, shifts, widen_bias, narrow_bias = take(9)
    hidden, cotangent = take(2)
    own = take(4)
    out, din_kept, din_got, small_got, small_sum, small_mine = take(6)
    grad0, grad1, e_hbm = take(3)
    saved = take(9)
    v = Refs(**dict(zip(VMEM_NAMES, take(len(VMEM_NAMES)))))
    small_send, small_acc, small_recv = take(3)
    weight_sems, sent_sems, arrived_sems, free_sems, saved_sems, e_sems, h_sems, stage_sems, vec_sems, small_sems = take(10)
    din_sems, = take(1)
    section = lax.axis_index("section")
    width = v.h.shape[1]
    total = GradientSum(plan, slots, width, (grad0, grad1), out, *split(refs))
    compute = Compute(
        v,
        Refs(own=own, other=total.peer, saved=saved, e=e_hbm, hidden=hidden, din_kept=din_kept, din_got=din_got),
        Refs(
            weights=weight_sems, sent=sent_sems, arrived=arrived_sems, free=free_sems, saved=saved_sems, e=e_sems, h=h_sems,
            stage=stage_sems, din=din_sems,
        ),
        section, valid_ref[section], [cls_ref[section, i] for i in range(8)],
    )

    def vec_sent():
        return pltpu.make_async_remote_copy(
            src_ref=v.vec_own, dst_ref=v.vec_peer, send_sem=vec_sems.at[0], recv_sem=vec_sems.at[1],
            device_id=total.peer, device_id_type=MESH,
        )

    compute.load_input(hidden).start()
    v.vec_own[0:2, :] = proj_bias[0]
    v.vec_own[2:3, :] = out_shift[...]
    v.vec_own[3:5, :] = gains[0]
    v.vec_own[5:7, :] = shifts[0]
    v.vec_own[7:11, :] = jnp.zeros((4, width), F32)
    v.vec_own[11:12, :] = narrow_bias[...]
    v.vec_own[12:24, :] = jnp.zeros((12, width), F32)
    for i in range(widen_bias.shape[1] // TILE):
        v.vec_own[12 + i : 13 + i, 0:TILE] = widen_bias[:, i * TILE : (i + 1) * TILE]
    total.barrier()
    vec_sent().start()
    for name in WEIGHTS:
        compute.start_weight(0, name, 0)
    segments = seg_ref[pl.ds(section, 1), :]
    columns = jnp.broadcast_to(segments.astype(F32), (128, compute.length)).T[:, :1]
    v.bias[...] = jnp.where(columns == segments.astype(F32), 0.0, MASKED)
    compute.load_cotangent(cotangent).start()
    vec_sent().wait_recv()
    for layer in range(2):
        v.vec[layer] = jnp.where(section == layer, v.vec_own[...], v.vec_peer[...])
    compute.load_input(hidden).wait()

    small0, small1 = v.small.at[0], v.small.at[1]
    compute.forward(0, small0)
    compute.forward(1, small1)
    compute.e_drain(1)
    compute.e_load(1, 0, 0).start()
    compute.load_cotangent(cotangent).wait()

    def small_trade():
        return pltpu.make_async_remote_copy(
            src_ref=small_send, dst_ref=small_got, send_sem=small_sems.at[0, total.stages],
            recv_sem=small_sems.at[1, total.stages], device_id=total.peer, device_id_type=MESH,
        )

    def small_copy(stage):
        return pltpu.make_async_remote_copy(
            src_ref=small_acc.at[stage], dst_ref=small_recv.at[stage], send_sem=small_sems.at[0, stage],
            recv_sem=small_sems.at[1, stage], device_id=total.partner(0, stage), device_id_type=MESH,
        )

    def small_start():
        small_mine[...] = jnp.where(section == 0, small0[...], small1[...])
        small_send[...] = jnp.where(section == 0, small1[...], small0[...])
        small_trade().start()

    def small_step(stage):
        if stage == 0:
            small_trade().wait_recv()
            small_acc[0] = small_mine[8:, :] + small_got[8:, :]
        else:
            small_copy(stage - 1).wait_recv()
            small_acc[stage] = small_acc[stage - 1] + small_recv[stage - 1]
        if stage < total.stages:
            small_copy(stage).start()
        else:
            small_sum[...] = small_acc[stage]

    one = compute.backward(1, grad1, small1)
    zero = compute.backward(0, grad0, small0)
    restore = compute.restore
    third, two = compute.ff // TILE // 4, HEADS // 6

    def after_first():
        restore("slope", "wid", "xhat1", "rr")

    def after_input_grad():
        restore("qkv", "win")

    one.second()
    one.tiles(0, third)
    events = [
        [lambda: one.tiles(third, 2 * third)],
        [lambda: one.tiles(2 * third, 3 * third)],
        [lambda: one.tiles(3 * third, 4 * third), lambda: restore("nar", "act", "firstb", "xhat2")],
        [one.first, after_first],
        [one.out_grad, lambda: restore("wout", "rinv"), lambda: one.pairs(0, two)],
        [lambda: one.pairs(two, 2 * two)],
        [lambda: one.pairs(2 * two, 3 * two), lambda: restore("mixed"), lambda: compute.e_load(0, 0, 0).start()],
        [one.in_grad, lambda: compute.load_input(hidden).start()],
        [one.input_grad, after_input_grad],
        [zero.second, lambda: zero.tiles(0, third)],
        [lambda: zero.tiles(third, 2 * third)],
        [lambda: zero.tiles(2 * third, 3 * third)],
        [lambda: zero.tiles(3 * third, 4 * third)],
        [zero.first],
        [zero.out_grad, lambda: zero.pairs(0, two)],
        [lambda: zero.pairs(two, 2 * two)],
        [lambda: zero.pairs(2 * two, 3 * two)],
        [zero.in_grad],
        [zero.input_grad],
        [small_start],
    ] + [[functools.partial(small_step, s)] for s in range(total.stages + 1)]

    def body(t, carry):
        total.step(t)
        for i, event in enumerate(events):

            @pl.when(t == i)
            def _(event=event):
                for action in event:
                    action()

        return carry

    lax.fori_loop(0, total.length, body, 0)
    total.finish()
    vec_sent().wait_send()
    for i in range(4):
        compute.weight_sent(i).wait_send()
    small_trade().wait_send()
    for stage in range(total.stages):
        small_copy(stage).wait_send()
    compute.din_sent(v.feed).wait_recv()


VMEM_NAMES = (
    "h", "g", "win", "wout", "wid", "nar", "qkv", "e", "rinv", "mixed", "xhat1", "rr", "first", "firstb", "act", "slope",
    "xhat2", "feed", "bias", "dfeed", "dm", "row_stage", "col_stage", "wbias", "sums", "vec", "vec_own", "vec_peer", "small",
)


def layers(valid_counts, cls_positions, segment_ids, vectors, hidden, cotangent, own):
    rows, length = segment_ids.shape
    width, ff = hidden.shape[1], own[2].shape[2]
    devices = lax.axis_size("dp")
    plan = sum_plan(devices, 12 * width)
    stages = len(plan[0][3])
    slots = 2 * stages + 3
    shapes, split = sum_scratch(plan, slots, width)
    row_b, row_f = ((length, width), BF16), ((length, width), F32)
    saved = [
        ((length, 3 * width), BF16), row_f, row_b, row_f, ((2, length, 128), F32), row_b, ((length, ff), BF16),
        ((length, ff), BF16), row_f,
    ]
    grad = ((12, width, width), BF16)
    small = ((32, width), F32)
    sums = (24, width)
    outs = [grad, row_f, row_f, small, (sums, F32), small, grad, grad, ((2, HEADS, length, length), BF16), *saved]
    scratch = dict(
        h=row_b, g=row_b, win=(own[0].shape[1:], BF16), wout=(own[1].shape[1:], BF16), wid=(own[2].shape[1:], BF16),
        nar=(own[3].shape[1:], BF16), qkv=saved[0], e=((2, 2, length, length), BF16), rinv=row_f, mixed=row_b, xhat1=row_f,
        rr=saved[4], first=row_f, firstb=row_b, act=saved[6], slope=saved[7], xhat2=row_f, feed=row_f,
        bias=((length, length), F32), dfeed=row_b, dm=row_b, row_stage=((2, TILE, width), BF16),
        col_stage=((2, width, TILE), BF16), wbias=((16, TILE), F32), sums=((8, width), F32), vec=((2, 24, width), F32),
        vec_own=((24, width), F32), vec_peer=((24, width), F32), small=((2, 32, width), F32),
    )
    in_vmem = (3, 4, 5)
    got = pl.pallas_call(
        functools.partial(layers_kernel, plan, slots, split),
        out_shape=[jax.ShapeDtypeStruct(s, d) for s, d in outs],
        in_specs=[SMEM, SMEM] + [VMEM] * 7 + [ANY] * 6,
        out_specs=[VMEM if i in in_vmem else ANY for i in range(len(outs))],
        scratch_shapes=[
            *[pltpu.VMEM(*scratch[name]) for name in VMEM_NAMES],
            pltpu.VMEM(*small),
            pltpu.VMEM((stages + 1, *sums), F32),
            pltpu.VMEM((stages, *sums), F32),
            pltpu.SemaphoreType.DMA((4,)),
            pltpu.SemaphoreType.DMA((4,)),
            pltpu.SemaphoreType.DMA((4,)),
            pltpu.SemaphoreType.REGULAR((4,)),
            pltpu.SemaphoreType.DMA((9,)),
            pltpu.SemaphoreType.DMA((2,)),
            pltpu.SemaphoreType.DMA((3,)),
            pltpu.SemaphoreType.DMA((4,)),
            pltpu.SemaphoreType.DMA((2,)),
            pltpu.SemaphoreType.DMA((2, stages + 1)),
            pltpu.SemaphoreType.DMA((2,)),
            *shapes,
        ],
        compiler_params=pltpu.CompilerParams(collective_id=0, has_side_effects=True, vmem_limit_bytes=63 * MIB),
        cost_estimate=pl.CostEstimate(flops=54 * 10**9, bytes_accessed=200 * 10**6, transcendentals=10**7),
        name="layers_and_sum",
    )(valid_counts, cls_positions, segment_ids, *vectors, hidden, cotangent, *own)
    return got[:6]


def finish_kernel(
    flags, blocks, din_kept, din_got, small_mine, small_got, small_sum,
    cls_o, input_o, in_o, bias_o, out_o, out_shift_o, gain_o, shift_o, widen_o, widen_bias_o, narrow_o, narrow_bias_o, rms_o,
    dins, wide, sems,
):
    block = pl.program_id(0)
    section = flags[0]
    length, width = din_got.shape
    got_row = 1 - section

    def rows(row):
        return input_o.at[0, pl.ds(pl.multiple_of(row * length, 16), length)]

    places = (rows(section), rows(got_row))

    def load_din(i, source):
        return pltpu.make_async_copy(source, dins.at[i], sems.at[i])

    def store_din(i):
        return pltpu.make_async_copy(dins.at[i], places[i], sems.at[i])

    @pl.when(block == 0)
    def _():
        load_din(1, din_got).start()
        load_din(0, din_kept).start()
        cls_o[0, section] = small_mine[0:8, :]
        cls_o[0, got_row] = small_got[0:8, :]
        bias_o[0] = small_sum[8:10, :]
        out_shift_o[...] = small_sum[10:11, :]
        gain_o[0] = small_sum[11:13, :]
        shift_o[0] = small_sum[13:15, :]
        for i in range(4):
            widen_bias_o[0:1, i * width : (i + 1) * width] = small_sum[15 + i : 16 + i, :]
        narrow_bias_o[...] = small_sum[19:20, :]
        squares = jnp.sum(small_sum[0:3, :], axis=1, keepdims=True)
        rms_o[...] = jnp.sqrt(squares / (small_sum[3:4, 0:1] * width))

    def target(index):
        part = slice(index // 2 * width, (index // 2 + 1) * width)
        if index >= IN:
            return in_o.at[0, :, (index - IN) * width : (index - IN + 1) * width]
        if index == OUT:
            return out_o.at[0]
        return narrow_o.at[0, part, :] if index % 2 == 0 else widen_o.at[0, :, part]

    slot = lax.rem(block, 2)
    for index in range(12):

        @pl.when(block == index)
        def _(index=index):
            if index >= 2:
                pltpu.make_async_copy(wide.at[slot], target(index - 2), sems.at[2 + index % 2]).wait()
            wide[slot] = blocks[0].astype(F32)
            pltpu.make_async_copy(wide.at[slot], target(index), sems.at[2 + index % 2]).start()
            if index == 2:
                for i in range(2):
                    load_din(i, din_kept).wait()
                    store_din(i).start()
            if index == 11:
                for i in (10, 11):
                    pltpu.make_async_copy(wide.at[i % 2], target(i), sems.at[2 + i % 2]).wait()
                for i in range(2):
                    store_din(i).wait()


def finish(section, blocks, din_kept, din_got, small_mine, small_got, small_sum):
    length, width = din_got.shape
    shapes = [
        (1, 2, 8, width), (1, 2 * length, width), (1, width, 3 * width), (1, 2, width), (1, width, width), (1, width),
        (1, 2, width), (1, 2, width), (1, width, 4 * width), (1, 4 * width), (1, 4 * width, width), (1, width), (3, 1),
    ]
    big = (1, 2, 4, 8, 10)
    whole = lambda shape: pl.BlockSpec(shape, lambda i: (0,) * len(shape))
    return pl.pallas_call(
        finish_kernel,
        grid=(12,),
        out_shape=[jax.ShapeDtypeStruct(s, F32) for s in shapes],
        in_specs=[SMEM, pl.BlockSpec((1, width, width), lambda i: (i, 0, 0)), ANY, ANY]
        + [whole(a.shape) for a in (small_mine, small_got, small_sum)],
        out_specs=[ANY if i in big else whole(s) for i, s in enumerate(shapes)],
        scratch_shapes=[
            pltpu.VMEM((2, length, width), F32),
            pltpu.VMEM((2, width, width), F32),
            pltpu.SemaphoreType.DMA((4,)),
        ],
        compiler_params=pltpu.CompilerParams(vmem_limit_bytes=63 * MIB),
        cost_estimate=pl.CostEstimate(flops=10**7, bytes_accessed=46 * 10**6, transcendentals=0),
        name="finish",
    )(section[None], blocks, din_kept, din_got, small_mine, small_got, small_sum)


def local(
    hidden_in, segment_ids, cls_positions, valid_counts, proj_in, proj_bias, proj_out, out_shift, norm_gains,
    norm_shifts, widen, widen_bias, narrow, narrow_bias, cotangent,
):
    section = lax.axis_index("section")
    vectors = (proj_bias, out_shift, norm_gains, norm_shifts, widen_bias, narrow_bias)
    blocks, din_kept, din_got, small_got, small_sum, small_mine = layers(
        valid_counts, cls_positions, segment_ids, vectors, hidden_in, cotangent, (proj_in, proj_out, widen, narrow)
    )
    outs = finish(section, blocks, din_kept, din_got, small_mine, small_got, small_sum)
    return (*outs[:-1], outs[-1].reshape(1, 3))


def solution(mesh):
    placed = (
        P("dp", None),
        P("dp", None),
        P("dp", None),
        P("dp"),
        P("section", None, None),
        P("section", None, None),
        P("section", None, None),
        P("section", None),
        P("section", None, None),
        P("section", None, None),
        P("section", None, None),
        P("section", None),
        P("section", None, None),
        P("section", None),
        P("dp", None),
    )
    return jax.shard_map(
        local,
        mesh=mesh,
        in_specs=placed,
        out_specs=(
            P("section", "dp", None, None),
            P("section", "dp", None),
            P("section", None, None),
            P("section", None, None),
            P("section", None, None),
            P("section", None),
            P("section", None, None),
            P("section", None, None),
            P("section", None, None),
            P("section", None),
            P("section", None, None),
            P("section", None),
            P("section", None),
        ),
        check_vma=False,
    )
```

```python
import functools

import jax
import jax.numpy as jnp
from jax import lax
from jax.experimental import pallas as pl
from jax.experimental.pallas import tpu as pltpu
from jax.sharding import PartitionSpec as P

HEADS = 12
HEAD_DIM = 64
EPSILON = 1e-12
MASKED = -1e30
F32 = jnp.float32
BF16 = jnp.bfloat16
MIB = 2**20
TILE = 256
BLOCK = 128
ANY = pl.BlockSpec(memory_space=pl.ANY)
VMEM = pl.BlockSpec(memory_space=pltpu.VMEM)
SMEM = pl.BlockSpec(memory_space=pltpu.SMEM)
MESH = pl.DeviceIdType.MESH
OUT, IN = 8, 9


def mm(left, right):
    return jnp.dot(left, right, preferred_element_type=F32)


def mm_left_t(left, right):
    return lax.dot_general(left, right, (((0,), (0,)), ((), ())), preferred_element_type=F32)


def mm_right_t(left, right):
    return lax.dot_general(left, right, (((1,), (1,)), ((), ())), preferred_element_type=F32)


def lanes(start, size):
    return pl.ds(pl.multiple_of(start, size), size)


def rows_of(b, size):
    return pl.ds(pl.multiple_of(b * size, size), size)


def gelu_and_slope(v):
    z = jnp.abs(v) * 0.7071067811865476
    t = 1.0 / (1.0 + 0.3275911 * z)
    e = jnp.exp(-0.5 * v * v)
    poly = t * (
        0.127414796 + t * (-0.142248368 + t * (0.7107068705 + t * (-0.7265760135 + t * 0.5307027145)))
    )
    tail = poly * e
    cdf = jnp.where(v >= 0, 1.0 - tail, tail)
    return v * cdf, cdf + v * e * 0.3989422804014327


def norm_back(up, x, f):
    return f * (up - jnp.mean(up, axis=1, keepdims=True) - x * jnp.mean(up * x, axis=1, keepdims=True))


class Refs:
    def __init__(self, **refs):
        self.__dict__.update(refs)


SAVED = ("qkv", "rinv", "mixed", "xhat1", "rr", "firstb", "act", "slope", "xhat2")
WEIGHTS = ("win", "wout", "wid", "nar")


class Compute:
    def __init__(self, v, a, sems, section, valid, cls_at):
        self.v, self.a, self.sems = v, a, sems
        self.section, self.valid, self.cls_at = section, valid, cls_at
        self.length, self.width = v.h.shape
        self.ff = v.wid.shape[1]

    def piece(self, name, q):
        i = WEIGHTS.index(name)
        source, target = self.a.own[i].at[0], getattr(self.v, name)
        if name == "wid":
            at = lanes(q * self.width, self.width)
            return source.at[:, at], target.at[:, at], 2 + q
        if name == "nar":
            at = rows_of(q, self.width)
            return source.at[at, :], target.at[at, :], 6 + q
        return source, target, i

    def pieces(self, name):
        return self.ff // self.width if name in ("wid", "nar") else 1

    def weight_copy(self, name, q):
        source, target, i = self.piece(name, q)
        return pltpu.make_async_copy(source, target, self.sems.weights.at[i])

    def weight_sent(self, name, q):
        source, target, i = self.piece(name, q)
        return pltpu.make_async_remote_copy(
            src_ref=source, dst_ref=target, send_sem=self.sems.sent.at[i], recv_sem=self.sems.arrived.at[i],
            device_id=self.a.other, device_id_type=MESH,
        )

    def start_weight(self, layer, name, use, q=None):
        i = WEIGHTS.index(name)

        @pl.when(self.section == layer)
        def _():
            some = range(self.pieces(name)) if q is None else (q,)
            for p in some:
                self.weight_copy(name, p).start()
            if use > 0:
                pl.semaphore_wait(self.sems.free.at[i], 1)
            for p in some:
                if use == 2:
                    self.weight_sent(name, p).wait_send()
                self.weight_sent(name, p).start()

        if use > 0:

            @pl.when(self.section != layer)
            def _():
                pl.semaphore_signal(self.sems.free.at[i], inc=1, device_id=self.a.other, device_id_type=MESH)

    def wait_piece(self, layer, name, q):
        pl.when(self.section == layer)(lambda: self.weight_copy(name, q).wait())
        pl.when(self.section != layer)(lambda: self.weight_sent(name, q).wait_recv())

    def wait_weight(self, layer, name):
        for q in range(self.pieces(name)):
            self.wait_piece(layer, name, q)

    def saving(self, name):
        i = SAVED.index(name)
        return pltpu.make_async_copy(getattr(self.v, name), self.a.saved[i], self.sems.saved.at[i])

    def restoring(self, name):
        i = SAVED.index(name)
        return pltpu.make_async_copy(self.a.saved[i], getattr(self.v, name), self.sems.saved.at[i])

    def load_input(self, layer_input):
        return pltpu.make_async_copy(layer_input.at[self.rows()], self.v.h, self.sems.h.at[0])

    def load_cotangent(self, cotangent):
        return pltpu.make_async_copy(cotangent.at[self.rows()], self.v.g, self.sems.h.at[1])

    def rows(self):
        return pl.ds(pl.multiple_of(self.section * self.length, self.length), self.length)

    def e_store(self, layer, p, slot):
        return pltpu.make_async_copy(
            self.v.e.at[slot], self.a.e.at[layer, pl.ds(2 * p, 2)], self.sems.e.at[slot]
        )

    def e_load(self, layer, p, slot):
        return pltpu.make_async_copy(
            self.a.e.at[layer, pl.ds(2 * p, 2)], self.v.e.at[slot], self.sems.e.at[slot]
        )

    def e_drain(self, layer):
        for slot in range(2):
            self.e_store(layer, 0, slot).wait()

    def forward(self, layer, small):
        v, width = self.v, self.width
        vec = v.vec.at[layer]
        again = layer == 1

        def before(*names):
            if again:
                for name in names:
                    self.saving(name).wait()

        def done(*names):
            if not again:
                for name in names:
                    self.saving(name).start()

        self.wait_weight(layer, "win")
        before("qkv")
        for part in range(3):
            shift = [vec[0:1, :], None, vec[1:2, :]][part]
            for j in range(width // TILE):
                at = part * width + j * TILE
                got = mm(v.h[...], v.win[:, at : at + TILE])
                if shift is not None:
                    got = got + shift[:, j * TILE : (j + 1) * TILE]
                got = got.astype(BF16)
                if part == 0:
                    got = got * BF16(HEAD_DIM**-0.5)
                v.qkv[:, at : at + TILE] = got
        done("qkv")
        if again:
            self.e_drain(0)
        else:
            self.start_weight(1, "win", 1)
        before("rinv", "mixed")
        low = lax.broadcasted_iota(jnp.int32, (self.length, 128), 1) < HEAD_DIM
        ones = jnp.ones((self.length, 128), BF16)

        def pair(p, carry):
            slot = lax.rem(p, 2)

            @pl.when(p >= 2)
            def _():
                self.e_store(layer, p, slot).wait()

            q = v.qkv[:, lanes(p * 128, 128)]
            k = v.qkv[:, lanes(width + p * 128, 128)]
            values = jnp.concatenate([v.qkv[:, lanes(2 * width + p * 128, 128)], ones], axis=1)
            outs = []
            for i in range(2):
                qm = jnp.where(low if i == 0 else ~low, q, BF16(0))
                s = mm_right_t(qm, k) + v.bias[...]
                top = jnp.max(s, axis=1, keepdims=True)
                e = jnp.exp(s - top).astype(BF16)
                v.e[slot, i] = e
                outs.append(mm(e, values))
            self.e_store(layer, p, slot).start()
            r0 = 1.0 / outs[0][:, 128:]
            r1 = 1.0 / outs[1][:, 128:]
            m = jnp.where(low, outs[0][:, :128] * r0, outs[1][:, :128] * r1)
            v.mixed[:, lanes(p * 128, 128)] = m.astype(BF16)
            v.rinv[:, lanes(p * 128, 128)] = jnp.where(low, r0, r1)
            return carry

        lax.fori_loop(0, HEADS // 2, pair, 0)
        done("rinv", "mixed")

        self.wait_weight(layer, "wout")
        before("xhat1", "rr", "firstb")

        def mask(b):
            place = lax.broadcasted_iota(jnp.int32, (BLOCK, 1), 0) + b * BLOCK
            return (place < self.valid).astype(F32)

        def norm_first(b, total):
            rows = rows_of(b, BLOCK)
            branch = mm(v.mixed[rows, :], v.wout[...]) + vec[2:3, :]
            u = v.h[rows, :].astype(F32) + branch
            c = u - jnp.mean(u, axis=1, keepdims=True)
            f = lax.rsqrt(jnp.mean(c * c, axis=1, keepdims=True) + EPSILON)
            x = c * f
            v.xhat1[rows, :] = x
            v.rr[0, rows, :] = jnp.broadcast_to(f, (BLOCK, 128))
            y = x * vec[3:4, :] + vec[5:6, :]
            v.first[rows, :] = y
            v.firstb[rows, :] = y.astype(BF16)
            return total + jnp.sum(mask(b) * branch * branch, axis=0, keepdims=True)

        zero = jnp.zeros((1, width), F32)
        blocks = self.length // BLOCK
        branch_sum = lax.fori_loop(0, blocks, norm_first, zero)
        done("xhat1", "firstb")
        if not again:
            self.start_weight(1, "wout", 1)

        before("act", "slope")
        v.feed[...] = jnp.broadcast_to(vec[11:12, :], v.feed.shape)

        def widen(j):
            at = lanes(j * TILE, TILE)
            hid = mm(v.firstb[...], v.wid[:, at]) + vec[pl.ds(12 + j, 1), 0:TILE]
            a, d = gelu_and_slope(hid)
            v.act[:, at] = a.astype(BF16)
            v.slope[:, at] = d.astype(BF16)

        def narrow(j):
            v.feed[...] += mm(v.act[:, lanes(j * TILE, TILE)], v.nar[rows_of(j, TILE), :])

        self.wait_piece(layer, "wid", 0)
        widen(0)

        def ffn(j, carry):
            @pl.when(lax.rem(j, width // TILE) == 0)
            def _():
                self.wait_piece(layer, "wid", j // (width // TILE))

            @pl.when(lax.rem(j, width // TILE) == 1)
            def _():
                self.wait_piece(layer, "nar", j // (width // TILE))

            narrow(j - 1)
            widen(j)
            return carry

        lax.fori_loop(1, self.ff // TILE, ffn, 0)
        done("act", "slope")
        narrow(self.ff // TILE - 1)
        if not again:
            self.start_weight(1, "wid", 1)
            self.start_weight(1, "nar", 1)
        before("xhat2")

        def norm_second(b, totals):
            rows = rows_of(b, BLOCK)
            fd = v.feed[rows, :]
            u = v.first[rows, :] + fd
            c = u - jnp.mean(u, axis=1, keepdims=True)
            f = lax.rsqrt(jnp.mean(c * c, axis=1, keepdims=True) + EPSILON)
            x = c * f
            v.xhat2[rows, :] = x
            v.rr[1, rows, :] = jnp.broadcast_to(f, (BLOCK, 128))
            y = x * vec[4:5, :] + vec[6:7, :]
            v.first[rows, :] = y
            if not again:
                v.h[rows, :] = y.astype(BF16)
            ok = mask(b)
            return (
                totals[0] + jnp.sum(ok * u * u, axis=0, keepdims=True),
                totals[1] + jnp.sum(ok * fd * fd, axis=0, keepdims=True),
            )

        stream_sum, feed_sum = lax.fori_loop(0, blocks, norm_second, (zero, zero))
        done("xhat2", "rr")
        for i in range(8):
            small[i : i + 1, :] = v.first[pl.ds(self.cls_at[i], 1), :]
        small[8:9, :] = stream_sum
        small[9:10, :] = branch_sum
        small[10:11, :] = feed_sum
        small[11:12, :] = jnp.full((1, width), self.valid.astype(F32))
        small[12:16, :] = jnp.zeros((4, width), F32)

    def wait_saved(self, restored, *names):
        if restored:
            for name in names:
                if name in WEIGHTS:
                    self.wait_weight(0, name)
                else:
                    self.restoring(name).wait()

    def restore(self, *names):
        for name in names:
            if name in WEIGHTS:
                self.start_weight(0, name, 2)
            else:
                self.restoring(name).start()

    def send_out(self, stage, shift, n, value, target):
        slot = lax.rem(n, 2)

        @pl.when(n >= 2)
        def _():
            pltpu.make_async_copy(stage.at[slot], target, self.sems.stage.at[shift + slot]).wait()

        stage[slot] = value.astype(BF16)
        pltpu.make_async_copy(stage.at[slot], target, self.sems.stage.at[shift + slot]).start()

    def put_rows(self, n, value, target):
        self.send_out(self.v.row_stage, 0, n, value, target)

    def put_cols(self, n, value, target):
        self.send_out(self.v.col_stage, 2, n, value, target)

    def drain_rows(self, grad):
        for slot in range(2):
            pltpu.make_async_copy(self.v.row_stage.at[slot], grad.at[0, 0:TILE, :], self.sems.stage.at[slot]).wait()

    def drain_cols(self, grad):
        for slot in range(2):
            pltpu.make_async_copy(
                self.v.col_stage.at[slot], grad.at[0, :, 0:TILE], self.sems.stage.at[2 + slot]
            ).wait()

    def norms(self, vec, source, x_ref, f_at, gain, target, target_b, where):
        v = self.v
        zero = jnp.zeros((1, self.width), F32)

        def body(b, total):
            rows = rows_of(b, BLOCK)
            up = source[rows, :].astype(F32)
            x = x_ref[rows, :]
            d = norm_back(up * vec[gain : gain + 1, :], x, v.rr[f_at, rows, 0:1])
            target[rows, :] = d
            db = d.astype(BF16)
            target_b[rows, :] = db
            return (
                total[0] + jnp.sum(up * x, axis=0, keepdims=True),
                total[1] + jnp.sum(up, axis=0, keepdims=True),
                total[2] + jnp.sum(db.astype(F32), axis=0, keepdims=True),
            )

        got = lax.fori_loop(0, self.length // BLOCK, body, (zero, zero, zero))
        for i in range(3):
            v.sums[where + i : where + i + 1, :] = got[i]

    def din_kept(self, source):
        return pltpu.make_async_copy(source, self.a.din_kept, self.sems.h.at[2])

    def din_sent(self, source):
        return pltpu.make_async_remote_copy(
            src_ref=source, dst_ref=self.a.din_got, send_sem=self.sems.din.at[0], recv_sem=self.sems.din.at[1],
            device_id=self.a.other, device_id_type=MESH,
        )

    def backward(self, layer, grad, small):
        v, width, restored = self.v, self.width, layer == 0
        vec = v.vec.at[layer]
        dh, dqkv, dbr, dres, ds = v.slope, v.qkv, v.g, v.feed, v.first

        def second():
            self.wait_saved(restored, "xhat2", "rr")
            self.norms(vec, v.g, v.xhat2, 1, 4, ds, v.dfeed, 0)
            self.wait_saved(restored, "nar", "act", "slope", "firstb")

        def ffn(low, i, carry):
            at = lanes(i * 2 * TILE, 2 * TILE)
            da = mm_right_t(v.dfeed[...], v.nar[at, :])
            d = (v.slope[:, at].astype(F32) * da).astype(BF16)
            dh[:, at] = d
            d_narrow = mm_left_t(v.act[:, at], v.dfeed[...])
            d_widen = mm_left_t(v.firstb[...], d)
            d_bias = jnp.sum(d.astype(F32), axis=0, keepdims=True)
            for half in range(2):
                j, part = 2 * i + half, slice(half * TILE, (half + 1) * TILE)
                place = lanes(lax.rem(j, 3) * TILE, TILE)
                v.wbias[pl.ds(j, 1), :] = d_bias[:, part]
                self.put_rows(j - low, d_narrow[part, :], grad.at[2 * (j // 3), place, :])
                self.put_cols(j - low, d_widen[:, part], grad.at[2 * (j // 3) + 1, :, place])
            return carry

        def tiles(low, high):
            lax.fori_loop(low // 2, high // 2, functools.partial(ffn, low), 0)
            self.drain_rows(grad)
            self.drain_cols(grad)

        def first_grad():
            self.wait_saved(restored, "wid")

            def body(j, carry):
                at = lanes(j * TILE, TILE)
                ds[:, at] = ds[:, at] + mm_right_t(dh[...], v.wid[at, :])
                return carry

            lax.fori_loop(0, width // TILE, body, 0)

        def first():
            self.wait_saved(restored, "xhat1")
            self.norms(vec, ds, v.xhat1, 0, 3, dres, dbr, 3)

        def out_grad():
            self.wait_saved(restored, "mixed", "wout", "rinv")

            def body(j, carry):
                at = lanes(j * TILE, TILE)
                self.put_cols(j, mm_left_t(v.mixed[...], dbr[:, at]), grad.at[OUT, :, at])
                d = mm_right_t(dbr[...], v.wout[at, :]).astype(BF16).astype(F32)
                v.dm[:, at] = (d * v.rinv[:, at]).astype(BF16)
                return carry

            lax.fori_loop(0, width // TILE, body, 0)
            self.drain_cols(grad)

        def pair(p, carry):
            low = lax.broadcasted_iota(jnp.int32, (self.length, 128), 1) < HEAD_DIM
            slot = lax.rem(p, 2)

            @pl.when(p + 1 < HEADS // 2)
            def _():
                self.e_load(layer, p + 1, 1 - slot).start()

            at_q, at_k, at_v = lanes(p * 128, 128), lanes(width + p * 128, 128), lanes(2 * width + p * 128, 128)
            q, k, values = v.qkv[:, at_q], v.qkv[:, at_k], v.qkv[:, at_v]
            d = v.dm[:, at_q]
            prod = d.astype(F32) * v.mixed[:, at_q].astype(F32)
            self.e_load(layer, p, slot).wait()
            dq, dk, dv = [], [], []
            for i in range(2):
                mine = low if i == 0 else ~low
                delta = jnp.sum(jnp.where(mine, prod, 0.0), axis=1, keepdims=True)
                dp = mm_right_t(jnp.where(mine, d, BF16(0)), values)
                e = v.e[slot, i]
                s = (e.astype(F32) * (dp - delta)).astype(BF16)
                dq.append(mm(s, k))
                dk.append(mm_left_t(s, q))
                dv.append(mm_left_t(e, d))
            dqkv[:, at_q] = (jnp.where(low, dq[0], dq[1]) * HEAD_DIM**-0.5).astype(BF16)
            dqkv[:, at_k] = jnp.where(low, dk[0], dk[1]).astype(BF16)
            dqkv[:, at_v] = jnp.where(low, dv[0], dv[1]).astype(BF16)
            return carry

        def pairs(low, high):
            if low == 0:
                self.wait_saved(restored, "qkv")
            lax.fori_loop(low, high, pair, 0)

        def in_grad(low, high):
            if restored and low == 0:
                self.load_input(self.a.hidden).wait()

            def body(j, carry):
                at = lanes(j * TILE, TILE)
                place = lanes(lax.rem(j, 3) * TILE, TILE)
                self.put_cols(j - low, mm_left_t(v.h[...], dqkv[:, at]), grad.at[IN + j // 3, :, place])
                return carry

            lax.fori_loop(low, high, body, 0)
            self.drain_cols(grad)

        def input_grad():
            self.wait_saved(restored, "win")

            def body(j, carry):
                at = lanes(j * TILE, TILE)
                d = dres[:, at] + mm_right_t(dqkv[...], v.win[at, :])
                dres[:, at] = d
                if layer == 1:
                    v.g[:, at] = d.astype(BF16)
                return carry

            lax.fori_loop(0, width // TILE, body, 0)
            pl.when(self.section == layer)(lambda: self.din_kept(dres).start())
            pl.when(self.section != layer)(lambda: self.din_sent(dres).start())
            small[16:17, :] = jnp.sum(dqkv[:, 0:width].astype(F32), axis=0, keepdims=True)
            small[17:18, :] = jnp.sum(dqkv[:, 2 * width :].astype(F32), axis=0, keepdims=True)
            for i, source in enumerate((5, 3, 0, 4, 1)):
                small[18 + i : 19 + i, :] = v.sums[source : source + 1, :]
            for i in range(self.ff // TILE):
                small[23 + i // 3 : 24 + i // 3, (i % 3) * TILE : (i % 3 + 1) * TILE] = v.wbias[i : i + 1, :]
            small[27:28, :] = v.sums[2:3, :]
            small[28:32, :] = jnp.zeros((4, width), F32)
            pl.when(self.section == layer)(lambda: self.din_kept(dres).wait())
            pl.when(self.section != layer)(lambda: self.din_sent(dres).wait_send())

        return Refs(
            second=second, tiles=tiles, first_grad=first_grad, first=first, out_grad=out_grad, pairs=pairs, in_grad=in_grad,
            input_grad=input_grad,
        )


def sum_plan(devices, rows):
    side = round((devices / 2) ** (1 / 3))
    extents = [side, side, devices // (side * side)]
    axes, stride = [], 1
    for extent in extents:
        steps, step = [], 1
        while step < extent:
            steps.append(stride * step)
            step *= 2
        axes.append(steps)
        stride *= extent
    x, y, z = axes
    distances = x + y + z
    swaps = lambda order, active=None: [("swap", distance, active) for distance in order]
    unit = 256 if devices <= 16 else 128
    run = 5 * unit // 2
    count, over = rows // run, rows % run
    return [
        (0, unit, count + (over >= unit), swaps(y + x + z)),
        (unit, unit, count + (over >= 2 * unit), swaps(x + y + z)),
        (2 * unit, unit // 2, count, swaps(z + x + y)),
    ], distances, None


class Stage:
    def __init__(self, kind, rows, cols, send, to, recv, source, sent, got):
        self.kind, self.rows, self.cols = kind, rows, cols
        self.send, self.to, self.recv, self.source, self.sent, self.got = send, to, recv, source, sent, got


def message_shapes(unit, width, spec):
    rows, cols, shapes = unit // 2, width, []
    for i, (kind, arg, _) in enumerate(spec):
        if kind == "chain":
            if arg == 0:
                rows //= 2
        elif kind != "fold":
            if rows >= 32:
                rows //= 2
            elif cols == width:
                cols //= 2
            else:
                kind = "full"
        shapes.append((kind, rows, cols))
    return shapes


def build_stages(unit, width, spec, me, line):
    rows, cols = unit // 2, width
    row = col = me * 0
    if line is not None:
        stride, depth = line
        z = me // stride
    flag = lambda condition: condition.astype(jnp.int32)
    stages = []
    for kind, arg, active in spec:
        if kind == "fold":
            first, third = flag(z == arg), flag(z == arg + 1)
            send, recv = (z == arg) | (z == depth - 1 - arg), (z == arg + 1) | (z == depth - 2 - arg)
            place = (row, col)
            stages.append(Stage(
                kind, rows, cols, send, me + stride * (2 * first - 1), recv, me + stride * (1 - 2 * third), place, place
            ))
        elif kind == "chain":
            if arg == 0:
                rows //= 2
                base = row
            up, came = flag(z == arg), flag(z == arg + 1)
            send, recv = (z == arg) | (z == depth - 1 - arg), (z == arg + 1) | (z == depth - 2 - arg)
            stages.append(Stage(
                kind, rows, cols, send, me + stride * (2 * up - 1), recv, me + stride * (1 - 2 * came),
                (base + up * rows, col), (base + came * rows, col),
            ))
            if arg == depth - 2:
                row = base + flag(z == depth - 1) * rows
        else:
            if kind == "middle":
                bit, distance = flag(z >= depth // 2), stride
                active = "middle"
            else:
                bit, distance = lax.rem(me // arg, 2), arg
            if active == "middle":
                on = (z == depth // 2 - 1) | (z == depth // 2)
            elif active == "ends":
                on = (z == 0) | (z == depth - 1)
            else:
                on = None
            partner = me + distance * (1 - 2 * bit)
            sent = (row, col)
            kind = "swap"
            if rows >= 32:
                rows //= 2
                sent, row = (row + (1 - bit) * rows, col), row + bit * rows
            elif cols == width:
                cols //= 2
                sent, col = (row, col + (1 - bit) * cols), col + bit * cols
            else:
                kind = "full"
            stages.append(Stage(kind, rows, cols, on, partner, on, partner, sent, (row, col)))
    return stages


def when(condition, action):
    if condition is None:
        action()
    else:
        pl.when(condition)(action)


class GradientSum:
    def __init__(self, plan, distances, line, width, grads, out, buffers, sems):
        self.plan, self.distances, self.line, self.width, self.grads, self.out = plan, distances, line, width, grads, out
        self.run = sum(unit for _, unit, _, _ in plan)
        self.section, self.me = lax.axis_index("section"), lax.axis_index("dp")
        self.peer = (1 - self.section, self.me)
        self.parts = [build_stages(unit, width, spec, self.me, line) for _, unit, _, spec in plan]
        self.slots = [slots_of(spec) for _, _, _, spec in plan]
        self.total, self.other, self.recvs, self.fulls = buffers
        self.keep_sems, self.pair_sems, self.trade_sems, self.end_sems, self.send_sems, self.rs_sems, self.ag_sems = sems[:7]
        self.free, self.full_free = sems[7:]
        self.length = max(2 * count + 2 * len(spec) + 2 for _, _, count, spec in plan)

    def partner(self, distance):
        return (self.section, self.me + distance * (1 - 2 * lax.rem(self.me // distance, 2)))

    def barrier(self):
        barrier = pltpu.get_barrier_semaphore()
        for device in [self.peer] + [self.partner(distance) for distance in self.distances]:
            pl.semaphore_signal(barrier, inc=1, device_id=device, device_id_type=MESH)
        neighbours = []
        if self.line is not None:
            stride, depth = self.line
            z = self.me // stride
            neighbours = [(z > 0, -stride), (z < depth - 1, stride)]
        for there, distance in neighbours:

            @pl.when(there)
            def _(distance=distance):
                pl.semaphore_signal(
                    barrier, inc=1, device_id=(self.section, self.me + distance), device_id_type=MESH
                )

        pl.semaphore_wait(barrier, len(self.distances) + 1)
        for there, _ in neighbours:
            pl.when(there)(lambda: pl.semaphore_wait(barrier, 1))

    def slot(self, part, k):
        return lax.rem(k, self.slots[part])

    def stage_slot(self, part, k, s):
        return lax.rem(k, stage_slots_of(self.plan[part][3], s))

    def half_rows(self, ref, part, k, which):
        base, unit, count, _ = self.plan[part]
        row = base + lax.rem(k, count) * self.run + which * (unit // 2)
        return ref.at[row // self.width, pl.ds(pl.multiple_of(lax.rem(row, self.width), 16), unit // 2)]

    def load(self, part, k, source):
        slot = self.slot(part, k)
        return pltpu.make_async_copy(
            self.half_rows(source, part, k, self.section), self.total[part].at[slot], self.keep_sems[part].at[slot]
        )

    def trade(self, part, k, source):
        slot = self.slot(part, k)
        return pltpu.make_async_remote_copy(
            src_ref=self.half_rows(source, part, k, 1 - self.section), dst_ref=self.other[part].at[slot],
            send_sem=self.pair_sems[part].at[slot], recv_sem=self.trade_sems[part].at[slot],
            device_id=self.peer, device_id_type=MESH,
        )

    def keep(self, part, k):
        slot = self.slot(part, k)
        return pltpu.make_async_copy(
            self.other[part].at[slot], self.half_rows(self.out, part, k, self.section), self.keep_sems[part].at[slot]
        )

    def hand_over(self, part, k):
        slot = self.slot(part, k)
        return pltpu.make_async_remote_copy(
            src_ref=self.other[part].at[slot], dst_ref=self.half_rows(self.out, part, k, self.section),
            send_sem=self.pair_sems[part].at[slot], recv_sem=self.end_sems[part].at[slot],
            device_id=self.peer, device_id_type=MESH,
        )

    def view(self, ref, slot, stage, place):
        row, col = place
        at = pl.ds(pl.multiple_of(row, 16), stage.rows)
        if stage.cols == self.width:
            return ref.at[slot, at]
        return ref.at[slot, at, pl.ds(pl.multiple_of(col, 128), stage.cols)]

    def held(self, part, k, s, place):
        stages = self.parts[part]
        fulls = [i for i in range(s + 1) if stages[i].kind == "full"]
        if fulls:
            return self.fulls[part][fulls[-1]].at[self.slot(part, k)]
        return self.view(self.total[part], self.slot(part, k), stages[s], place)

    def reduce_copy(self, part, k, s, device):
        stage = self.parts[part][s]
        at = self.stage_slot(part, k, s)
        if stage.kind == "full":
            source = self.held(part, k, s - 1, self.parts[part][s - 1].got)
        else:
            source = self.view(self.total[part], self.slot(part, k), stage, stage.sent)
        return pltpu.make_async_remote_copy(
            src_ref=source, dst_ref=self.recvs[part][s].at[at],
            send_sem=self.send_sems[part][s].at[self.slot(part, k)], recv_sem=self.rs_sems[part][s].at[at],
            device_id=(self.section, device), device_id_type=MESH,
        )

    def gather_copy(self, part, k, s, device, place):
        stage = self.parts[part][s]
        ref = self.view(self.other[part], self.slot(part, k), stage, place)
        return pltpu.make_async_remote_copy(
            src_ref=ref, dst_ref=ref, send_sem=self.send_sems[part][s].at[self.slot(part, k)],
            recv_sem=self.ag_sems[part][s].at[self.stage_slot(part, k, s)],
            device_id=(self.section, device), device_id_type=MESH,
        )

    def start_reduce(self, part, k, s):
        stage = self.parts[part][s]

        def action():
            if stage.kind == "full":

                @pl.when(k >= stage_slots_of(self.plan[part][3], s))
                def _():
                    pl.semaphore_wait(self.full_free[part][s].at[0], 1)

            self.reduce_copy(part, k, s, stage.to).start()

        when(stage.send, action)

    def end_reduce(self, part, k, s):
        stage = self.parts[part][s]
        slot, at = self.slot(part, k), self.stage_slot(part, k, s)
        last = len(self.parts[part]) - 1

        def action():
            self.reduce_copy(part, k, s, stage.source).wait_recv()
            if stage.kind == "full":
                left = self.held(part, k, s - 1, self.parts[part][s - 1].got)
            else:
                left = self.view(self.total[part], slot, stage, stage.got)
            target = self.view(self.other[part], slot, stage, stage.got) if s == last else self.held(part, k, s, stage.got)
            self.add(target, left, self.recvs[part][s].at[at], stage.rows)
            if stage.kind == "full":

                @pl.when(k + stage_slots_of(self.plan[part][3], s) < 2 * self.plan[part][2])
                def _():
                    pl.semaphore_signal(
                        self.full_free[part][s].at[0], inc=1, device_id=(self.section, stage.source),
                        device_id_type=MESH,
                    )

        when(stage.recv, action)

    def start_gather(self, part, k, s):
        stage = self.parts[part][s]
        if stage.kind == "full":
            return
        when(stage.send, lambda: self.reduce_copy(part, k, s, stage.to).wait_send())
        when(stage.recv, lambda: self.gather_copy(part, k, s, stage.source, stage.got).start())

    def end_gather(self, part, k, s):
        stage = self.parts[part][s]
        if stage.kind != "full":
            when(stage.send, lambda: self.gather_copy(part, k, s, stage.to, stage.sent).wait_recv())

    def owned(self, part, k):
        return (k < self.plan[part][2]) == (self.section == 1)

    def add(self, target, left, right, rows):
        block = min(rows, 32)

        def body(i, carry):
            at = pl.ds(pl.multiple_of(i * block, 16), block)
            target[at, :] = left[at, :] + right[at, :]
            return carry

        lax.fori_loop(0, rows // block, body, 0)

    def retire(self, part, k):
        for s, stage in enumerate(self.parts[part]):
            if stage.kind == "full":
                when(stage.send, lambda s=s, stage=stage: self.reduce_copy(part, k, s, stage.to).wait_send())
            else:
                when(stage.recv, lambda s=s, stage=stage: self.gather_copy(part, k, s, stage.source, stage.got).wait_send())
        mine = self.owned(part, k)
        pl.when(mine)(lambda: self.keep(part, k).wait())
        pl.when(jnp.logical_not(mine))(lambda: self.hand_over(part, k).wait_send())

    def task(self, part, k, s):
        last = len(self.parts[part]) - 1
        slots, count = self.slots[part], self.plan[part][2]
        if s == 0:

            @pl.when(k >= slots)
            def _():
                self.retire(part, k - slots)
                pl.semaphore_signal(self.free.at[part], inc=1, device_id=self.peer, device_id_type=MESH)
                pl.semaphore_wait(self.free.at[part], 1)

            first = k < count

            @pl.when(first)
            def _():
                self.load(part, k, self.grads[1]).start()
                self.trade(part, k, self.grads[1]).start()

            @pl.when(jnp.logical_not(first))
            def _():
                self.load(part, k, self.grads[0]).start()
                self.trade(part, k, self.grads[0]).start()

        elif s == 1:
            self.load(part, k, self.grads[0]).wait()
            self.trade(part, k, self.grads[0]).wait_recv()
            total = self.total[part].at[self.slot(part, k)]
            self.add(total, total, self.other[part].at[self.slot(part, k)], self.plan[part][1] // 2)
            self.start_reduce(part, k, 0)
        elif s <= last + 2:
            self.end_reduce(part, k, s - 2)
            if s - 1 <= last:
                self.start_reduce(part, k, s - 1)
            else:
                self.start_gather(part, k, last)
        elif s <= 2 * last + 3:
            j = 2 * last + 3 - s
            self.end_gather(part, k, j)
            if j > 0:
                self.start_gather(part, k, j - 1)
            else:
                self.trade(part, k, self.grads[0]).wait_send()
                mine = self.owned(part, k)
                pl.when(mine)(lambda: self.keep(part, k).start())
                pl.when(jnp.logical_not(mine))(lambda: self.hand_over(part, k).start())
        else:
            pl.when(self.owned(part, k))(lambda: self.hand_over(part, k).wait_recv())

    def step(self, t):
        most = max(len(stages) for stages in self.parts)
        for s in range(2 * most + 3):
            for part, (_, _, count, spec) in enumerate(self.plan):
                if s < 2 * len(spec) + 3:
                    k = t - s
                    pl.when((k >= 0) & (k < 2 * count))(lambda part=part, s=s, k=k: self.task(part, k, s))

    def finish(self):
        for part, (_, _, count, _) in enumerate(self.plan):

            def body(k, carry, part=part):
                self.retire(part, k)
                return carry

            lax.fori_loop(max(2 * count - self.slots[part], 0), 2 * count, body, 0)


def slots_of(spec):
    return 2 * len(spec) + 3


def stage_slots_of(spec, s):
    return 2 * (len(spec) - s) + 1


def sum_scratch(plan, width):
    shapes, names = [], []

    def need(name, part, s, shape):
        names.append((name, part, s))
        shapes.append(shape)

    for part, (_, unit, _, spec) in enumerate(plan):
        slots = slots_of(spec)
        steps = message_shapes(unit, width, spec)
        for name in ("total", "other"):
            need(name, part, 0, pltpu.VMEM((slots, unit // 2, width), BF16))
        for name in ("keep", "pair", "trade", "end"):
            need(name, part, 0, pltpu.SemaphoreType.DMA((slots,)))
        for s, (kind, rows, cols) in enumerate(steps):
            at = stage_slots_of(spec, s)
            need("recv", part, s, pltpu.VMEM((at, rows, cols), BF16))
            need("send", part, s, pltpu.SemaphoreType.DMA((slots,)))
            need("rs", part, s, pltpu.SemaphoreType.DMA((at,)))
            if kind == "full":
                need("full_free", part, s, pltpu.SemaphoreType.REGULAR((1,)))
                if s < len(steps) - 1:
                    need("full", part, s, pltpu.VMEM((slots, rows, cols), BF16))
            else:
                need("ag", part, s, pltpu.SemaphoreType.DMA((at,)))
    need("free", 0, 0, pltpu.SemaphoreType.REGULAR((len(plan),)))

    def split(refs):
        by_name = {}
        for (name, part, s), ref in zip(names, refs):
            by_name.setdefault(name, {}).setdefault(part, {})[s] = ref
        one = lambda name: [by_name[name][part][0] for part in range(len(plan))]
        many = lambda name: [by_name.get(name, {}).get(part, {}) for part in range(len(plan))]
        buffers = (one("total"), one("other"), many("recv"), many("full"))
        sems = (
            one("keep"), one("pair"), one("trade"), one("end"), many("send"), many("rs"), many("ag"),
            by_name["free"][0][0], many("full_free"),
        )
        return buffers, sems

    return shapes, split


def layers_kernel(plan, distances, line, split, *refs):
    refs = list(refs)
    take = lambda n: [refs.pop(0) for _ in range(n)]
    valid_ref, cls_ref, seg_ref, proj_bias, out_shift, gains, shifts, widen_bias, narrow_bias = take(9)
    hidden, cotangent = take(2)
    own = take(4)
    out, din_kept, din_got, small_got, small_sum, small_mine = take(6)
    grad0, grad1, e_hbm = take(3)
    saved = take(9)
    v = Refs(**dict(zip(VMEM_NAMES, take(len(VMEM_NAMES)))))
    small_send, small_acc, small_recv = take(3)
    weight_sems, sent_sems, arrived_sems, free_sems, saved_sems, e_sems, h_sems, stage_sems, vec_sems, small_sems = take(10)
    din_sems, = take(1)
    section = lax.axis_index("section")
    width = v.h.shape[1]
    total = GradientSum(plan, distances, line, width, (grad0, grad1), out, *split(refs))
    compute = Compute(
        v,
        Refs(own=own, other=total.peer, saved=saved, e=e_hbm, hidden=hidden, din_kept=din_kept, din_got=din_got),
        Refs(
            weights=weight_sems, sent=sent_sems, arrived=arrived_sems, free=free_sems, saved=saved_sems, e=e_sems, h=h_sems,
            stage=stage_sems, din=din_sems,
        ),
        section, valid_ref[section], [cls_ref[section, i] for i in range(8)],
    )

    def vec_sent():
        return pltpu.make_async_remote_copy(
            src_ref=v.vec_own, dst_ref=v.vec_peer, send_sem=vec_sems.at[0], recv_sem=vec_sems.at[1],
            device_id=total.peer, device_id_type=MESH,
        )

    compute.load_input(hidden).start()
    v.vec_own[0:2, :] = proj_bias[0]
    v.vec_own[2:3, :] = out_shift[...]
    v.vec_own[3:5, :] = gains[0]
    v.vec_own[5:7, :] = shifts[0]
    v.vec_own[7:11, :] = jnp.zeros((4, width), F32)
    v.vec_own[11:12, :] = narrow_bias[...]
    v.vec_own[12:24, :] = jnp.zeros((12, width), F32)
    for i in range(widen_bias.shape[1] // TILE):
        v.vec_own[12 + i : 13 + i, 0:TILE] = widen_bias[:, i * TILE : (i + 1) * TILE]
    total.barrier()
    vec_sent().start()
    compute.start_weight(0, "win", 0)
    compute.start_weight(0, "wout", 0)
    for q in range(compute.pieces("wid")):
        compute.start_weight(0, "wid", 0, q)
        compute.start_weight(0, "nar", 0, q)
    segments = seg_ref[pl.ds(section, 1), :]
    columns = jnp.broadcast_to(segments.astype(F32), (128, compute.length)).T[:, :1]
    v.bias[...] = jnp.where(columns == segments.astype(F32), 0.0, MASKED)
    compute.load_cotangent(cotangent).start()
    vec_sent().wait_recv()
    for layer in range(2):
        v.vec[layer] = jnp.where(section == layer, v.vec_own[...], v.vec_peer[...])
    compute.load_input(hidden).wait()

    small0, small1 = v.small.at[0], v.small.at[1]
    compute.forward(0, small0)
    compute.forward(1, small1)
    compute.e_drain(1)
    compute.e_load(1, 0, 0).start()
    compute.load_cotangent(cotangent).wait()

    rounds = len(distances)

    def small_trade():
        return pltpu.make_async_remote_copy(
            src_ref=small_send, dst_ref=small_got, send_sem=small_sems.at[0, rounds], recv_sem=small_sems.at[1, rounds],
            device_id=total.peer, device_id_type=MESH,
        )

    def small_copy(i):
        return pltpu.make_async_remote_copy(
            src_ref=small_acc.at[i], dst_ref=small_recv.at[i], send_sem=small_sems.at[0, i],
            recv_sem=small_sems.at[1, i], device_id=total.partner(distances[i]), device_id_type=MESH,
        )

    def small_start():
        small_mine[...] = jnp.where(section == 0, small0[...], small1[...])
        small_send[...] = jnp.where(section == 0, small1[...], small0[...])
        small_trade().start()

    def small_step(stage):
        if stage == 0:
            small_trade().wait_recv()
            small_acc[0] = small_mine[8:, :] + small_got[8:, :]
        else:
            small_copy(stage - 1).wait_recv()
            small_acc[stage] = small_acc[stage - 1] + small_recv[stage - 1]
        if stage < rounds:
            small_copy(stage).start()
        else:
            small_sum[...] = small_acc[stage]

    one = compute.backward(1, grad1, small1)
    zero = compute.backward(0, grad0, small0)
    restore = compute.restore
    one.second()
    one.tiles(0, 4)
    do = functools.partial
    events = [
        [do(one.tiles, 4, 6)],
        [do(one.tiles, 6, 8)],
        [do(one.tiles, 8, 10)],
        [do(one.tiles, 10, 12), do(restore, "nar", "act", "firstb", "xhat2")],
        [one.first_grad, do(restore, "slope", "wid")],
        [one.first, do(restore, "xhat1", "rr"), one.out_grad, do(restore, "wout", "rinv")],
        [do(one.pairs, 0, 2)],
        [do(one.pairs, 2, 4)],
        [do(one.pairs, 4, 6), do(restore, "mixed"), lambda: compute.e_load(0, 0, 0).start()],
        [do(one.in_grad, 0, 5)],
        [do(one.in_grad, 5, 9), lambda: compute.load_input(hidden).start()],
        [one.input_grad, do(restore, "qkv", "win"), zero.second],
        [do(zero.tiles, 0, 4)],
        [do(zero.tiles, 4, 6)],
        [do(zero.tiles, 6, 10)],
        [do(zero.tiles, 10, 12)],
        [zero.first_grad],
        [zero.first, zero.out_grad],
        [do(zero.pairs, 0, 2)],
        [do(zero.pairs, 2, 4)],
        [do(zero.pairs, 4, 6)],
        [do(zero.in_grad, 0, 5)],
        [do(zero.in_grad, 5, 9)],
        [zero.input_grad, small_start],
    ] + [[do(small_step, s)] for s in range(rounds + 1)]

    def body(t, carry):
        total.step(t)
        for i, event in enumerate(events):

            @pl.when(t == i)
            def _(event=event):
                for action in event:
                    action()

        return carry

    lax.fori_loop(0, total.length, body, 0)
    total.finish()
    vec_sent().wait_send()
    for name in WEIGHTS:
        for q in range(compute.pieces(name)):
            compute.weight_sent(name, q).wait_send()
    small_trade().wait_send()
    for i in range(rounds):
        small_copy(i).wait_send()
    compute.din_sent(v.feed).wait_recv()


VMEM_NAMES = (
    "h", "g", "win", "wout", "wid", "nar", "qkv", "e", "rinv", "mixed", "xhat1", "rr", "first", "firstb", "act", "slope",
    "xhat2", "feed", "bias", "dfeed", "dm", "row_stage", "col_stage", "wbias", "sums", "vec", "vec_own", "vec_peer", "small",
)


def layers(valid_counts, cls_positions, segment_ids, vectors, hidden, cotangent, own):
    rows, length = segment_ids.shape
    width, ff = hidden.shape[1], own[2].shape[2]
    devices = lax.axis_size("dp")
    plan, distances, line = sum_plan(devices, 12 * width)
    stages = len(distances)
    shapes, split = sum_scratch(plan, width)
    row_b, row_f = ((length, width), BF16), ((length, width), F32)
    saved = [
        ((length, 3 * width), BF16), row_f, row_b, row_f, ((2, length, 128), F32), row_b, ((length, ff), BF16),
        ((length, ff), BF16), row_f,
    ]
    grad = ((12, width, width), BF16)
    small = ((32, width), F32)
    sums = (24, width)
    outs = [grad, row_f, row_f, small, (sums, F32), small, grad, grad, ((2, HEADS, length, length), BF16), *saved]
    scratch = dict(
        h=row_b, g=row_b, win=(own[0].shape[1:], BF16), wout=(own[1].shape[1:], BF16), wid=(own[2].shape[1:], BF16),
        nar=(own[3].shape[1:], BF16), qkv=saved[0], e=((2, 2, length, length), BF16), rinv=row_f, mixed=row_b, xhat1=row_f,
        rr=saved[4], first=row_f, firstb=row_b, act=saved[6], slope=saved[7], xhat2=row_f, feed=row_f,
        bias=((length, length), F32), dfeed=row_b, dm=row_b, row_stage=((2, TILE, width), BF16),
        col_stage=((2, width, TILE), BF16), wbias=((16, TILE), F32), sums=((8, width), F32), vec=((2, 24, width), F32),
        vec_own=((24, width), F32), vec_peer=((24, width), F32), small=((2, 32, width), F32),
    )
    in_vmem = (3, 4, 5)
    got = pl.pallas_call(
        functools.partial(layers_kernel, plan, distances, line, split),
        out_shape=[jax.ShapeDtypeStruct(s, d) for s, d in outs],
        in_specs=[SMEM, SMEM] + [VMEM] * 7 + [ANY] * 6,
        out_specs=[VMEM if i in in_vmem else ANY for i in range(len(outs))],
        scratch_shapes=[
            *[pltpu.VMEM(*scratch[name]) for name in VMEM_NAMES],
            pltpu.VMEM(*small),
            pltpu.VMEM((stages + 1, *sums), F32),
            pltpu.VMEM((stages, *sums), F32),
            pltpu.SemaphoreType.DMA((10,)),
            pltpu.SemaphoreType.DMA((10,)),
            pltpu.SemaphoreType.DMA((10,)),
            pltpu.SemaphoreType.REGULAR((4,)),
            pltpu.SemaphoreType.DMA((9,)),
            pltpu.SemaphoreType.DMA((2,)),
            pltpu.SemaphoreType.DMA((3,)),
            pltpu.SemaphoreType.DMA((4,)),
            pltpu.SemaphoreType.DMA((2,)),
            pltpu.SemaphoreType.DMA((2, stages + 1)),
            pltpu.SemaphoreType.DMA((2,)),
            *shapes,
        ],
        compiler_params=pltpu.CompilerParams(collective_id=0, has_side_effects=True, vmem_limit_bytes=63 * MIB),
        cost_estimate=pl.CostEstimate(flops=54 * 10**9, bytes_accessed=200 * 10**6, transcendentals=10**7),
        name="layers_and_sum",
    )(valid_counts, cls_positions, segment_ids, *vectors, hidden, cotangent, *own)
    return got[:6]


def finish_kernel(
    flags, blocks, din_kept, din_got, small_mine, small_got, small_sum,
    cls_o, input_o, in_o, bias_o, out_o, out_shift_o, gain_o, shift_o, widen_o, widen_bias_o, narrow_o, narrow_bias_o, rms_o,
    dins, halves, wide, block_sems, din_sems, wide_sems,
):
    section = flags[0]
    got_row = 1 - section
    length, width = din_got.shape
    slots = wide.shape[0]

    def rows(row):
        return input_o.at[0, pl.ds(pl.multiple_of(row * length, 16), length)]

    def target(index):
        part = slice(index // 2 * width, (index // 2 + 1) * width)
        if index >= IN:
            return in_o.at[0, :, (index - IN) * width : (index - IN + 1) * width]
        if index == OUT:
            return out_o.at[0]
        return narrow_o.at[0, part, :] if index % 2 == 0 else widen_o.at[0, :, part]

    loads = [pltpu.make_async_copy(blocks.at[i], halves.at[i], block_sems.at[i]) for i in range(12)]
    stores = [pltpu.make_async_copy(wide.at[i % slots], target(i), wide_sems.at[i % slots]) for i in range(12)]
    din_loads = [pltpu.make_async_copy(din, dins.at[i], din_sems.at[i]) for i, din in enumerate((din_kept, din_got))]
    din_stores = [
        pltpu.make_async_copy(dins.at[i], rows(row), din_sems.at[i]) for i, row in enumerate((section, got_row))
    ]
    for copy in loads[:2] + din_loads + loads[2:]:
        copy.start()
    cls_o[0, section] = small_mine[0:8, :]
    cls_o[0, got_row] = small_got[0:8, :]
    bias_o[0] = small_sum[8:10, :]
    out_shift_o[...] = small_sum[10:11, :]
    gain_o[0] = small_sum[11:13, :]
    shift_o[0] = small_sum[13:15, :]
    for i in range(4):
        widen_bias_o[0:1, i * width : (i + 1) * width] = small_sum[15 + i : 16 + i, :]
    narrow_bias_o[...] = small_sum[19:20, :]
    for i in range(3):
        squares = jnp.sum(small_sum[i : i + 1, :], axis=1, keepdims=True)
        rms_o[0:1, i : i + 1] = jnp.sqrt(squares / (small_sum[3:4, 0:1] * width))

    for i in range(12):
        loads[i].wait()
        if i >= slots:
            stores[i - slots].wait()

        def widen_rows(b, carry, i=i):
            at = rows_of(b, 64)
            wide[i % slots, at, :] = halves[i, at, :].astype(F32)
            return carry

        lax.fori_loop(0, width // 64, widen_rows, 0)
        stores[i].start()
        if i == 1:
            for load, store in zip(din_loads, din_stores):
                load.wait()
                store.start()
    for copy in stores[12 - slots :] + din_stores:
        copy.wait()


def finish(section, blocks, din_kept, din_got, small_mine, small_got, small_sum):
    length, width = din_got.shape
    shapes = [
        (1, 2, 8, width), (1, 2 * length, width), (1, width, 3 * width), (1, 2, width), (1, width, width), (1, width),
        (1, 2, width), (1, 2, width), (1, width, 4 * width), (1, 4 * width), (1, 4 * width, width), (1, width), (1, 3),
    ]
    big = (1, 2, 4, 8, 10)
    return pl.pallas_call(
        finish_kernel,
        out_shape=[jax.ShapeDtypeStruct(s, F32) for s in shapes],
        in_specs=[SMEM] + [ANY] * 3 + [VMEM] * 3,
        out_specs=[ANY if i in big else VMEM for i in range(len(shapes))],
        scratch_shapes=[
            pltpu.VMEM((2, length, width), F32),
            pltpu.VMEM(blocks.shape, BF16),
            pltpu.VMEM((6, width, width), F32),
            pltpu.SemaphoreType.DMA((12,)),
            pltpu.SemaphoreType.DMA((2,)),
            pltpu.SemaphoreType.DMA((6,)),
        ],
        compiler_params=pltpu.CompilerParams(vmem_limit_bytes=63 * MIB),
        cost_estimate=pl.CostEstimate(flops=10**7, bytes_accessed=46 * 10**6, transcendentals=0),
        name="finish",
    )(section[None], blocks, din_kept, din_got, small_mine, small_got, small_sum)


def local(
    hidden_in, segment_ids, cls_positions, valid_counts, proj_in, proj_bias, proj_out, out_shift, norm_gains,
    norm_shifts, widen, widen_bias, narrow, narrow_bias, cotangent,
):
    section = lax.axis_index("section")
    vectors = (proj_bias, out_shift, norm_gains, norm_shifts, widen_bias, narrow_bias)
    blocks, din_kept, din_got, small_got, small_sum, small_mine = layers(
        valid_counts, cls_positions, segment_ids, vectors, hidden_in, cotangent, (proj_in, proj_out, widen, narrow)
    )
    return finish(section, blocks, din_kept, din_got, small_mine, small_got, small_sum)


def solution(mesh):
    placed = (
        P("dp", None),
        P("dp", None),
        P("dp", None),
        P("dp"),
        P("section", None, None),
        P("section", None, None),
        P("section", None, None),
        P("section", None),
        P("section", None, None),
        P("section", None, None),
        P("section", None, None),
        P("section", None),
        P("section", None, None),
        P("section", None),
        P("dp", None),
    )
    return jax.shard_map(
        local,
        mesh=mesh,
        in_specs=placed,
        out_specs=(
            P("section", "dp", None, None),
            P("section", "dp", None),
            P("section", None, None),
            P("section", None, None),
            P("section", None, None),
            P("section", None),
            P("section", None, None),
            P("section", None, None),
            P("section", None, None),
            P("section", None),
            P("section", None, None),
            P("section", None),
            P("section", None),
        ),
        check_vma=False,
    )
```

```python
import functools

import jax
import jax.numpy as jnp
from jax import lax
from jax.experimental import pallas as pl
from jax.experimental.pallas import tpu as pltpu
from jax.sharding import PartitionSpec as P

HEADS = 12
HEAD_DIM = 64
EPSILON = 1e-12
MASKED = -1e30
F32 = jnp.float32
BF16 = jnp.bfloat16
MIB = 2**20
TILE = 256
BLOCK = 128
ANY = pl.BlockSpec(memory_space=pl.ANY)
VMEM = pl.BlockSpec(memory_space=pltpu.VMEM)
SMEM = pl.BlockSpec(memory_space=pltpu.SMEM)
MESH = pl.DeviceIdType.MESH
OUT, IN = 8, 9


def mm(left, right):
    return jnp.dot(left, right, preferred_element_type=F32)


def mm_left_t(left, right):
    return lax.dot_general(left, right, (((0,), (0,)), ((), ())), preferred_element_type=F32)


def mm_right_t(left, right):
    return lax.dot_general(left, right, (((1,), (1,)), ((), ())), preferred_element_type=F32)


def lanes(start, size):
    return pl.ds(pl.multiple_of(start, size), size)


def rows_of(b, size):
    return pl.ds(pl.multiple_of(b * size, size), size)


def gelu_and_slope(v):
    z = jnp.abs(v) * 0.7071067811865476
    t = 1.0 / (1.0 + 0.3275911 * z)
    e = jnp.exp(-0.5 * v * v)
    poly = t * (
        0.127414796 + t * (-0.142248368 + t * (0.7107068705 + t * (-0.7265760135 + t * 0.5307027145)))
    )
    tail = poly * e
    cdf = jnp.where(v >= 0, 1.0 - tail, tail)
    return v * cdf, cdf + v * e * 0.3989422804014327


def norm_back(up, x, f):
    return f * (up - jnp.mean(up, axis=1, keepdims=True) - x * jnp.mean(up * x, axis=1, keepdims=True))


class Refs:
    def __init__(self, **refs):
        self.__dict__.update(refs)


SAVED = ("qkv", "rinv", "mixed", "xhat1", "rr", "firstb", "act", "slope", "xhat2")
WEIGHTS = ("win", "wout", "wid", "nar")


class Compute:
    def __init__(self, v, a, sems, section, valid, cls_at):
        self.v, self.a, self.sems = v, a, sems
        self.section, self.valid, self.cls_at = section, valid, cls_at
        self.length, self.width = v.h.shape
        self.ff = v.wid.shape[1]

    def piece(self, name, q):
        i = WEIGHTS.index(name)
        source, target = self.a.own[i].at[0], getattr(self.v, name)
        if name == "wid":
            at = lanes(q * self.width, self.width)
            return source.at[:, at], target.at[:, at], 2 + q
        if name == "nar":
            at = rows_of(q, self.width)
            return source.at[at, :], target.at[at, :], 6 + q
        return source, target, i

    def pieces(self, name):
        return self.ff // self.width if name in ("wid", "nar") else 1

    def weight_copy(self, name, q):
        source, target, i = self.piece(name, q)
        return pltpu.make_async_copy(source, target, self.sems.weights.at[i])

    def weight_sent(self, name, q):
        source, target, i = self.piece(name, q)
        return pltpu.make_async_remote_copy(
            src_ref=source, dst_ref=target, send_sem=self.sems.sent.at[i], recv_sem=self.sems.arrived.at[i],
            device_id=self.a.other, device_id_type=MESH,
        )

    def start_weight(self, layer, name, use, q=None):
        i = WEIGHTS.index(name)

        @pl.when(self.section == layer)
        def _():
            some = range(self.pieces(name)) if q is None else (q,)
            for p in some:
                self.weight_copy(name, p).start()
            if use > 0:
                pl.semaphore_wait(self.sems.free.at[i], 1)
            for p in some:
                if use == 2:
                    self.weight_sent(name, p).wait_send()
                self.weight_sent(name, p).start()

        if use > 0:

            @pl.when(self.section != layer)
            def _():
                pl.semaphore_signal(self.sems.free.at[i], inc=1, device_id=self.a.other, device_id_type=MESH)

    def wait_piece(self, layer, name, q):
        pl.when(self.section == layer)(lambda: self.weight_copy(name, q).wait())
        pl.when(self.section != layer)(lambda: self.weight_sent(name, q).wait_recv())

    def wait_weight(self, layer, name):
        for q in range(self.pieces(name)):
            self.wait_piece(layer, name, q)

    def saving(self, name):
        i = SAVED.index(name)
        return pltpu.make_async_copy(getattr(self.v, name), self.a.saved[i], self.sems.saved.at[i])

    def restoring(self, name):
        i = SAVED.index(name)
        return pltpu.make_async_copy(self.a.saved[i], getattr(self.v, name), self.sems.saved.at[i])

    def load_input(self, layer_input):
        return pltpu.make_async_copy(layer_input.at[self.rows()], self.v.h, self.sems.h.at[0])

    def load_cotangent(self, cotangent):
        return pltpu.make_async_copy(cotangent.at[self.rows()], self.v.g, self.sems.h.at[1])

    def rows(self):
        return pl.ds(pl.multiple_of(self.section * self.length, self.length), self.length)

    def e_store(self, layer, p, slot):
        return pltpu.make_async_copy(
            self.v.e.at[slot], self.a.e.at[layer, pl.ds(2 * p, 2)], self.sems.e.at[slot]
        )

    def e_load(self, layer, p, slot):
        return pltpu.make_async_copy(
            self.a.e.at[layer, pl.ds(2 * p, 2)], self.v.e.at[slot], self.sems.e.at[slot]
        )

    def e_drain(self, layer):
        for slot in range(2):
            self.e_store(layer, 0, slot).wait()

    def forward(self, layer, small):
        v, width = self.v, self.width
        vec = v.vec.at[layer]
        again = layer == 1

        def before(*names):
            if again:
                for name in names:
                    self.saving(name).wait()

        def done(*names):
            if not again:
                for name in names:
                    self.saving(name).start()

        self.wait_weight(layer, "win")
        before("qkv")
        for part in range(3):
            shift = [vec[0:1, :], None, vec[1:2, :]][part]
            for j in range(width // TILE):
                at = part * width + j * TILE
                got = mm(v.h[...], v.win[:, at : at + TILE])
                if shift is not None:
                    got = got + shift[:, j * TILE : (j + 1) * TILE]
                got = got.astype(BF16)
                if part == 0:
                    got = got * BF16(HEAD_DIM**-0.5)
                v.qkv[:, at : at + TILE] = got
        done("qkv")
        if again:
            self.e_drain(0)
        else:
            self.start_weight(1, "win", 1)
        before("rinv", "mixed")
        low = lax.broadcasted_iota(jnp.int32, (self.length, 128), 1) < HEAD_DIM
        ones = jnp.ones((self.length, 128), BF16)

        def pair(p, carry):
            slot = lax.rem(p, 2)

            @pl.when(p >= 2)
            def _():
                self.e_store(layer, p, slot).wait()

            q = v.qkv[:, lanes(p * 128, 128)]
            k = v.qkv[:, lanes(width + p * 128, 128)]
            values = jnp.concatenate([v.qkv[:, lanes(2 * width + p * 128, 128)], ones], axis=1)
            outs = []
            for i in range(2):
                qm = jnp.where(low if i == 0 else ~low, q, BF16(0))
                s = mm_right_t(qm, k) + v.bias[...]
                top = jnp.max(s, axis=1, keepdims=True)
                e = jnp.exp(s - top).astype(BF16)
                v.e[slot, i] = e
                outs.append(mm(e, values))
            self.e_store(layer, p, slot).start()
            r0 = 1.0 / outs[0][:, 128:]
            r1 = 1.0 / outs[1][:, 128:]
            m = jnp.where(low, outs[0][:, :128] * r0, outs[1][:, :128] * r1)
            v.mixed[:, lanes(p * 128, 128)] = m.astype(BF16)
            v.rinv[:, lanes(p * 128, 128)] = jnp.where(low, r0, r1)
            return carry

        lax.fori_loop(0, HEADS // 2, pair, 0)
        done("rinv", "mixed")

        self.wait_weight(layer, "wout")
        before("xhat1", "rr", "firstb")

        def mask(b):
            place = lax.broadcasted_iota(jnp.int32, (BLOCK, 1), 0) + b * BLOCK
            return (place < self.valid).astype(F32)

        def norm_first(b, total):
            rows = rows_of(b, BLOCK)
            branch = mm(v.mixed[rows, :], v.wout[...]) + vec[2:3, :]
            u = v.h[rows, :].astype(F32) + branch
            c = u - jnp.mean(u, axis=1, keepdims=True)
            f = lax.rsqrt(jnp.mean(c * c, axis=1, keepdims=True) + EPSILON)
            x = c * f
            v.xhat1[rows, :] = x
            v.rr[0, rows, :] = jnp.broadcast_to(f, (BLOCK, 128))
            y = x * vec[3:4, :] + vec[5:6, :]
            v.first[rows, :] = y
            v.firstb[rows, :] = y.astype(BF16)
            return total + jnp.sum(mask(b) * branch * branch, axis=0, keepdims=True)

        zero = jnp.zeros((1, width), F32)
        blocks = self.length // BLOCK
        branch_sum = lax.fori_loop(0, blocks, norm_first, zero)
        done("xhat1", "firstb")
        if not again:
            self.start_weight(1, "wout", 1)

        before("act", "slope")
        v.feed[...] = jnp.broadcast_to(vec[11:12, :], v.feed.shape)

        def widen(j):
            at = lanes(j * TILE, TILE)
            hid = mm(v.firstb[...], v.wid[:, at]) + vec[pl.ds(12 + j, 1), 0:TILE]
            a, d = gelu_and_slope(hid)
            v.act[:, at] = a.astype(BF16)
            v.slope[:, at] = d.astype(BF16)

        def narrow(j):
            v.feed[...] += mm(v.act[:, lanes(j * TILE, TILE)], v.nar[rows_of(j, TILE), :])

        self.wait_piece(layer, "wid", 0)
        widen(0)

        def ffn(j, carry):
            @pl.when(lax.rem(j, width // TILE) == 0)
            def _():
                self.wait_piece(layer, "wid", j // (width // TILE))

            @pl.when(lax.rem(j, width // TILE) == 1)
            def _():
                self.wait_piece(layer, "nar", j // (width // TILE))

            narrow(j - 1)
            widen(j)
            return carry

        lax.fori_loop(1, self.ff // TILE, ffn, 0)
        done("act", "slope")
        narrow(self.ff // TILE - 1)
        if not again:
            self.start_weight(1, "wid", 1)
            self.start_weight(1, "nar", 1)
        before("xhat2")

        def norm_second(b, totals):
            rows = rows_of(b, BLOCK)
            fd = v.feed[rows, :]
            u = v.first[rows, :] + fd
            c = u - jnp.mean(u, axis=1, keepdims=True)
            f = lax.rsqrt(jnp.mean(c * c, axis=1, keepdims=True) + EPSILON)
            x = c * f
            v.xhat2[rows, :] = x
            v.rr[1, rows, :] = jnp.broadcast_to(f, (BLOCK, 128))
            y = x * vec[4:5, :] + vec[6:7, :]
            v.first[rows, :] = y
            if not again:
                v.h[rows, :] = y.astype(BF16)
            ok = mask(b)
            return (
                totals[0] + jnp.sum(ok * u * u, axis=0, keepdims=True),
                totals[1] + jnp.sum(ok * fd * fd, axis=0, keepdims=True),
            )

        stream_sum, feed_sum = lax.fori_loop(0, blocks, norm_second, (zero, zero))
        done("xhat2", "rr")
        for i in range(8):
            small[i : i + 1, :] = v.first[pl.ds(self.cls_at[i], 1), :]
        small[8:9, :] = stream_sum
        small[9:10, :] = branch_sum
        small[10:11, :] = feed_sum
        small[11:12, :] = jnp.full((1, width), self.valid.astype(F32))
        small[12:16, :] = jnp.zeros((4, width), F32)

    def wait_saved(self, restored, *names):
        if restored:
            for name in names:
                if name in WEIGHTS:
                    self.wait_weight(0, name)
                else:
                    self.restoring(name).wait()

    def restore(self, *names):
        for name in names:
            if name in WEIGHTS:
                self.start_weight(0, name, 2)
            else:
                self.restoring(name).start()

    def send_out(self, stage, shift, n, value, target):
        slot = lax.rem(n, 2)

        @pl.when(n >= 2)
        def _():
            pltpu.make_async_copy(stage.at[slot], target, self.sems.stage.at[shift + slot]).wait()

        stage[slot] = value.astype(BF16)
        pltpu.make_async_copy(stage.at[slot], target, self.sems.stage.at[shift + slot]).start()

    def put_rows(self, n, value, target):
        self.send_out(self.v.row_stage, 0, n, value, target)

    def put_cols(self, n, value, target):
        self.send_out(self.v.col_stage, 2, n, value, target)

    def drain_rows(self, grad):
        for slot in range(2):
            pltpu.make_async_copy(self.v.row_stage.at[slot], grad.at[0, 0:TILE, :], self.sems.stage.at[slot]).wait()

    def drain_cols(self, grad):
        for slot in range(2):
            pltpu.make_async_copy(
                self.v.col_stage.at[slot], grad.at[0, :, 0:TILE], self.sems.stage.at[2 + slot]
            ).wait()

    def norms(self, vec, source, x_ref, f_at, gain, target, target_b, where):
        v = self.v
        zero = jnp.zeros((1, self.width), F32)

        def body(b, total):
            rows = rows_of(b, BLOCK)
            up = source[rows, :].astype(F32)
            x = x_ref[rows, :]
            d = norm_back(up * vec[gain : gain + 1, :], x, v.rr[f_at, rows, 0:1])
            target[rows, :] = d
            db = d.astype(BF16)
            target_b[rows, :] = db
            return (
                total[0] + jnp.sum(up * x, axis=0, keepdims=True),
                total[1] + jnp.sum(up, axis=0, keepdims=True),
                total[2] + jnp.sum(db.astype(F32), axis=0, keepdims=True),
            )

        got = lax.fori_loop(0, self.length // BLOCK, body, (zero, zero, zero))
        for i in range(3):
            v.sums[where + i : where + i + 1, :] = got[i]

    def din_kept(self, source):
        return pltpu.make_async_copy(source, self.a.din_kept, self.sems.h.at[2])

    def din_sent(self, source):
        return pltpu.make_async_remote_copy(
            src_ref=source, dst_ref=self.a.din_got, send_sem=self.sems.din.at[0], recv_sem=self.sems.din.at[1],
            device_id=self.a.other, device_id_type=MESH,
        )

    def backward(self, layer, grad, small):
        v, width, restored = self.v, self.width, layer == 0
        vec = v.vec.at[layer]
        dh, dqkv, dbr, dres, ds = v.slope, v.qkv, v.g, v.feed, v.first

        def second():
            self.wait_saved(restored, "xhat2", "rr")
            self.norms(vec, v.g, v.xhat2, 1, 4, ds, v.dfeed, 0)
            self.wait_saved(restored, "nar", "act", "slope", "firstb")

        def ffn(low, i, carry):
            at = lanes(i * 2 * TILE, 2 * TILE)
            da = mm_right_t(v.dfeed[...], v.nar[at, :])
            d = (v.slope[:, at].astype(F32) * da).astype(BF16)
            dh[:, at] = d
            d_narrow = mm_left_t(v.act[:, at], v.dfeed[...])
            d_widen = mm_left_t(v.firstb[...], d)
            d_bias = jnp.sum(d.astype(F32), axis=0, keepdims=True)
            for half in range(2):
                j, part = 2 * i + half, slice(half * TILE, (half + 1) * TILE)
                place = lanes(lax.rem(j, 3) * TILE, TILE)
                v.wbias[pl.ds(j, 1), :] = d_bias[:, part]
                self.put_rows(j - low, d_narrow[part, :], grad.at[2 * (j // 3), place, :])
                self.put_cols(j - low, d_widen[:, part], grad.at[2 * (j // 3) + 1, :, place])
            return carry

        def tiles(low, high):
            lax.fori_loop(low // 2, high // 2, functools.partial(ffn, low), 0)

        def first_grad():
            self.wait_saved(restored, "wid")

            def body(j, carry):
                at = lanes(j * TILE, TILE)
                ds[:, at] = ds[:, at] + mm_right_t(dh[...], v.wid[at, :])
                return carry

            lax.fori_loop(0, width // TILE, body, 0)

        def first():
            self.wait_saved(restored, "xhat1")
            self.norms(vec, ds, v.xhat1, 0, 3, dres, dbr, 3)

        def out_grad():
            self.wait_saved(restored, "mixed", "wout", "rinv")

            def body(j, carry):
                at = lanes(j * TILE, TILE)
                self.put_cols(j, mm_left_t(v.mixed[...], dbr[:, at]), grad.at[OUT, :, at])
                d = mm_right_t(dbr[...], v.wout[at, :]).astype(BF16).astype(F32)
                v.dm[:, at] = (d * v.rinv[:, at]).astype(BF16)
                return carry

            lax.fori_loop(0, width // TILE, body, 0)

        def pair(p, carry):
            low = lax.broadcasted_iota(jnp.int32, (self.length, 128), 1) < HEAD_DIM
            slot = lax.rem(p, 2)

            @pl.when(p + 1 < HEADS // 2)
            def _():
                self.e_load(layer, p + 1, 1 - slot).start()

            at_q, at_k, at_v = lanes(p * 128, 128), lanes(width + p * 128, 128), lanes(2 * width + p * 128, 128)
            q, k, values = v.qkv[:, at_q], v.qkv[:, at_k], v.qkv[:, at_v]
            d = v.dm[:, at_q]
            prod = d.astype(F32) * v.mixed[:, at_q].astype(F32)
            self.e_load(layer, p, slot).wait()
            dq, dk, dv = [], [], []
            for i in range(2):
                mine = low if i == 0 else ~low
                delta = jnp.sum(jnp.where(mine, prod, 0.0), axis=1, keepdims=True)
                dp = mm_right_t(jnp.where(mine, d, BF16(0)), values)
                e = v.e[slot, i]
                s = (e.astype(F32) * (dp - delta)).astype(BF16)
                dq.append(mm(s, k))
                dk.append(mm_left_t(s, q))
                dv.append(mm_left_t(e, d))
            dqkv[:, at_q] = (jnp.where(low, dq[0], dq[1]) * HEAD_DIM**-0.5).astype(BF16)
            dqkv[:, at_k] = jnp.where(low, dk[0], dk[1]).astype(BF16)
            dqkv[:, at_v] = jnp.where(low, dv[0], dv[1]).astype(BF16)
            return carry

        def pairs(low, high):
            if low == 0:
                self.wait_saved(restored, "qkv")
            lax.fori_loop(low, high, pair, 0)

        def in_grad(low, high):
            if restored and low == 0:
                self.load_input(self.a.hidden).wait()

            def body(j, carry):
                at = lanes(j * TILE, TILE)
                place = lanes(lax.rem(j, 3) * TILE, TILE)
                self.put_cols(j - low, mm_left_t(v.h[...], dqkv[:, at]), grad.at[IN + j // 3, :, place])
                return carry

            lax.fori_loop(low, high, body, 0)

        def input_grad():
            self.wait_saved(restored, "win")

            def body(j, carry):
                at = lanes(j * TILE, TILE)
                d = dres[:, at] + mm_right_t(dqkv[...], v.win[at, :])
                dres[:, at] = d
                if layer == 1:
                    v.g[:, at] = d.astype(BF16)
                return carry

            lax.fori_loop(0, width // TILE, body, 0)
            pl.when(self.section == layer)(lambda: self.din_kept(dres).start())
            pl.when(self.section != layer)(lambda: self.din_sent(dres).start())
            small[16:17, :] = jnp.sum(dqkv[:, 0:width].astype(F32), axis=0, keepdims=True)
            small[17:18, :] = jnp.sum(dqkv[:, 2 * width :].astype(F32), axis=0, keepdims=True)
            for i, source in enumerate((5, 3, 0, 4, 1)):
                small[18 + i : 19 + i, :] = v.sums[source : source + 1, :]
            for i in range(self.ff // TILE):
                small[23 + i // 3 : 24 + i // 3, (i % 3) * TILE : (i % 3 + 1) * TILE] = v.wbias[i : i + 1, :]
            small[27:28, :] = v.sums[2:3, :]
            small[28:32, :] = jnp.zeros((4, width), F32)

        def input_done():
            pl.when(self.section == layer)(lambda: self.din_kept(dres).wait())
            pl.when(self.section != layer)(lambda: self.din_sent(dres).wait_send())

        def tiles_done():
            self.drain_rows(grad)
            self.drain_cols(grad)

        return Refs(
            second=second, tiles=tiles, first_grad=first_grad, first=first, out_grad=out_grad, pairs=pairs, in_grad=in_grad,
            input_grad=input_grad, input_done=input_done, tiles_done=tiles_done,
            cols_done=lambda: self.drain_cols(grad),
        )


def sum_plan(devices, rows):
    side = round((devices / 2) ** (1 / 3))
    extents = [side, side, devices // (side * side)]
    axes, stride = [], 1
    for extent in extents:
        steps, step = [], 1
        while step < extent:
            steps.append(stride * step)
            step *= 2
        axes.append(steps)
        stride *= extent
    x, y, z = axes
    distances = x + y + z
    swaps = lambda order, active=None: [("swap", distance, active) for distance in order]
    unit = 256 if devices <= 16 else 128
    run = 5 * unit // 2
    count, over = rows // run, rows % run
    return [
        (0, unit, count + (over >= unit), swaps(y + x + z)),
        (unit, unit, count + (over >= 2 * unit), swaps(x + y + z)),
        (2 * unit, unit // 2, count, swaps(z + x + y)),
    ], distances, None


class Stage:
    def __init__(self, kind, rows, cols, send, to, recv, source, sent, got):
        self.kind, self.rows, self.cols = kind, rows, cols
        self.send, self.to, self.recv, self.source, self.sent, self.got = send, to, recv, source, sent, got


def message_shapes(unit, width, spec):
    rows, cols, shapes = unit // 2, width, []
    for i, (kind, arg, _) in enumerate(spec):
        if kind == "chain":
            if arg == 0:
                rows //= 2
        elif kind != "fold":
            if rows >= 32:
                rows //= 2
            elif cols == width:
                cols //= 2
            else:
                kind = "full"
        shapes.append((kind, rows, cols))
    return shapes


def build_stages(unit, width, spec, me, line):
    rows, cols = unit // 2, width
    row = col = me * 0
    if line is not None:
        stride, depth = line
        z = me // stride
    flag = lambda condition: condition.astype(jnp.int32)
    stages = []
    for kind, arg, active in spec:
        if kind == "fold":
            first, third = flag(z == arg), flag(z == arg + 1)
            send, recv = (z == arg) | (z == depth - 1 - arg), (z == arg + 1) | (z == depth - 2 - arg)
            place = (row, col)
            stages.append(Stage(
                kind, rows, cols, send, me + stride * (2 * first - 1), recv, me + stride * (1 - 2 * third), place, place
            ))
        elif kind == "chain":
            if arg == 0:
                rows //= 2
                base = row
            up, came = flag(z == arg), flag(z == arg + 1)
            send, recv = (z == arg) | (z == depth - 1 - arg), (z == arg + 1) | (z == depth - 2 - arg)
            stages.append(Stage(
                kind, rows, cols, send, me + stride * (2 * up - 1), recv, me + stride * (1 - 2 * came),
                (base + up * rows, col), (base + came * rows, col),
            ))
            if arg == depth - 2:
                row = base + flag(z == depth - 1) * rows
        else:
            if kind == "middle":
                bit, distance = flag(z >= depth // 2), stride
                active = "middle"
            else:
                bit, distance = lax.rem(me // arg, 2), arg
            if active == "middle":
                on = (z == depth // 2 - 1) | (z == depth // 2)
            elif active == "ends":
                on = (z == 0) | (z == depth - 1)
            else:
                on = None
            partner = me + distance * (1 - 2 * bit)
            sent = (row, col)
            kind = "swap"
            if rows >= 32:
                rows //= 2
                sent, row = (row + (1 - bit) * rows, col), row + bit * rows
            elif cols == width:
                cols //= 2
                sent, col = (row, col + (1 - bit) * cols), col + bit * cols
            else:
                kind = "full"
            stages.append(Stage(kind, rows, cols, on, partner, on, partner, sent, (row, col)))
    return stages


def when(condition, action):
    if condition is None:
        action()
    else:
        pl.when(condition)(action)


class GradientSum:
    def __init__(self, plan, distances, line, width, grads, out, buffers, sems):
        self.plan, self.distances, self.line, self.width, self.grads, self.out = plan, distances, line, width, grads, out
        self.run = sum(unit for _, unit, _, _ in plan)
        self.section, self.me = lax.axis_index("section"), lax.axis_index("dp")
        self.peer = (1 - self.section, self.me)
        self.parts = [build_stages(unit, width, spec, self.me, line) for _, unit, _, spec in plan]
        self.slots = [slots_of(spec) for _, _, _, spec in plan]
        self.total, self.other, self.recvs, self.fulls = buffers
        self.keep_sems, self.pair_sems, self.trade_sems, self.end_sems, self.send_sems, self.rs_sems, self.ag_sems = sems[:7]
        self.free, self.full_free = sems[7:]
        self.length = max(2 * count + 2 * len(spec) + 2 for _, _, count, spec in plan)

    def partner(self, distance):
        return (self.section, self.me + distance * (1 - 2 * lax.rem(self.me // distance, 2)))

    def barrier(self):
        barrier = pltpu.get_barrier_semaphore()
        for device in [self.peer] + [self.partner(distance) for distance in self.distances]:
            pl.semaphore_signal(barrier, inc=1, device_id=device, device_id_type=MESH)
        neighbours = []
        if self.line is not None:
            stride, depth = self.line
            z = self.me // stride
            neighbours = [(z > 0, -stride), (z < depth - 1, stride)]
        for there, distance in neighbours:

            @pl.when(there)
            def _(distance=distance):
                pl.semaphore_signal(
                    barrier, inc=1, device_id=(self.section, self.me + distance), device_id_type=MESH
                )

        pl.semaphore_wait(barrier, len(self.distances) + 1)
        for there, _ in neighbours:
            pl.when(there)(lambda: pl.semaphore_wait(barrier, 1))

    def slot(self, part, k):
        return lax.rem(k, self.slots[part])

    def stage_slot(self, part, k, s):
        return lax.rem(k, stage_slots_of(self.plan[part][3], s))

    def half_rows(self, ref, part, k, which):
        base, unit, count, _ = self.plan[part]
        row = base + lax.rem(k, count) * self.run + which * (unit // 2)
        return ref.at[row // self.width, pl.ds(pl.multiple_of(lax.rem(row, self.width), 16), unit // 2)]

    def load(self, part, k, source):
        slot = self.slot(part, k)
        return pltpu.make_async_copy(
            self.half_rows(source, part, k, self.section), self.total[part].at[slot], self.keep_sems[part].at[slot]
        )

    def trade(self, part, k, source):
        slot = self.slot(part, k)
        return pltpu.make_async_remote_copy(
            src_ref=self.half_rows(source, part, k, 1 - self.section), dst_ref=self.other[part].at[slot],
            send_sem=self.pair_sems[part].at[slot], recv_sem=self.trade_sems[part].at[slot],
            device_id=self.peer, device_id_type=MESH,
        )

    def keep(self, part, k):
        slot = self.slot(part, k)
        return pltpu.make_async_copy(
            self.other[part].at[slot], self.half_rows(self.out, part, k, self.section), self.keep_sems[part].at[slot]
        )

    def hand_over(self, part, k):
        slot = self.slot(part, k)
        return pltpu.make_async_remote_copy(
            src_ref=self.other[part].at[slot], dst_ref=self.half_rows(self.out, part, k, self.section),
            send_sem=self.pair_sems[part].at[slot], recv_sem=self.end_sems[part].at[slot],
            device_id=self.peer, device_id_type=MESH,
        )

    def view(self, ref, slot, stage, place):
        row, col = place
        at = pl.ds(pl.multiple_of(row, 16), stage.rows)
        if stage.cols == self.width:
            return ref.at[slot, at]
        return ref.at[slot, at, pl.ds(pl.multiple_of(col, 128), stage.cols)]

    def held(self, part, k, s, place):
        stages = self.parts[part]
        fulls = [i for i in range(s + 1) if stages[i].kind == "full"]
        if fulls:
            return self.fulls[part][fulls[-1]].at[self.slot(part, k)]
        return self.view(self.total[part], self.slot(part, k), stages[s], place)

    def reduce_copy(self, part, k, s, device):
        stage = self.parts[part][s]
        at = self.stage_slot(part, k, s)
        if stage.kind == "full":
            source = self.held(part, k, s - 1, self.parts[part][s - 1].got)
        else:
            source = self.view(self.total[part], self.slot(part, k), stage, stage.sent)
        return pltpu.make_async_remote_copy(
            src_ref=source, dst_ref=self.recvs[part][s].at[at],
            send_sem=self.send_sems[part][s].at[self.slot(part, k)], recv_sem=self.rs_sems[part][s].at[at],
            device_id=(self.section, device), device_id_type=MESH,
        )

    def gather_copy(self, part, k, s, device, place):
        stage = self.parts[part][s]
        ref = self.view(self.other[part], self.slot(part, k), stage, place)
        return pltpu.make_async_remote_copy(
            src_ref=ref, dst_ref=ref, send_sem=self.send_sems[part][s].at[self.slot(part, k)],
            recv_sem=self.ag_sems[part][s].at[self.stage_slot(part, k, s)],
            device_id=(self.section, device), device_id_type=MESH,
        )

    def start_reduce(self, part, k, s):
        stage = self.parts[part][s]

        def action():
            if stage.kind == "full":

                @pl.when(k >= stage_slots_of(self.plan[part][3], s))
                def _():
                    pl.semaphore_wait(self.full_free[part][s].at[0], 1)

            self.reduce_copy(part, k, s, stage.to).start()

        when(stage.send, action)

    def end_reduce(self, part, k, s):
        stage = self.parts[part][s]
        slot, at = self.slot(part, k), self.stage_slot(part, k, s)
        last = len(self.parts[part]) - 1

        def action():
            self.reduce_copy(part, k, s, stage.source).wait_recv()
            if stage.kind == "full":
                left = self.held(part, k, s - 1, self.parts[part][s - 1].got)
            else:
                left = self.view(self.total[part], slot, stage, stage.got)
            target = self.view(self.other[part], slot, stage, stage.got) if s == last else self.held(part, k, s, stage.got)
            self.add(target, left, self.recvs[part][s].at[at], stage.rows)
            if stage.kind == "full":

                @pl.when(k + stage_slots_of(self.plan[part][3], s) < 2 * self.plan[part][2])
                def _():
                    pl.semaphore_signal(
                        self.full_free[part][s].at[0], inc=1, device_id=(self.section, stage.source),
                        device_id_type=MESH,
                    )

        when(stage.recv, action)

    def start_gather(self, part, k, s):
        stage = self.parts[part][s]
        if stage.kind == "full":
            return
        when(stage.send, lambda: self.reduce_copy(part, k, s, stage.to).wait_send())
        when(stage.recv, lambda: self.gather_copy(part, k, s, stage.source, stage.got).start())

    def end_gather(self, part, k, s):
        stage = self.parts[part][s]
        if stage.kind != "full":
            when(stage.send, lambda: self.gather_copy(part, k, s, stage.to, stage.sent).wait_recv())

    def owned(self, part, k):
        return (k < self.plan[part][2]) == (self.section == 1)

    def add(self, target, left, right, rows):
        block = min(rows, 32)

        def body(i, carry):
            at = pl.ds(pl.multiple_of(i * block, 16), block)
            target[at, :] = left[at, :] + right[at, :]
            return carry

        lax.fori_loop(0, rows // block, body, 0)

    def retire(self, part, k):
        for s, stage in enumerate(self.parts[part]):
            if stage.kind == "full":
                when(stage.send, lambda s=s, stage=stage: self.reduce_copy(part, k, s, stage.to).wait_send())
            else:
                when(stage.recv, lambda s=s, stage=stage: self.gather_copy(part, k, s, stage.source, stage.got).wait_send())
        mine = self.owned(part, k)
        pl.when(mine)(lambda: self.keep(part, k).wait())
        pl.when(jnp.logical_not(mine))(lambda: self.hand_over(part, k).wait_send())

    def task(self, part, k, s):
        last = len(self.parts[part]) - 1
        slots, count = self.slots[part], self.plan[part][2]
        if s == 0:

            @pl.when(k >= slots)
            def _():
                self.retire(part, k - slots)
                pl.semaphore_signal(self.free.at[part], inc=1, device_id=self.peer, device_id_type=MESH)
                pl.semaphore_wait(self.free.at[part], 1)

            first = k < count

            @pl.when(first)
            def _():
                self.load(part, k, self.grads[1]).start()
                self.trade(part, k, self.grads[1]).start()

            @pl.when(jnp.logical_not(first))
            def _():
                self.load(part, k, self.grads[0]).start()
                self.trade(part, k, self.grads[0]).start()

        elif s == 1:
            self.load(part, k, self.grads[0]).wait()
            self.trade(part, k, self.grads[0]).wait_recv()
            total = self.total[part].at[self.slot(part, k)]
            self.add(total, total, self.other[part].at[self.slot(part, k)], self.plan[part][1] // 2)
            self.start_reduce(part, k, 0)
        elif s <= last + 2:
            self.end_reduce(part, k, s - 2)
            if s - 1 <= last:
                self.start_reduce(part, k, s - 1)
            else:
                self.start_gather(part, k, last)
        elif s <= 2 * last + 3:
            j = 2 * last + 3 - s
            self.end_gather(part, k, j)
            if j > 0:
                self.start_gather(part, k, j - 1)
            else:
                self.trade(part, k, self.grads[0]).wait_send()
                mine = self.owned(part, k)
                pl.when(mine)(lambda: self.keep(part, k).start())
                pl.when(jnp.logical_not(mine))(lambda: self.hand_over(part, k).start())
        else:
            pl.when(self.owned(part, k))(lambda: self.hand_over(part, k).wait_recv())

    def step(self, t):
        most = max(len(stages) for stages in self.parts)
        for s in range(2 * most + 3):
            for part, (_, _, count, spec) in enumerate(self.plan):
                if s < 2 * len(spec) + 3:
                    k = t - s
                    pl.when((k >= 0) & (k < 2 * count))(lambda part=part, s=s, k=k: self.task(part, k, s))

    def finish(self):
        for part, (_, _, count, _) in enumerate(self.plan):

            def body(k, carry, part=part):
                self.retire(part, k)
                return carry

            lax.fori_loop(max(2 * count - self.slots[part], 0), 2 * count, body, 0)


def slots_of(spec):
    return 2 * len(spec) + 3


def stage_slots_of(spec, s):
    return 2 * (len(spec) - s) + 1


def sum_scratch(plan, width):
    shapes, names = [], []

    def need(name, part, s, shape):
        names.append((name, part, s))
        shapes.append(shape)

    for part, (_, unit, _, spec) in enumerate(plan):
        slots = slots_of(spec)
        steps = message_shapes(unit, width, spec)
        for name in ("total", "other"):
            need(name, part, 0, pltpu.VMEM((slots, unit // 2, width), BF16))
        for name in ("keep", "pair", "trade", "end"):
            need(name, part, 0, pltpu.SemaphoreType.DMA((slots,)))
        for s, (kind, rows, cols) in enumerate(steps):
            at = stage_slots_of(spec, s)
            need("recv", part, s, pltpu.VMEM((at, rows, cols), BF16))
            need("send", part, s, pltpu.SemaphoreType.DMA((slots,)))
            need("rs", part, s, pltpu.SemaphoreType.DMA((at,)))
            if kind == "full":
                need("full_free", part, s, pltpu.SemaphoreType.REGULAR((1,)))
                if s < len(steps) - 1:
                    need("full", part, s, pltpu.VMEM((slots, rows, cols), BF16))
            else:
                need("ag", part, s, pltpu.SemaphoreType.DMA((at,)))
    need("free", 0, 0, pltpu.SemaphoreType.REGULAR((len(plan),)))

    def split(refs):
        by_name = {}
        for (name, part, s), ref in zip(names, refs):
            by_name.setdefault(name, {}).setdefault(part, {})[s] = ref
        one = lambda name: [by_name[name][part][0] for part in range(len(plan))]
        many = lambda name: [by_name.get(name, {}).get(part, {}) for part in range(len(plan))]
        buffers = (one("total"), one("other"), many("recv"), many("full"))
        sems = (
            one("keep"), one("pair"), one("trade"), one("end"), many("send"), many("rs"), many("ag"),
            by_name["free"][0][0], many("full_free"),
        )
        return buffers, sems

    return shapes, split


def layers_kernel(plan, distances, line, split, *refs):
    refs = list(refs)
    take = lambda n: [refs.pop(0) for _ in range(n)]
    valid_ref, cls_ref, seg_ref, proj_bias, out_shift, gains, shifts, widen_bias, narrow_bias = take(9)
    hidden, cotangent = take(2)
    own = take(4)
    out, din_kept, din_got, small_got, small_sum, small_mine = take(6)
    grad0, grad1, e_hbm = take(3)
    saved = take(9)
    v = Refs(**dict(zip(VMEM_NAMES, take(len(VMEM_NAMES)))))
    small_send, small_acc, small_recv = take(3)
    weight_sems, sent_sems, arrived_sems, free_sems, saved_sems, e_sems, h_sems, stage_sems, vec_sems, small_sems = take(10)
    din_sems, = take(1)
    section = lax.axis_index("section")
    width = v.h.shape[1]
    total = GradientSum(plan, distances, line, width, (grad0, grad1), out, *split(refs))
    compute = Compute(
        v,
        Refs(own=own, other=total.peer, saved=saved, e=e_hbm, hidden=hidden, din_kept=din_kept, din_got=din_got),
        Refs(
            weights=weight_sems, sent=sent_sems, arrived=arrived_sems, free=free_sems, saved=saved_sems, e=e_sems, h=h_sems,
            stage=stage_sems, din=din_sems,
        ),
        section, valid_ref[section], [cls_ref[section, i] for i in range(8)],
    )

    def vec_sent():
        return pltpu.make_async_remote_copy(
            src_ref=v.vec_own, dst_ref=v.vec_peer, send_sem=vec_sems.at[0], recv_sem=vec_sems.at[1],
            device_id=total.peer, device_id_type=MESH,
        )

    compute.load_input(hidden).start()
    v.vec_own[0:2, :] = proj_bias[0]
    v.vec_own[2:3, :] = out_shift[...]
    v.vec_own[3:5, :] = gains[0]
    v.vec_own[5:7, :] = shifts[0]
    v.vec_own[7:11, :] = jnp.zeros((4, width), F32)
    v.vec_own[11:12, :] = narrow_bias[...]
    v.vec_own[12:24, :] = jnp.zeros((12, width), F32)
    for i in range(widen_bias.shape[1] // TILE):
        v.vec_own[12 + i : 13 + i, 0:TILE] = widen_bias[:, i * TILE : (i + 1) * TILE]
    total.barrier()
    vec_sent().start()
    compute.start_weight(0, "win", 0)
    compute.start_weight(0, "wout", 0)
    for q in range(compute.pieces("wid")):
        compute.start_weight(0, "wid", 0, q)
        compute.start_weight(0, "nar", 0, q)
    segments = seg_ref[pl.ds(section, 1), :]
    columns = jnp.broadcast_to(segments.astype(F32), (128, compute.length)).T[:, :1]
    v.bias[...] = jnp.where(columns == segments.astype(F32), 0.0, MASKED)
    compute.load_cotangent(cotangent).start()
    vec_sent().wait_recv()
    for layer in range(2):
        v.vec[layer] = jnp.where(section == layer, v.vec_own[...], v.vec_peer[...])
    compute.load_input(hidden).wait()

    small0, small1 = v.small.at[0], v.small.at[1]
    compute.forward(0, small0)
    compute.forward(1, small1)
    compute.e_drain(1)
    compute.e_load(1, 0, 0).start()
    compute.load_cotangent(cotangent).wait()

    rounds = len(distances)

    def small_trade():
        return pltpu.make_async_remote_copy(
            src_ref=small_send, dst_ref=small_got, send_sem=small_sems.at[0, rounds], recv_sem=small_sems.at[1, rounds],
            device_id=total.peer, device_id_type=MESH,
        )

    def small_copy(i):
        return pltpu.make_async_remote_copy(
            src_ref=small_acc.at[i], dst_ref=small_recv.at[i], send_sem=small_sems.at[0, i],
            recv_sem=small_sems.at[1, i], device_id=total.partner(distances[i]), device_id_type=MESH,
        )

    def small_start():
        small_mine[...] = jnp.where(section == 0, small0[...], small1[...])
        small_send[...] = jnp.where(section == 0, small1[...], small0[...])
        small_trade().start()

    def small_step(stage):
        if stage == 0:
            small_trade().wait_recv()
            small_acc[0] = small_mine[8:, :] + small_got[8:, :]
        else:
            small_copy(stage - 1).wait_recv()
            small_acc[stage] = small_acc[stage - 1] + small_recv[stage - 1]
        if stage < rounds:
            small_copy(stage).start()
        else:
            small_sum[...] = small_acc[stage]

    one = compute.backward(1, grad1, small1)
    zero = compute.backward(0, grad0, small0)
    restore = compute.restore
    one.second()
    one.tiles(0, 4)
    one.tiles_done()
    do = functools.partial
    events = [
        [do(one.tiles, 4, 6)],
        [one.tiles_done, do(one.tiles, 6, 8)],
        [one.tiles_done, do(one.tiles, 8, 10)],
        [one.tiles_done, do(one.tiles, 10, 12), do(restore, "nar", "act", "firstb", "xhat2")],
        [one.tiles_done, one.first_grad, do(restore, "slope", "wid")],
        [one.first, do(restore, "xhat1", "rr"), one.out_grad, do(restore, "wout", "rinv")],
        [one.cols_done, do(one.pairs, 0, 2)],
        [do(one.pairs, 2, 4)],
        [do(one.pairs, 4, 6), do(restore, "mixed"), lambda: compute.e_load(0, 0, 0).start()],
        [do(one.in_grad, 0, 5), one.cols_done],
        [do(one.in_grad, 5, 9), lambda: compute.load_input(hidden).start()],
        [one.cols_done, one.input_grad, do(restore, "qkv", "win"), zero.second],
        [one.input_done, do(zero.tiles, 0, 4)],
        [zero.tiles_done, do(zero.tiles, 4, 6)],
        [zero.tiles_done, do(zero.tiles, 6, 10)],
        [zero.tiles_done, do(zero.tiles, 10, 12)],
        [zero.tiles_done, zero.first_grad],
        [zero.first, zero.out_grad],
        [zero.cols_done, do(zero.pairs, 0, 2)],
        [do(zero.pairs, 2, 4)],
        [do(zero.pairs, 4, 6)],
        [do(zero.in_grad, 0, 5)],
        [zero.cols_done, do(zero.in_grad, 5, 9)],
        [zero.cols_done, zero.input_grad, small_start],
    ] + [[do(small_step, s)] for s in range(rounds + 1)]

    def body(t, carry):
        total.step(t)
        for i, event in enumerate(events):

            @pl.when(t == i)
            def _(event=event):
                for action in event:
                    action()

        return carry

    lax.fori_loop(0, total.length, body, 0)
    total.finish()
    zero.input_done()
    vec_sent().wait_send()
    for name in WEIGHTS:
        for q in range(compute.pieces(name)):
            compute.weight_sent(name, q).wait_send()
    small_trade().wait_send()
    for i in range(rounds):
        small_copy(i).wait_send()
    compute.din_sent(v.feed).wait_recv()


VMEM_NAMES = (
    "h", "g", "win", "wout", "wid", "nar", "qkv", "e", "rinv", "mixed", "xhat1", "rr", "first", "firstb", "act", "slope",
    "xhat2", "feed", "bias", "dfeed", "dm", "row_stage", "col_stage", "wbias", "sums", "vec", "vec_own", "vec_peer", "small",
)


def layers(valid_counts, cls_positions, segment_ids, vectors, hidden, cotangent, own):
    rows, length = segment_ids.shape
    width, ff = hidden.shape[1], own[2].shape[2]
    devices = lax.axis_size("dp")
    plan, distances, line = sum_plan(devices, 12 * width)
    stages = len(distances)
    shapes, split = sum_scratch(plan, width)
    row_b, row_f = ((length, width), BF16), ((length, width), F32)
    saved = [
        ((length, 3 * width), BF16), row_f, row_b, row_f, ((2, length, 128), F32), row_b, ((length, ff), BF16),
        ((length, ff), BF16), row_f,
    ]
    grad = ((12, width, width), BF16)
    small = ((32, width), F32)
    sums = (24, width)
    outs = [grad, row_f, row_f, small, (sums, F32), small, grad, grad, ((2, HEADS, length, length), BF16), *saved]
    scratch = dict(
        h=row_b, g=row_b, win=(own[0].shape[1:], BF16), wout=(own[1].shape[1:], BF16), wid=(own[2].shape[1:], BF16),
        nar=(own[3].shape[1:], BF16), qkv=saved[0], e=((2, 2, length, length), BF16), rinv=row_f, mixed=row_b, xhat1=row_f,
        rr=saved[4], first=row_f, firstb=row_b, act=saved[6], slope=saved[7], xhat2=row_f, feed=row_f,
        bias=((length, length), F32), dfeed=row_b, dm=row_b, row_stage=((2, TILE, width), BF16),
        col_stage=((2, width, TILE), BF16), wbias=((16, TILE), F32), sums=((8, width), F32), vec=((2, 24, width), F32),
        vec_own=((24, width), F32), vec_peer=((24, width), F32), small=((2, 32, width), F32),
    )
    in_vmem = (3, 4, 5)
    got = pl.pallas_call(
        functools.partial(layers_kernel, plan, distances, line, split),
        out_shape=[jax.ShapeDtypeStruct(s, d) for s, d in outs],
        in_specs=[SMEM, SMEM] + [VMEM] * 7 + [ANY] * 6,
        out_specs=[VMEM if i in in_vmem else ANY for i in range(len(outs))],
        scratch_shapes=[
            *[pltpu.VMEM(*scratch[name]) for name in VMEM_NAMES],
            pltpu.VMEM(*small),
            pltpu.VMEM((stages + 1, *sums), F32),
            pltpu.VMEM((stages, *sums), F32),
            pltpu.SemaphoreType.DMA((10,)),
            pltpu.SemaphoreType.DMA((10,)),
            pltpu.SemaphoreType.DMA((10,)),
            pltpu.SemaphoreType.REGULAR((4,)),
            pltpu.SemaphoreType.DMA((9,)),
            pltpu.SemaphoreType.DMA((2,)),
            pltpu.SemaphoreType.DMA((3,)),
            pltpu.SemaphoreType.DMA((4,)),
            pltpu.SemaphoreType.DMA((2,)),
            pltpu.SemaphoreType.DMA((2, stages + 1)),
            pltpu.SemaphoreType.DMA((2,)),
            *shapes,
        ],
        compiler_params=pltpu.CompilerParams(collective_id=0, has_side_effects=True, vmem_limit_bytes=63 * MIB),
        cost_estimate=pl.CostEstimate(flops=54 * 10**9, bytes_accessed=200 * 10**6, transcendentals=10**7),
        name="layers_and_sum",
    )(valid_counts, cls_positions, segment_ids, *vectors, hidden, cotangent, *own)
    return got[:6]


def finish_kernel(
    flags, blocks, din_kept, din_got, small_mine, small_got, small_sum,
    cls_o, input_o, in_o, bias_o, out_o, out_shift_o, gain_o, shift_o, widen_o, widen_bias_o, narrow_o, narrow_bias_o, rms_o,
    dins, halves, wide, block_sems, din_sems, wide_sems,
):
    section = flags[0]
    got_row = 1 - section
    length, width = din_got.shape
    slots = wide.shape[0]

    def rows(row):
        return input_o.at[0, pl.ds(pl.multiple_of(row * length, 16), length)]

    def target(index):
        part = slice(index // 2 * width, (index // 2 + 1) * width)
        if index >= IN:
            return in_o.at[0, :, (index - IN) * width : (index - IN + 1) * width]
        if index == OUT:
            return out_o.at[0]
        return narrow_o.at[0, part, :] if index % 2 == 0 else widen_o.at[0, :, part]

    loads = [pltpu.make_async_copy(blocks.at[i], halves.at[i], block_sems.at[i]) for i in range(12)]
    stores = [pltpu.make_async_copy(wide.at[i % slots], target(i), wide_sems.at[i % slots]) for i in range(12)]
    din_loads = [pltpu.make_async_copy(din, dins.at[i], din_sems.at[i]) for i, din in enumerate((din_kept, din_got))]
    din_stores = [
        pltpu.make_async_copy(dins.at[i], rows(row), din_sems.at[i]) for i, row in enumerate((section, got_row))
    ]
    for copy in loads[:2] + din_loads + loads[2:]:
        copy.start()
    cls_o[0, section] = small_mine[0:8, :]
    cls_o[0, got_row] = small_got[0:8, :]
    bias_o[0] = small_sum[8:10, :]
    out_shift_o[...] = small_sum[10:11, :]
    gain_o[0] = small_sum[11:13, :]
    shift_o[0] = small_sum[13:15, :]
    for i in range(4):
        widen_bias_o[0:1, i * width : (i + 1) * width] = small_sum[15 + i : 16 + i, :]
    narrow_bias_o[...] = small_sum[19:20, :]
    for i in range(3):
        squares = jnp.sum(small_sum[i : i + 1, :], axis=1, keepdims=True)
        rms_o[0:1, i : i + 1] = jnp.sqrt(squares / (small_sum[3:4, 0:1] * width))

    for i in range(12):
        loads[i].wait()
        if i >= slots:
            stores[i - slots].wait()

        def widen_rows(b, carry, i=i):
            at = rows_of(b, 64)
            wide[i % slots, at, :] = halves[i, at, :].astype(F32)
            return carry

        lax.fori_loop(0, width // 64, widen_rows, 0)
        stores[i].start()
        if i == 1:
            for load, store in zip(din_loads, din_stores):
                load.wait()
                store.start()
    for copy in stores[12 - slots :] + din_stores:
        copy.wait()


def finish(section, blocks, din_kept, din_got, small_mine, small_got, small_sum):
    length, width = din_got.shape
    shapes = [
        (1, 2, 8, width), (1, 2 * length, width), (1, width, 3 * width), (1, 2, width), (1, width, width), (1, width),
        (1, 2, width), (1, 2, width), (1, width, 4 * width), (1, 4 * width), (1, 4 * width, width), (1, width), (1, 3),
    ]
    big = (1, 2, 4, 8, 10)
    return pl.pallas_call(
        finish_kernel,
        out_shape=[jax.ShapeDtypeStruct(s, F32) for s in shapes],
        in_specs=[SMEM] + [ANY] * 3 + [VMEM] * 3,
        out_specs=[ANY if i in big else VMEM for i in range(len(shapes))],
        scratch_shapes=[
            pltpu.VMEM((2, length, width), F32),
            pltpu.VMEM(blocks.shape, BF16),
            pltpu.VMEM((6, width, width), F32),
            pltpu.SemaphoreType.DMA((12,)),
            pltpu.SemaphoreType.DMA((2,)),
            pltpu.SemaphoreType.DMA((6,)),
        ],
        compiler_params=pltpu.CompilerParams(vmem_limit_bytes=63 * MIB),
        cost_estimate=pl.CostEstimate(flops=10**7, bytes_accessed=46 * 10**6, transcendentals=0),
        name="finish",
    )(section[None], blocks, din_kept, din_got, small_mine, small_got, small_sum)


def local(
    hidden_in, segment_ids, cls_positions, valid_counts, proj_in, proj_bias, proj_out, out_shift, norm_gains,
    norm_shifts, widen, widen_bias, narrow, narrow_bias, cotangent,
):
    section = lax.axis_index("section")
    vectors = (proj_bias, out_shift, norm_gains, norm_shifts, widen_bias, narrow_bias)
    blocks, din_kept, din_got, small_got, small_sum, small_mine = layers(
        valid_counts, cls_positions, segment_ids, vectors, hidden_in, cotangent, (proj_in, proj_out, widen, narrow)
    )
    return finish(section, blocks, din_kept, din_got, small_mine, small_got, small_sum)


def solution(mesh):
    placed = (
        P("dp", None),
        P("dp", None),
        P("dp", None),
        P("dp"),
        P("section", None, None),
        P("section", None, None),
        P("section", None, None),
        P("section", None),
        P("section", None, None),
        P("section", None, None),
        P("section", None, None),
        P("section", None),
        P("section", None, None),
        P("section", None),
        P("dp", None),
    )
    return jax.shard_map(
        local,
        mesh=mesh,
        in_specs=placed,
        out_specs=(
            P("section", "dp", None, None),
            P("section", "dp", None),
            P("section", None, None),
            P("section", None, None),
            P("section", None, None),
            P("section", None),
            P("section", None, None),
            P("section", None, None),
            P("section", None, None),
            P("section", None),
            P("section", None, None),
            P("section", None),
            P("section", None),
        ),
        check_vma=False,
    )
```

```python
import functools

import jax
import jax.numpy as jnp
from jax import lax
from jax.experimental import pallas as pl
from jax.experimental.pallas import tpu as pltpu
from jax.sharding import PartitionSpec as P

HEADS = 12
HEAD_DIM = 64
EPSILON = 1e-12
MASKED = -1e30
F32 = jnp.float32
BF16 = jnp.bfloat16
MIB = 2**20
TILE = 256
BLOCK = 128
ANY = pl.BlockSpec(memory_space=pl.ANY)
VMEM = pl.BlockSpec(memory_space=pltpu.VMEM)
SMEM = pl.BlockSpec(memory_space=pltpu.SMEM)
MESH = pl.DeviceIdType.MESH
OUT, IN = 8, 9


def mm(left, right):
    return jnp.dot(left, right, preferred_element_type=F32)


def mm_left_t(left, right):
    return lax.dot_general(left, right, (((0,), (0,)), ((), ())), preferred_element_type=F32)


def mm_right_t(left, right):
    return lax.dot_general(left, right, (((1,), (1,)), ((), ())), preferred_element_type=F32)


def lanes(start, size):
    return pl.ds(pl.multiple_of(start, size), size)


def rows_of(b, size):
    return pl.ds(pl.multiple_of(b * size, size), size)


def gelu_and_slope(v):
    z = jnp.abs(v) * 0.7071067811865476
    t = 1.0 / (1.0 + 0.3275911 * z)
    e = jnp.exp(-0.5 * v * v)
    poly = t * (
        0.127414796 + t * (-0.142248368 + t * (0.7107068705 + t * (-0.7265760135 + t * 0.5307027145)))
    )
    tail = poly * e
    cdf = jnp.where(v >= 0, 1.0 - tail, tail)
    return v * cdf, cdf + v * e * 0.3989422804014327


def norm_back(up, x, f):
    return f * (up - jnp.mean(up, axis=1, keepdims=True) - x * jnp.mean(up * x, axis=1, keepdims=True))


class Refs:
    def __init__(self, **refs):
        self.__dict__.update(refs)


SAVED = ("qkv", "rinv", "mixed", "xhat1", "rr", "firstb", "act", "slope", "xhat2")
WEIGHTS = ("win", "wout", "wid", "nar")


class Compute:
    def __init__(self, v, a, sems, section, valid, cls_at):
        self.v, self.a, self.sems = v, a, sems
        self.section, self.valid, self.cls_at = section, valid, cls_at
        self.length, self.width = v.h.shape
        self.ff = v.wid.shape[1]

    def piece(self, name, q):
        i = WEIGHTS.index(name)
        source, target = self.a.own[i].at[0], getattr(self.v, name)
        if name == "wid":
            at = lanes(q * self.width, self.width)
            return source.at[:, at], target.at[:, at], 2 + q
        if name == "nar":
            at = rows_of(q, self.width)
            return source.at[at, :], target.at[at, :], 6 + q
        return source, target, i

    def pieces(self, name):
        return self.ff // self.width if name in ("wid", "nar") else 1

    def weight_copy(self, name, q):
        source, target, i = self.piece(name, q)
        return pltpu.make_async_copy(source, target, self.sems.weights.at[i])

    def weight_sent(self, name, q):
        source, target, i = self.piece(name, q)
        return pltpu.make_async_remote_copy(
            src_ref=source, dst_ref=target, send_sem=self.sems.sent.at[i], recv_sem=self.sems.arrived.at[i],
            device_id=self.a.other, device_id_type=MESH,
        )

    def start_weight(self, layer, name, use, q=None):
        i = WEIGHTS.index(name)

        @pl.when(self.section == layer)
        def _():
            some = range(self.pieces(name)) if q is None else (q,)
            for p in some:
                self.weight_copy(name, p).start()
            if use > 0:
                pl.semaphore_wait(self.sems.free.at[i], 1)
            for p in some:
                if use == 2:
                    self.weight_sent(name, p).wait_send()
                self.weight_sent(name, p).start()

        if use > 0:

            @pl.when(self.section != layer)
            def _():
                pl.semaphore_signal(self.sems.free.at[i], inc=1, device_id=self.a.other, device_id_type=MESH)

    def wait_piece(self, layer, name, q):
        pl.when(self.section == layer)(lambda: self.weight_copy(name, q).wait())
        pl.when(self.section != layer)(lambda: self.weight_sent(name, q).wait_recv())

    def wait_weight(self, layer, name):
        for q in range(self.pieces(name)):
            self.wait_piece(layer, name, q)

    def saving(self, name):
        i = SAVED.index(name)
        return pltpu.make_async_copy(getattr(self.v, name), self.a.saved[i], self.sems.saved.at[i])

    def restoring(self, name):
        i = SAVED.index(name)
        return pltpu.make_async_copy(self.a.saved[i], getattr(self.v, name), self.sems.saved.at[i])

    def load_input(self, layer_input):
        return pltpu.make_async_copy(layer_input.at[self.rows()], self.v.h, self.sems.h.at[0])

    def load_cotangent(self, cotangent):
        return pltpu.make_async_copy(cotangent.at[self.rows()], self.v.g, self.sems.h.at[1])

    def rows(self):
        return pl.ds(pl.multiple_of(self.section * self.length, self.length), self.length)

    def e_store(self, layer, p, slot):
        return pltpu.make_async_copy(
            self.v.e.at[slot], self.a.e.at[layer, pl.ds(2 * p, 2)], self.sems.e.at[slot]
        )

    def e_load(self, layer, p, slot):
        return pltpu.make_async_copy(
            self.a.e.at[layer, pl.ds(2 * p, 2)], self.v.e.at[slot], self.sems.e.at[slot]
        )

    def e_drain(self, layer):
        for slot in range(2):
            self.e_store(layer, 0, slot).wait()

    def forward(self, layer, small):
        v, width = self.v, self.width
        vec = v.vec.at[layer]
        again = layer == 1

        def before(*names):
            if again:
                for name in names:
                    self.saving(name).wait()

        def done(*names):
            if not again:
                for name in names:
                    self.saving(name).start()

        self.wait_weight(layer, "win")
        before("qkv")
        for part in range(3):
            shift = [vec[0:1, :], None, vec[1:2, :]][part]
            for j in range(width // TILE):
                at = part * width + j * TILE
                got = mm(v.h[...], v.win[:, at : at + TILE])
                if shift is not None:
                    got = got + shift[:, j * TILE : (j + 1) * TILE]
                got = got.astype(BF16)
                if part == 0:
                    got = got * BF16(HEAD_DIM**-0.5)
                v.qkv[:, at : at + TILE] = got
        done("qkv")
        if again:
            self.e_drain(0)
        else:
            self.start_weight(1, "win", 1)
        before("rinv", "mixed")
        low = lax.broadcasted_iota(jnp.int32, (self.length, 128), 1) < HEAD_DIM
        ones = jnp.ones((self.length, 128), BF16)

        def pair(p, carry):
            slot = lax.rem(p, 2)

            @pl.when(p >= 2)
            def _():
                self.e_store(layer, p, slot).wait()

            q = v.qkv[:, lanes(p * 128, 128)]
            k = v.qkv[:, lanes(width + p * 128, 128)]
            values = jnp.concatenate([v.qkv[:, lanes(2 * width + p * 128, 128)], ones], axis=1)
            outs = []
            for i in range(2):
                qm = jnp.where(low if i == 0 else ~low, q, BF16(0))
                s = mm_right_t(qm, k) + v.bias[...]
                top = jnp.max(s, axis=1, keepdims=True)
                e = jnp.exp(s - top).astype(BF16)
                v.e[slot, i] = e
                outs.append(mm(e, values))
            self.e_store(layer, p, slot).start()
            r0 = 1.0 / outs[0][:, 128:]
            r1 = 1.0 / outs[1][:, 128:]
            m = jnp.where(low, outs[0][:, :128] * r0, outs[1][:, :128] * r1)
            v.mixed[:, lanes(p * 128, 128)] = m.astype(BF16)
            v.rinv[:, lanes(p * 128, 128)] = jnp.where(low, r0, r1)
            return carry

        lax.fori_loop(0, HEADS // 2, pair, 0)
        done("rinv", "mixed")

        self.wait_weight(layer, "wout")
        before("xhat1", "rr", "firstb")

        def mask(b):
            place = lax.broadcasted_iota(jnp.int32, (BLOCK, 1), 0) + b * BLOCK
            return (place < self.valid).astype(F32)

        def norm_first(b, total):
            rows = rows_of(b, BLOCK)
            branch = mm(v.mixed[rows, :], v.wout[...]) + vec[2:3, :]
            u = v.h[rows, :].astype(F32) + branch
            c = u - jnp.mean(u, axis=1, keepdims=True)
            f = lax.rsqrt(jnp.mean(c * c, axis=1, keepdims=True) + EPSILON)
            x = c * f
            v.xhat1[rows, :] = x
            v.rr[0, rows, :] = jnp.broadcast_to(f, (BLOCK, 128))
            y = x * vec[3:4, :] + vec[5:6, :]
            v.first[rows, :] = y
            v.firstb[rows, :] = y.astype(BF16)
            return total + jnp.sum(mask(b) * branch * branch, axis=0, keepdims=True)

        zero = jnp.zeros((1, width), F32)
        blocks = self.length // BLOCK
        branch_sum = lax.fori_loop(0, blocks, norm_first, zero)
        done("xhat1", "firstb")
        if not again:
            self.start_weight(1, "wout", 1)

        before("act", "slope")
        v.feed[...] = jnp.broadcast_to(vec[11:12, :], v.feed.shape)

        def widen(j):
            at = lanes(j * width, width)
            hid = mm(v.firstb[...], v.wid[:, at]) + vec[pl.ds(7 + j, 1), :]
            a, d = gelu_and_slope(hid)
            v.act[:, at] = a.astype(BF16)
            v.slope[:, at] = d.astype(BF16)

        def narrow(j):
            v.feed[...] += mm(v.act[:, lanes(j * width, width)], v.nar[rows_of(j, width), :])

        self.wait_piece(layer, "wid", 0)
        widen(0)

        def ffn(j, carry):
            self.wait_piece(layer, "wid", j)
            self.wait_piece(layer, "nar", j - 1)
            narrow(j - 1)
            widen(j)
            return carry

        parts = self.ff // width
        lax.fori_loop(1, parts, ffn, 0)
        done("act", "slope")
        self.wait_piece(layer, "nar", parts - 1)
        narrow(parts - 1)
        if not again:
            self.start_weight(1, "wid", 1)
            self.start_weight(1, "nar", 1)
        before("xhat2")

        def norm_second(b, totals):
            rows = rows_of(b, BLOCK)
            fd = v.feed[rows, :]
            u = v.first[rows, :] + fd
            c = u - jnp.mean(u, axis=1, keepdims=True)
            f = lax.rsqrt(jnp.mean(c * c, axis=1, keepdims=True) + EPSILON)
            x = c * f
            v.xhat2[rows, :] = x
            v.rr[1, rows, :] = jnp.broadcast_to(f, (BLOCK, 128))
            y = x * vec[4:5, :] + vec[6:7, :]
            v.first[rows, :] = y
            if not again:
                v.h[rows, :] = y.astype(BF16)
            ok = mask(b)
            return (
                totals[0] + jnp.sum(ok * u * u, axis=0, keepdims=True),
                totals[1] + jnp.sum(ok * fd * fd, axis=0, keepdims=True),
            )

        stream_sum, feed_sum = lax.fori_loop(0, blocks, norm_second, (zero, zero))
        done("xhat2", "rr")
        for i in range(8):
            small[i : i + 1, :] = v.first[pl.ds(self.cls_at[i], 1), :]
        small[8:9, :] = stream_sum
        small[9:10, :] = branch_sum
        small[10:11, :] = feed_sum
        small[11:12, :] = jnp.full((1, width), self.valid.astype(F32))
        small[12:16, :] = jnp.zeros((4, width), F32)

    def wait_saved(self, restored, *names):
        if restored:
            for name in names:
                if name in WEIGHTS:
                    self.wait_weight(0, name)
                else:
                    self.restoring(name).wait()

    def restore(self, *names):
        for name in names:
            if name in WEIGHTS:
                self.start_weight(0, name, 2)
            else:
                self.restoring(name).start()

    def send_out(self, stage, shift, n, value, target):
        slot = lax.rem(n, 2)

        @pl.when(n >= 2)
        def _():
            pltpu.make_async_copy(stage.at[slot], target, self.sems.stage.at[shift + slot]).wait()

        stage[slot] = value.astype(BF16)
        pltpu.make_async_copy(stage.at[slot], target, self.sems.stage.at[shift + slot]).start()

    def put_rows(self, n, value, target):
        self.send_out(self.v.row_stage, 0, n, value, target)

    def put_cols(self, n, value, target):
        self.send_out(self.v.col_stage, 2, n, value, target)

    def drain_rows(self, grad):
        for slot in range(2):
            pltpu.make_async_copy(self.v.row_stage.at[slot], grad.at[0, 0:TILE, :], self.sems.stage.at[slot]).wait()

    def drain_cols(self, grad):
        for slot in range(2):
            pltpu.make_async_copy(
                self.v.col_stage.at[slot], grad.at[0, :, 0:TILE], self.sems.stage.at[2 + slot]
            ).wait()

    def norms(self, vec, source, x_ref, f_at, gain, target, target_b, where):
        v = self.v
        zero = jnp.zeros((1, self.width), F32)

        def body(b, total):
            rows = rows_of(b, BLOCK)
            up = source[rows, :].astype(F32)
            x = x_ref[rows, :]
            d = norm_back(up * vec[gain : gain + 1, :], x, v.rr[f_at, rows, 0:1])
            target[rows, :] = d
            db = d.astype(BF16)
            target_b[rows, :] = db
            return (
                total[0] + jnp.sum(up * x, axis=0, keepdims=True),
                total[1] + jnp.sum(up, axis=0, keepdims=True),
                total[2] + jnp.sum(db.astype(F32), axis=0, keepdims=True),
            )

        got = lax.fori_loop(0, self.length // BLOCK, body, (zero, zero, zero))
        for i in range(3):
            v.sums[where + i : where + i + 1, :] = got[i]

    def din_kept(self, source):
        return pltpu.make_async_copy(source, self.a.din_kept, self.sems.h.at[2])

    def din_sent(self, source):
        return pltpu.make_async_remote_copy(
            src_ref=source, dst_ref=self.a.din_got, send_sem=self.sems.din.at[0], recv_sem=self.sems.din.at[1],
            device_id=self.a.other, device_id_type=MESH,
        )

    def backward(self, layer, grad, small):
        v, width, restored = self.v, self.width, layer == 0
        vec = v.vec.at[layer]
        dh, dqkv, dbr, dres, ds = v.slope, v.qkv, v.g, v.feed, v.first

        def second():
            self.wait_saved(restored, "xhat2", "rr")
            self.norms(vec, v.g, v.xhat2, 1, 4, ds, v.dfeed, 0)
            self.wait_saved(restored, "nar", "act", "slope", "firstb")

        def ffn(low, i, carry):
            at = lanes(i * 2 * TILE, 2 * TILE)
            da = mm_right_t(v.dfeed[...], v.nar[at, :])
            d = (v.slope[:, at].astype(F32) * da).astype(BF16)
            dh[:, at] = d
            d_narrow = mm_left_t(v.act[:, at], v.dfeed[...])
            d_widen = mm_left_t(v.firstb[...], d)
            d_bias = jnp.sum(d.astype(F32), axis=0, keepdims=True)
            for half in range(2):
                j, part = 2 * i + half, slice(half * TILE, (half + 1) * TILE)
                place = lanes(lax.rem(j, 3) * TILE, TILE)
                v.wbias[pl.ds(j, 1), :] = d_bias[:, part]
                self.put_rows(j - low, d_narrow[part, :], grad.at[2 * (j // 3), place, :])
                self.put_cols(j - low, d_widen[:, part], grad.at[2 * (j // 3) + 1, :, place])
            return carry

        def tiles(low, high):
            lax.fori_loop(low // 2, high // 2, functools.partial(ffn, low), 0)

        def first_grad():
            self.wait_saved(restored, "wid")

            def body(j, carry):
                at = lanes(j * TILE, TILE)
                ds[:, at] = ds[:, at] + mm_right_t(dh[...], v.wid[at, :])
                return carry

            lax.fori_loop(0, width // TILE, body, 0)

        def first():
            self.wait_saved(restored, "xhat1")
            self.norms(vec, ds, v.xhat1, 0, 3, dres, dbr, 3)

        def out_grad():
            self.wait_saved(restored, "mixed", "wout", "rinv", "qkv")

            def body(j, carry):
                at = lanes(j * TILE, TILE)
                self.put_cols(j, mm_left_t(v.mixed[...], dbr[:, at]), grad.at[OUT, :, at])
                d = mm_right_t(dbr[...], v.wout[at, :]).astype(BF16).astype(F32)
                v.dm[:, at] = (d * v.rinv[:, at]).astype(BF16)
                return carry

            lax.fori_loop(0, width // TILE, body, 0)

        def pair(p, carry):
            low = lax.broadcasted_iota(jnp.int32, (self.length, 128), 1) < HEAD_DIM
            slot = lax.rem(p, 2)

            @pl.when(p + 1 < HEADS // 2)
            def _():
                self.e_load(layer, p + 1, 1 - slot).start()

            at_q, at_k, at_v = lanes(p * 128, 128), lanes(width + p * 128, 128), lanes(2 * width + p * 128, 128)
            q, k, values = v.qkv[:, at_q], v.qkv[:, at_k], v.qkv[:, at_v]
            d = v.dm[:, at_q]
            prod = d.astype(F32) * v.mixed[:, at_q].astype(F32)
            self.e_load(layer, p, slot).wait()
            dq, dk, dv = [], [], []
            for i in range(2):
                mine = low if i == 0 else ~low
                delta = jnp.sum(jnp.where(mine, prod, 0.0), axis=1, keepdims=True)
                dp = mm_right_t(jnp.where(mine, d, BF16(0)), values)
                e = v.e[slot, i]
                s = (e.astype(F32) * (dp - delta)).astype(BF16)
                dq.append(mm(s, k))
                dk.append(mm_left_t(s, q))
                dv.append(mm_left_t(e, d))
            dqkv[:, at_q] = (jnp.where(low, dq[0], dq[1]) * HEAD_DIM**-0.5).astype(BF16)
            dqkv[:, at_k] = jnp.where(low, dk[0], dk[1]).astype(BF16)
            dqkv[:, at_v] = jnp.where(low, dv[0], dv[1]).astype(BF16)
            return carry

        def pairs(low, high):
            lax.fori_loop(low, high, pair, 0)

        def in_grad(low, high):
            if restored:
                pl.when(low == 0)(lambda: self.load_input(self.a.hidden).wait())

            def body(j, carry):
                at = lanes(j * TILE, TILE)
                place = lanes(lax.rem(j, 3) * TILE, TILE)
                self.put_cols(j - low, mm_left_t(v.h[...], dqkv[:, at]), grad.at[IN + j // 3, :, place])
                return carry

            lax.fori_loop(low, high, body, 0)

        def input_grad():
            self.wait_saved(restored, "win")

            def body(j, carry):
                at = lanes(j * TILE, TILE)
                d = dres[:, at] + mm_right_t(dqkv[...], v.win[at, :])
                dres[:, at] = d
                if layer == 1:
                    v.g[:, at] = d.astype(BF16)
                return carry

            lax.fori_loop(0, width // TILE, body, 0)
            pl.when(self.section == layer)(lambda: self.din_kept(dres).start())
            pl.when(self.section != layer)(lambda: self.din_sent(dres).start())
            small[16:17, :] = jnp.sum(dqkv[:, 0:width].astype(F32), axis=0, keepdims=True)
            small[17:18, :] = jnp.sum(dqkv[:, 2 * width :].astype(F32), axis=0, keepdims=True)
            for i, source in enumerate((5, 3, 0, 4, 1)):
                small[18 + i : 19 + i, :] = v.sums[source : source + 1, :]
            for i in range(self.ff // TILE):
                small[23 + i // 3 : 24 + i // 3, (i % 3) * TILE : (i % 3 + 1) * TILE] = v.wbias[i : i + 1, :]
            small[27:28, :] = v.sums[2:3, :]
            small[28:32, :] = jnp.zeros((4, width), F32)

        def input_done():
            pl.when(self.section == layer)(lambda: self.din_kept(dres).wait())
            pl.when(self.section != layer)(lambda: self.din_sent(dres).wait_send())

        def tiles_done():
            self.drain_rows(grad)
            self.drain_cols(grad)

        return Refs(
            second=second, tiles=tiles, first_grad=first_grad, first=first, out_grad=out_grad, pairs=pairs, in_grad=in_grad,
            input_grad=input_grad, input_done=input_done, tiles_done=tiles_done,
            cols_done=lambda: self.drain_cols(grad),
        )


def sum_plan(devices, rows):
    side = round((devices / 2) ** (1 / 3))
    extents = [side, side, devices // (side * side)]
    axes, stride = [], 1
    for extent in extents:
        steps, step = [], 1
        while step < extent:
            steps.append(stride * step)
            step *= 2
        axes.append(steps)
        stride *= extent
    x, y, z = axes
    distances = x + y + z
    swaps = lambda order, active=None: [("swap", distance, active) for distance in order]
    unit = 256 if devices <= 16 else 128
    run = 5 * unit // 2
    count, over = rows // run, rows % run
    return [
        (0, unit, count + (over >= unit), swaps(y + x + z)),
        (unit, unit, count + (over >= 2 * unit), swaps(x + y + z)),
        (2 * unit, unit // 2, count, swaps(z + x + y)),
    ], distances, None


class Stage:
    def __init__(self, kind, rows, cols, send, to, recv, source, sent, got):
        self.kind, self.rows, self.cols = kind, rows, cols
        self.send, self.to, self.recv, self.source, self.sent, self.got = send, to, recv, source, sent, got


def message_shapes(unit, width, spec):
    rows, cols, shapes = unit // 2, width, []
    for i, (kind, arg, _) in enumerate(spec):
        if kind == "chain":
            if arg == 0:
                rows //= 2
        elif kind != "fold":
            if rows >= 32:
                rows //= 2
            elif cols == width:
                cols //= 2
            else:
                kind = "full"
        shapes.append((kind, rows, cols))
    return shapes


def build_stages(unit, width, spec, me, line):
    rows, cols = unit // 2, width
    row = col = me * 0
    if line is not None:
        stride, depth = line
        z = me // stride
    flag = lambda condition: condition.astype(jnp.int32)
    stages = []
    for kind, arg, active in spec:
        if kind == "fold":
            first, third = flag(z == arg), flag(z == arg + 1)
            send, recv = (z == arg) | (z == depth - 1 - arg), (z == arg + 1) | (z == depth - 2 - arg)
            place = (row, col)
            stages.append(Stage(
                kind, rows, cols, send, me + stride * (2 * first - 1), recv, me + stride * (1 - 2 * third), place, place
            ))
        elif kind == "chain":
            if arg == 0:
                rows //= 2
                base = row
            up, came = flag(z == arg), flag(z == arg + 1)
            send, recv = (z == arg) | (z == depth - 1 - arg), (z == arg + 1) | (z == depth - 2 - arg)
            stages.append(Stage(
                kind, rows, cols, send, me + stride * (2 * up - 1), recv, me + stride * (1 - 2 * came),
                (base + up * rows, col), (base + came * rows, col),
            ))
            if arg == depth - 2:
                row = base + flag(z == depth - 1) * rows
        else:
            if kind == "middle":
                bit, distance = flag(z >= depth // 2), stride
                active = "middle"
            else:
                bit, distance = lax.rem(me // arg, 2), arg
            if active == "middle":
                on = (z == depth // 2 - 1) | (z == depth // 2)
            elif active == "ends":
                on = (z == 0) | (z == depth - 1)
            else:
                on = None
            partner = me + distance * (1 - 2 * bit)
            sent = (row, col)
            kind = "swap"
            if rows >= 32:
                rows //= 2
                sent, row = (row + (1 - bit) * rows, col), row + bit * rows
            elif cols == width:
                cols //= 2
                sent, col = (row, col + (1 - bit) * cols), col + bit * cols
            else:
                kind = "full"
            stages.append(Stage(kind, rows, cols, on, partner, on, partner, sent, (row, col)))
    return stages


def when(condition, action):
    if condition is None:
        action()
    else:
        pl.when(condition)(action)


class GradientSum:
    def __init__(self, plan, distances, line, width, grads, out, buffers, sems):
        self.plan, self.distances, self.line, self.width, self.grads, self.out = plan, distances, line, width, grads, out
        self.run = sum(unit for _, unit, _, _ in plan)
        self.section, self.me = lax.axis_index("section"), lax.axis_index("dp")
        self.peer = (1 - self.section, self.me)
        self.parts = [build_stages(unit, width, spec, self.me, line) for _, unit, _, spec in plan]
        self.slots = [slots_of(spec) for _, _, _, spec in plan]
        self.total, self.other, self.recvs, self.fulls = buffers
        self.keep_sems, self.pair_sems, self.trade_sems, self.end_sems, self.send_sems, self.rs_sems, self.ag_sems = sems[:7]
        self.free, self.full_free = sems[7:]
        self.length = max(2 * count + 2 * len(spec) + 2 for _, _, count, spec in plan)

    def partner(self, distance):
        return (self.section, self.me + distance * (1 - 2 * lax.rem(self.me // distance, 2)))

    def barrier(self):
        barrier = pltpu.get_barrier_semaphore()
        for device in [self.peer] + [self.partner(distance) for distance in self.distances]:
            pl.semaphore_signal(barrier, inc=1, device_id=device, device_id_type=MESH)
        neighbours = []
        if self.line is not None:
            stride, depth = self.line
            z = self.me // stride
            neighbours = [(z > 0, -stride), (z < depth - 1, stride)]
        for there, distance in neighbours:

            @pl.when(there)
            def _(distance=distance):
                pl.semaphore_signal(
                    barrier, inc=1, device_id=(self.section, self.me + distance), device_id_type=MESH
                )

        pl.semaphore_wait(barrier, len(self.distances) + 1)
        for there, _ in neighbours:
            pl.when(there)(lambda: pl.semaphore_wait(barrier, 1))

    def slot(self, part, k):
        return lax.rem(k, self.slots[part])

    def stage_slot(self, part, k, s):
        return lax.rem(k, stage_slots_of(self.plan[part][3], s))

    def half_rows(self, ref, part, k, which):
        base, unit, count, _ = self.plan[part]
        row = base + lax.rem(k, count) * self.run + which * (unit // 2)
        return ref.at[row // self.width, pl.ds(pl.multiple_of(lax.rem(row, self.width), 16), unit // 2)]

    def load(self, part, k, source):
        slot = self.slot(part, k)
        return pltpu.make_async_copy(
            self.half_rows(source, part, k, self.section), self.total[part].at[slot], self.keep_sems[part].at[slot]
        )

    def trade(self, part, k, source):
        slot = self.slot(part, k)
        return pltpu.make_async_remote_copy(
            src_ref=self.half_rows(source, part, k, 1 - self.section), dst_ref=self.other[part].at[slot],
            send_sem=self.pair_sems[part].at[slot], recv_sem=self.trade_sems[part].at[slot],
            device_id=self.peer, device_id_type=MESH,
        )

    def keep(self, part, k):
        slot = self.slot(part, k)
        return pltpu.make_async_copy(
            self.other[part].at[slot], self.half_rows(self.out, part, k, self.section), self.keep_sems[part].at[slot]
        )

    def hand_over(self, part, k):
        slot = self.slot(part, k)
        return pltpu.make_async_remote_copy(
            src_ref=self.other[part].at[slot], dst_ref=self.half_rows(self.out, part, k, self.section),
            send_sem=self.pair_sems[part].at[slot], recv_sem=self.end_sems[part].at[slot],
            device_id=self.peer, device_id_type=MESH,
        )

    def view(self, ref, slot, stage, place):
        row, col = place
        at = pl.ds(pl.multiple_of(row, 16), stage.rows)
        if stage.cols == self.width:
            return ref.at[slot, at]
        return ref.at[slot, at, pl.ds(pl.multiple_of(col, 128), stage.cols)]

    def held(self, part, k, s, place):
        stages = self.parts[part]
        fulls = [i for i in range(s + 1) if stages[i].kind == "full"]
        if fulls:
            return self.fulls[part][fulls[-1]].at[self.slot(part, k)]
        return self.view(self.total[part], self.slot(part, k), stages[s], place)

    def reduce_copy(self, part, k, s, device):
        stage = self.parts[part][s]
        at = self.stage_slot(part, k, s)
        if stage.kind == "full":
            source = self.held(part, k, s - 1, self.parts[part][s - 1].got)
        else:
            source = self.view(self.total[part], self.slot(part, k), stage, stage.sent)
        return pltpu.make_async_remote_copy(
            src_ref=source, dst_ref=self.recvs[part][s].at[at],
            send_sem=self.send_sems[part][s].at[self.slot(part, k)], recv_sem=self.rs_sems[part][s].at[at],
            device_id=(self.section, device), device_id_type=MESH,
        )

    def gather_copy(self, part, k, s, device, place):
        stage = self.parts[part][s]
        ref = self.view(self.other[part], self.slot(part, k), stage, place)
        return pltpu.make_async_remote_copy(
            src_ref=ref, dst_ref=ref, send_sem=self.send_sems[part][s].at[self.slot(part, k)],
            recv_sem=self.ag_sems[part][s].at[self.stage_slot(part, k, s)],
            device_id=(self.section, device), device_id_type=MESH,
        )

    def start_reduce(self, part, k, s):
        stage = self.parts[part][s]

        def action():
            if stage.kind == "full":

                @pl.when(k >= stage_slots_of(self.plan[part][3], s))
                def _():
                    pl.semaphore_wait(self.full_free[part][s].at[0], 1)

            self.reduce_copy(part, k, s, stage.to).start()

        when(stage.send, action)

    def end_reduce(self, part, k, s):
        stage = self.parts[part][s]
        slot, at = self.slot(part, k), self.stage_slot(part, k, s)
        last = len(self.parts[part]) - 1

        def action():
            self.reduce_copy(part, k, s, stage.source).wait_recv()
            if stage.kind == "full":
                left = self.held(part, k, s - 1, self.parts[part][s - 1].got)
            else:
                left = self.view(self.total[part], slot, stage, stage.got)
            target = self.view(self.other[part], slot, stage, stage.got) if s == last else self.held(part, k, s, stage.got)
            self.add(target, left, self.recvs[part][s].at[at], stage.rows)
            if stage.kind == "full":

                @pl.when(k + stage_slots_of(self.plan[part][3], s) < 2 * self.plan[part][2])
                def _():
                    pl.semaphore_signal(
                        self.full_free[part][s].at[0], inc=1, device_id=(self.section, stage.source),
                        device_id_type=MESH,
                    )

        when(stage.recv, action)

    def start_gather(self, part, k, s):
        stage = self.parts[part][s]
        if stage.kind == "full":
            return
        when(stage.send, lambda: self.reduce_copy(part, k, s, stage.to).wait_send())
        when(stage.recv, lambda: self.gather_copy(part, k, s, stage.source, stage.got).start())

    def end_gather(self, part, k, s):
        stage = self.parts[part][s]
        if stage.kind != "full":
            when(stage.send, lambda: self.gather_copy(part, k, s, stage.to, stage.sent).wait_recv())

    def owned(self, part, k):
        return (k < self.plan[part][2]) == (self.section == 1)

    def add(self, target, left, right, rows):
        block = min(rows, 32)

        def body(i, carry):
            at = pl.ds(pl.multiple_of(i * block, 16), block)
            target[at, :] = left[at, :] + right[at, :]
            return carry

        lax.fori_loop(0, rows // block, body, 0)

    def retire(self, part, k):
        for s, stage in enumerate(self.parts[part]):
            if stage.kind == "full":
                when(stage.send, lambda s=s, stage=stage: self.reduce_copy(part, k, s, stage.to).wait_send())
            else:
                when(stage.recv, lambda s=s, stage=stage: self.gather_copy(part, k, s, stage.source, stage.got).wait_send())
        mine = self.owned(part, k)
        pl.when(mine)(lambda: self.keep(part, k).wait())
        pl.when(jnp.logical_not(mine))(lambda: self.hand_over(part, k).wait_send())

    def task(self, part, k, s):
        last = len(self.parts[part]) - 1
        slots, count = self.slots[part], self.plan[part][2]
        if s == 0:

            @pl.when(k >= slots)
            def _():
                self.retire(part, k - slots)
                pl.semaphore_signal(self.free.at[part], inc=1, device_id=self.peer, device_id_type=MESH)
                pl.semaphore_wait(self.free.at[part], 1)

            first = k < count

            @pl.when(first)
            def _():
                self.load(part, k, self.grads[1]).start()
                self.trade(part, k, self.grads[1]).start()

            @pl.when(jnp.logical_not(first))
            def _():
                self.load(part, k, self.grads[0]).start()
                self.trade(part, k, self.grads[0]).start()

        elif s == 1:
            self.load(part, k, self.grads[0]).wait()
            self.trade(part, k, self.grads[0]).wait_recv()
            total = self.total[part].at[self.slot(part, k)]
            self.add(total, total, self.other[part].at[self.slot(part, k)], self.plan[part][1] // 2)
            self.start_reduce(part, k, 0)
        elif s <= last + 2:
            self.end_reduce(part, k, s - 2)
            if s - 1 <= last:
                self.start_reduce(part, k, s - 1)
            else:
                self.start_gather(part, k, last)
        elif s <= 2 * last + 3:
            j = 2 * last + 3 - s
            self.end_gather(part, k, j)
            if j > 0:
                self.start_gather(part, k, j - 1)
            else:
                self.trade(part, k, self.grads[0]).wait_send()
                mine = self.owned(part, k)
                pl.when(mine)(lambda: self.keep(part, k).start())
                pl.when(jnp.logical_not(mine))(lambda: self.hand_over(part, k).start())
        else:
            pl.when(self.owned(part, k))(lambda: self.hand_over(part, k).wait_recv())

    def step(self, t):
        most = max(len(stages) for stages in self.parts)
        for s in range(2 * most + 3):
            for part, (_, _, count, spec) in enumerate(self.plan):
                if s < 2 * len(spec) + 3:
                    k = t - s
                    pl.when((k >= 0) & (k < 2 * count))(lambda part=part, s=s, k=k: self.task(part, k, s))

    def finish(self):
        for part, (_, _, count, _) in enumerate(self.plan):

            def body(k, carry, part=part):
                self.retire(part, k)
                return carry

            lax.fori_loop(max(2 * count - self.slots[part], 0), 2 * count, body, 0)


def slots_of(spec):
    return 2 * len(spec) + 3


def stage_slots_of(spec, s):
    return 2 * (len(spec) - s) + 1


def sum_scratch(plan, width):
    shapes, names = [], []

    def need(name, part, s, shape):
        names.append((name, part, s))
        shapes.append(shape)

    for part, (_, unit, _, spec) in enumerate(plan):
        slots = slots_of(spec)
        steps = message_shapes(unit, width, spec)
        for name in ("total", "other"):
            need(name, part, 0, pltpu.VMEM((slots, unit // 2, width), BF16))
        for name in ("keep", "pair", "trade", "end"):
            need(name, part, 0, pltpu.SemaphoreType.DMA((slots,)))
        for s, (kind, rows, cols) in enumerate(steps):
            at = stage_slots_of(spec, s)
            need("recv", part, s, pltpu.VMEM((at, rows, cols), BF16))
            need("send", part, s, pltpu.SemaphoreType.DMA((slots,)))
            need("rs", part, s, pltpu.SemaphoreType.DMA((at,)))
            if kind == "full":
                need("full_free", part, s, pltpu.SemaphoreType.REGULAR((1,)))
                if s < len(steps) - 1:
                    need("full", part, s, pltpu.VMEM((slots, rows, cols), BF16))
            else:
                need("ag", part, s, pltpu.SemaphoreType.DMA((at,)))
    need("free", 0, 0, pltpu.SemaphoreType.REGULAR((len(plan),)))

    def split(refs):
        by_name = {}
        for (name, part, s), ref in zip(names, refs):
            by_name.setdefault(name, {}).setdefault(part, {})[s] = ref
        one = lambda name: [by_name[name][part][0] for part in range(len(plan))]
        many = lambda name: [by_name.get(name, {}).get(part, {}) for part in range(len(plan))]
        buffers = (one("total"), one("other"), many("recv"), many("full"))
        sems = (
            one("keep"), one("pair"), one("trade"), one("end"), many("send"), many("rs"), many("ag"),
            by_name["free"][0][0], many("full_free"),
        )
        return buffers, sems

    return shapes, split


def layers_kernel(plan, distances, line, split, *refs):
    refs = list(refs)
    take = lambda n: [refs.pop(0) for _ in range(n)]
    valid_ref, cls_ref, seg_ref, proj_bias, out_shift, gains, shifts, widen_bias, narrow_bias = take(9)
    hidden, cotangent = take(2)
    own = take(4)
    out, din_kept, din_got, small_got, small_sum, small_mine = take(6)
    grad0, grad1, e_hbm = take(3)
    saved = take(9)
    v = Refs(**dict(zip(VMEM_NAMES, take(len(VMEM_NAMES)))))
    small_send, small_acc, small_recv = take(3)
    weight_sems, sent_sems, arrived_sems, free_sems, saved_sems, e_sems, h_sems, stage_sems, vec_sems, small_sems = take(10)
    din_sems, = take(1)
    section = lax.axis_index("section")
    width = v.h.shape[1]
    total = GradientSum(plan, distances, line, width, (grad0, grad1), out, *split(refs))
    compute = Compute(
        v,
        Refs(own=own, other=total.peer, saved=saved, e=e_hbm, hidden=hidden, din_kept=din_kept, din_got=din_got),
        Refs(
            weights=weight_sems, sent=sent_sems, arrived=arrived_sems, free=free_sems, saved=saved_sems, e=e_sems, h=h_sems,
            stage=stage_sems, din=din_sems,
        ),
        section, valid_ref[section], [cls_ref[section, i] for i in range(8)],
    )

    def vec_sent():
        return pltpu.make_async_remote_copy(
            src_ref=v.vec_own, dst_ref=v.vec_peer, send_sem=vec_sems.at[0], recv_sem=vec_sems.at[1],
            device_id=total.peer, device_id_type=MESH,
        )

    compute.load_input(hidden).start()
    v.vec_own[0:2, :] = proj_bias[0]
    v.vec_own[2:3, :] = out_shift[...]
    v.vec_own[3:5, :] = gains[0]
    v.vec_own[5:7, :] = shifts[0]
    for i in range(4):
        v.vec_own[7 + i : 8 + i, :] = widen_bias[:, i * width : (i + 1) * width]
    v.vec_own[11:12, :] = narrow_bias[...]
    v.vec_own[12:16, :] = jnp.zeros((4, width), F32)
    total.barrier()
    vec_sent().start()
    compute.start_weight(0, "win", 0)
    compute.start_weight(0, "wout", 0)
    for q in range(compute.pieces("wid")):
        compute.start_weight(0, "wid", 0, q)
        compute.start_weight(0, "nar", 0, q)
    segments = seg_ref[pl.ds(section, 1), :]
    columns = jnp.broadcast_to(segments.astype(F32), (128, compute.length)).T[:, :1]
    v.bias[...] = jnp.where(columns == segments.astype(F32), 0.0, MASKED)
    compute.load_cotangent(cotangent).start()
    vec_sent().wait_recv()
    for layer in range(2):
        v.vec[layer] = jnp.where(section == layer, v.vec_own[...], v.vec_peer[...])
    compute.load_input(hidden).wait()

    small0, small1 = v.small.at[0], v.small.at[1]
    compute.forward(0, small0)
    compute.forward(1, small1)
    compute.e_drain(1)
    compute.e_load(1, 0, 0).start()
    compute.load_cotangent(cotangent).wait()

    rounds = len(distances)

    def small_trade():
        return pltpu.make_async_remote_copy(
            src_ref=small_send, dst_ref=small_got, send_sem=small_sems.at[0, rounds], recv_sem=small_sems.at[1, rounds],
            device_id=total.peer, device_id_type=MESH,
        )

    def small_copy(i):
        return pltpu.make_async_remote_copy(
            src_ref=small_acc.at[i], dst_ref=small_recv.at[i], send_sem=small_sems.at[0, i],
            recv_sem=small_sems.at[1, i], device_id=total.partner(distances[i]), device_id_type=MESH,
        )

    def small_start():
        small_mine[...] = jnp.where(section == 0, small0[...], small1[...])
        small_send[...] = jnp.where(section == 0, small1[...], small0[...])
        small_trade().start()

    def small_step(stage):
        if stage == 0:
            small_trade().wait_recv()
            small_acc[0] = small_mine[8:, :] + small_got[8:, :]
        else:
            small_copy(stage - 1).wait_recv()
            small_acc[stage] = small_acc[stage - 1] + small_recv[stage - 1]
        if stage < rounds:
            small_copy(stage).start()
        else:
            small_sum[...] = small_acc[stage]

    one = compute.backward(1, grad1, small1)
    zero = compute.backward(0, grad0, small0)
    restore = compute.restore
    def tiles_of(layer, first):
        def action(t):
            begin = t == first
            pl.when(t > first)(layer.tiles_done)
            number = jnp.clip(t - first, 0, 4)
            layer.tiles(jnp.where(begin, 0, 2 + 2 * number), 4 + 2 * number)

        return first, first + 4, action

    def pairs_of(layer, first):
        def action(t):
            pl.when(t == first)(layer.cols_done)
            number = jnp.clip(t - first, 0, 2)
            layer.pairs(2 * number, 2 * number + 2)

        return first, first + 2, action

    def in_grad_of(layer, first, drained=0):
        def action(t):
            begin = t == first
            pl.when(t > first + drained)(layer.cols_done)
            layer.in_grad(jnp.where(begin, 0, 5), jnp.where(begin, 5, 9))

        return first, first + 1, action

    def at(t, *actions):
        def action(_):
            for act in actions:
                act()

        return t, t, action

    def later_tiles(t):
        pl.when(t > 0)(one.tiles_done)
        number = jnp.clip(t, 0, 3)
        one.tiles(4 + 2 * number, 6 + 2 * number)

    do = functools.partial
    one.second()
    one.tiles(0, 4)
    one.tiles_done()
    events = [
        (0, 3, later_tiles),
        at(3, do(restore, "nar", "act", "firstb", "xhat2")),
        at(4, one.tiles_done, one.first_grad, do(restore, "slope", "wid")),
        at(5, one.first, do(restore, "xhat1", "rr"), one.out_grad, do(restore, "wout", "rinv")),
        pairs_of(one, 6),
        at(8, do(restore, "mixed"), lambda: compute.e_load(0, 0, 0).start()),
        in_grad_of(one, 9, 1),
        at(9, one.cols_done),
        at(10, lambda: compute.load_input(hidden).start()),
        at(11, one.cols_done, one.input_grad, do(restore, "qkv", "win"), zero.second),
        at(12, one.input_done),
        tiles_of(zero, 12),
        at(17, zero.tiles_done, zero.first_grad),
        at(18, zero.first, zero.out_grad),
        pairs_of(zero, 19),
        in_grad_of(zero, 22),
        at(24, zero.cols_done, zero.input_grad, small_start),
    ] + [at(25 + s, do(small_step, s)) for s in range(rounds + 1)]

    def body(t, carry):
        total.step(t)
        for first, last, action in events:
            pl.when((t >= first) & (t <= last))(lambda action=action: action(t))
        return carry

    lax.fori_loop(0, total.length, body, 0)
    total.finish()
    zero.input_done()
    vec_sent().wait_send()
    for name in WEIGHTS:
        for q in range(compute.pieces(name)):
            compute.weight_sent(name, q).wait_send()
    small_trade().wait_send()
    for i in range(rounds):
        small_copy(i).wait_send()
    compute.din_sent(v.feed).wait_recv()


VMEM_NAMES = (
    "h", "g", "win", "wout", "wid", "nar", "qkv", "e", "rinv", "mixed", "xhat1", "rr", "first", "firstb", "act", "slope",
    "xhat2", "feed", "bias", "dfeed", "dm", "row_stage", "col_stage", "wbias", "sums", "vec", "vec_own", "vec_peer", "small",
)


def layers(valid_counts, cls_positions, segment_ids, vectors, hidden, cotangent, own):
    rows, length = segment_ids.shape
    width, ff = hidden.shape[1], own[2].shape[2]
    devices = lax.axis_size("dp")
    plan, distances, line = sum_plan(devices, 12 * width)
    stages = len(distances)
    shapes, split = sum_scratch(plan, width)
    row_b, row_f = ((length, width), BF16), ((length, width), F32)
    saved = [
        ((length, 3 * width), BF16), row_f, row_b, row_f, ((2, length, 128), F32), row_b, ((length, ff), BF16),
        ((length, ff), BF16), row_f,
    ]
    grad = ((12, width, width), BF16)
    small = ((32, width), F32)
    sums = (24, width)
    outs = [grad, row_f, row_f, small, (sums, F32), small, grad, grad, ((2, HEADS, length, length), BF16), *saved]
    scratch = dict(
        h=row_b, g=row_b, win=(own[0].shape[1:], BF16), wout=(own[1].shape[1:], BF16), wid=(own[2].shape[1:], BF16),
        nar=(own[3].shape[1:], BF16), qkv=saved[0], e=((2, 2, length, length), BF16), rinv=row_f, mixed=row_b, xhat1=row_f,
        rr=saved[4], first=row_f, firstb=row_b, act=saved[6], slope=saved[7], xhat2=row_f, feed=row_f,
        bias=((length, length), F32), dfeed=row_b, dm=row_b, row_stage=((2, TILE, width), BF16),
        col_stage=((2, width, TILE), BF16), wbias=((16, TILE), F32), sums=((8, width), F32), vec=((2, 16, width), F32),
        vec_own=((16, width), F32), vec_peer=((16, width), F32), small=((2, 32, width), F32),
    )
    in_vmem = (3, 4, 5)
    got = pl.pallas_call(
        functools.partial(layers_kernel, plan, distances, line, split),
        out_shape=[jax.ShapeDtypeStruct(s, d) for s, d in outs],
        in_specs=[SMEM, SMEM] + [VMEM] * 7 + [ANY] * 6,
        out_specs=[VMEM if i in in_vmem else ANY for i in range(len(outs))],
        scratch_shapes=[
            *[pltpu.VMEM(*scratch[name]) for name in VMEM_NAMES],
            pltpu.VMEM(*small),
            pltpu.VMEM((stages + 1, *sums), F32),
            pltpu.VMEM((stages, *sums), F32),
            pltpu.SemaphoreType.DMA((10,)),
            pltpu.SemaphoreType.DMA((10,)),
            pltpu.SemaphoreType.DMA((10,)),
            pltpu.SemaphoreType.REGULAR((4,)),
            pltpu.SemaphoreType.DMA((9,)),
            pltpu.SemaphoreType.DMA((2,)),
            pltpu.SemaphoreType.DMA((3,)),
            pltpu.SemaphoreType.DMA((4,)),
            pltpu.SemaphoreType.DMA((2,)),
            pltpu.SemaphoreType.DMA((2, stages + 1)),
            pltpu.SemaphoreType.DMA((2,)),
            *shapes,
        ],
        compiler_params=pltpu.CompilerParams(collective_id=0, has_side_effects=True, vmem_limit_bytes=63 * MIB),
        cost_estimate=pl.CostEstimate(flops=54 * 10**9, bytes_accessed=200 * 10**6, transcendentals=10**7),
        name="layers_and_sum",
    )(valid_counts, cls_positions, segment_ids, *vectors, hidden, cotangent, *own)
    return got[:6]


def finish_kernel(
    flags, blocks, din_kept, din_got, small_mine, small_got, small_sum,
    cls_o, input_o, in_o, bias_o, out_o, out_shift_o, gain_o, shift_o, widen_o, widen_bias_o, narrow_o, narrow_bias_o, rms_o,
    dins, halves, wide, block_sems, din_sems, wide_sems,
):
    section = flags[0]
    got_row = 1 - section
    length, width = din_got.shape
    slots = wide.shape[0]

    def rows(row):
        return input_o.at[0, pl.ds(pl.multiple_of(row * length, 16), length)]

    def target(index):
        part = slice(index // 2 * width, (index // 2 + 1) * width)
        if index >= IN:
            return in_o.at[0, :, (index - IN) * width : (index - IN + 1) * width]
        if index == OUT:
            return out_o.at[0]
        return narrow_o.at[0, part, :] if index % 2 == 0 else widen_o.at[0, :, part]

    loads = [pltpu.make_async_copy(blocks.at[i], halves.at[i], block_sems.at[i]) for i in range(12)]
    stores = [pltpu.make_async_copy(wide.at[i % slots], target(i), wide_sems.at[i % slots]) for i in range(12)]
    din_loads = [pltpu.make_async_copy(din, dins.at[i], din_sems.at[i]) for i, din in enumerate((din_kept, din_got))]
    din_stores = [
        pltpu.make_async_copy(dins.at[i], rows(row), din_sems.at[i]) for i, row in enumerate((section, got_row))
    ]
    for copy in loads[:2] + din_loads + loads[2:]:
        copy.start()
    cls_o[0, section] = small_mine[0:8, :]
    cls_o[0, got_row] = small_got[0:8, :]
    bias_o[0] = small_sum[8:10, :]
    out_shift_o[...] = small_sum[10:11, :]
    gain_o[0] = small_sum[11:13, :]
    shift_o[0] = small_sum[13:15, :]
    for i in range(4):
        widen_bias_o[0:1, i * width : (i + 1) * width] = small_sum[15 + i : 16 + i, :]
    narrow_bias_o[...] = small_sum[19:20, :]
    for i in range(3):
        squares = jnp.sum(small_sum[i : i + 1, :], axis=1, keepdims=True)
        rms_o[0:1, i : i + 1] = jnp.sqrt(squares / (small_sum[3:4, 0:1] * width))

    for i in range(12):
        loads[i].wait()
        if i >= slots:
            stores[i - slots].wait()

        def widen_rows(b, carry, i=i):
            at = rows_of(b, 64)
            wide[i % slots, at, :] = halves[i, at, :].astype(F32)
            return carry

        lax.fori_loop(0, width // 64, widen_rows, 0)
        stores[i].start()
        if i == 1:
            for load, store in zip(din_loads, din_stores):
                load.wait()
                store.start()
    for copy in stores[12 - slots :] + din_stores:
        copy.wait()


def finish(section, blocks, din_kept, din_got, small_mine, small_got, small_sum):
    length, width = din_got.shape
    shapes = [
        (1, 2, 8, width), (1, 2 * length, width), (1, width, 3 * width), (1, 2, width), (1, width, width), (1, width),
        (1, 2, width), (1, 2, width), (1, width, 4 * width), (1, 4 * width), (1, 4 * width, width), (1, width), (1, 3),
    ]
    big = (1, 2, 4, 8, 10)
    return pl.pallas_call(
        finish_kernel,
        out_shape=[jax.ShapeDtypeStruct(s, F32) for s in shapes],
        in_specs=[SMEM] + [ANY] * 3 + [VMEM] * 3,
        out_specs=[ANY if i in big else VMEM for i in range(len(shapes))],
        scratch_shapes=[
            pltpu.VMEM((2, length, width), F32),
            pltpu.VMEM(blocks.shape, BF16),
            pltpu.VMEM((6, width, width), F32),
            pltpu.SemaphoreType.DMA((12,)),
            pltpu.SemaphoreType.DMA((2,)),
            pltpu.SemaphoreType.DMA((6,)),
        ],
        compiler_params=pltpu.CompilerParams(vmem_limit_bytes=63 * MIB),
        cost_estimate=pl.CostEstimate(flops=10**7, bytes_accessed=46 * 10**6, transcendentals=0),
        name="finish",
    )(section[None], blocks, din_kept, din_got, small_mine, small_got, small_sum)


def local(
    hidden_in, segment_ids, cls_positions, valid_counts, proj_in, proj_bias, proj_out, out_shift, norm_gains,
    norm_shifts, widen, widen_bias, narrow, narrow_bias, cotangent,
):
    section = lax.axis_index("section")
    vectors = (proj_bias, out_shift, norm_gains, norm_shifts, widen_bias, narrow_bias)
    blocks, din_kept, din_got, small_got, small_sum, small_mine = layers(
        valid_counts, cls_positions, segment_ids, vectors, hidden_in, cotangent, (proj_in, proj_out, widen, narrow)
    )
    return finish(section, blocks, din_kept, din_got, small_mine, small_got, small_sum)


def solution(mesh):
    placed = (
        P("dp", None),
        P("dp", None),
        P("dp", None),
        P("dp"),
        P("section", None, None),
        P("section", None, None),
        P("section", None, None),
        P("section", None),
        P("section", None, None),
        P("section", None, None),
        P("section", None, None),
        P("section", None),
        P("section", None, None),
        P("section", None),
        P("dp", None),
    )
    return jax.shard_map(
        local,
        mesh=mesh,
        in_specs=placed,
        out_specs=(
            P("section", "dp", None, None),
            P("section", "dp", None),
            P("section", None, None),
            P("section", None, None),
            P("section", None, None),
            P("section", None),
            P("section", None, None),
            P("section", None, None),
            P("section", None, None),
            P("section", None),
            P("section", None, None),
            P("section", None),
            P("section", None),
        ),
        check_vma=False,
    )
```

```python
import functools

import jax
import jax.numpy as jnp
from jax import lax
from jax.experimental import pallas as pl
from jax.experimental.pallas import tpu as pltpu
from jax.sharding import PartitionSpec as P

HEADS = 12
HEAD_DIM = 64
EPSILON = 1e-12
MASKED = -1e30
F32 = jnp.float32
BF16 = jnp.bfloat16
MIB = 2**20
TILE = 256
BLOCK = 128
ANY = pl.BlockSpec(memory_space=pl.ANY)
VMEM = pl.BlockSpec(memory_space=pltpu.VMEM)
SMEM = pl.BlockSpec(memory_space=pltpu.SMEM)
MESH = pl.DeviceIdType.MESH
OUT, IN = 8, 9


def mm(left, right):
    return jnp.dot(left, right, preferred_element_type=F32)


def mm_left_t(left, right):
    return lax.dot_general(left, right, (((0,), (0,)), ((), ())), preferred_element_type=F32)


def mm_right_t(left, right):
    return lax.dot_general(left, right, (((1,), (1,)), ((), ())), preferred_element_type=F32)


def lanes(start, size):
    return pl.ds(pl.multiple_of(start, size), size)


def rows_of(b, size):
    return pl.ds(pl.multiple_of(b * size, size), size)


def gelu_and_slope(v):
    z = jnp.abs(v) * 0.7071067811865476
    t = 1.0 / (1.0 + 0.3275911 * z)
    e = jnp.exp(-0.5 * v * v)
    poly = t * (
        0.127414796 + t * (-0.142248368 + t * (0.7107068705 + t * (-0.7265760135 + t * 0.5307027145)))
    )
    tail = poly * e
    cdf = jnp.where(v >= 0, 1.0 - tail, tail)
    return v * cdf, cdf + v * e * 0.3989422804014327


def norm_back(up, x, f):
    return f * (up - jnp.mean(up, axis=1, keepdims=True) - x * jnp.mean(up * x, axis=1, keepdims=True))


class Refs:
    def __init__(self, **refs):
        self.__dict__.update(refs)


SAVED = ("qkv", "rinv", "mixed", "xhat1", "rr", "firstb", "act", "slope", "xhat2")
WEIGHTS = ("win", "wout", "wid", "nar")


class Compute:
    def __init__(self, v, a, sems, section, valid, cls_at):
        self.v, self.a, self.sems = v, a, sems
        self.section, self.valid, self.cls_at = section, valid, cls_at
        self.length, self.width = v.h.shape
        self.ff = v.wid.shape[1]

    def piece(self, name, q):
        i = WEIGHTS.index(name)
        source, target = self.a.own[i].at[0], getattr(self.v, name)
        if name == "wid":
            at = lanes(q * self.width, self.width)
            return source.at[:, at], target.at[:, at], 2 + q
        if name == "nar":
            at = rows_of(q, self.width)
            return source.at[at, :], target.at[at, :], 6 + q
        return source, target, i

    def pieces(self, name):
        return self.ff // self.width if name in ("wid", "nar") else 1

    def weight_copy(self, name, q):
        source, target, i = self.piece(name, q)
        return pltpu.make_async_copy(source, target, self.sems.weights.at[i])

    def weight_sent(self, name, q):
        source, target, i = self.piece(name, q)
        return pltpu.make_async_remote_copy(
            src_ref=source, dst_ref=target, send_sem=self.sems.sent.at[i], recv_sem=self.sems.arrived.at[i],
            device_id=self.a.other, device_id_type=MESH,
        )

    def start_weight(self, layer, name, use, q=None):
        i = WEIGHTS.index(name)

        @pl.when(self.section == layer)
        def _():
            some = range(self.pieces(name)) if q is None else (q,)
            for p in some:
                self.weight_copy(name, p).start()
            if use > 0:
                pl.semaphore_wait(self.sems.free.at[i], 1)
            for p in some:
                if use == 2:
                    self.weight_sent(name, p).wait_send()
                self.weight_sent(name, p).start()

        if use > 0:

            @pl.when(self.section != layer)
            def _():
                pl.semaphore_signal(self.sems.free.at[i], inc=1, device_id=self.a.other, device_id_type=MESH)

    def wait_piece(self, layer, name, q):
        pl.when(self.section == layer)(lambda: self.weight_copy(name, q).wait())
        pl.when(self.section != layer)(lambda: self.weight_sent(name, q).wait_recv())

    def wait_weight(self, layer, name):
        for q in range(self.pieces(name)):
            self.wait_piece(layer, name, q)

    def saving(self, name):
        i = SAVED.index(name)
        return pltpu.make_async_copy(getattr(self.v, name), self.a.saved[i], self.sems.saved.at[i])

    def restoring(self, name):
        i = SAVED.index(name)
        return pltpu.make_async_copy(self.a.saved[i], getattr(self.v, name), self.sems.saved.at[i])

    def load_input(self, layer_input):
        return pltpu.make_async_copy(layer_input.at[self.rows()], self.v.h, self.sems.h.at[0])

    def load_cotangent(self, cotangent):
        return pltpu.make_async_copy(cotangent.at[self.rows()], self.v.g, self.sems.h.at[1])

    def rows(self):
        return pl.ds(pl.multiple_of(self.section * self.length, self.length), self.length)

    def e_store(self, layer, p, slot):
        return pltpu.make_async_copy(
            self.v.e.at[slot], self.a.e.at[layer, pl.ds(2 * p, 2)], self.sems.e.at[slot]
        )

    def e_load(self, layer, p, slot):
        return pltpu.make_async_copy(
            self.a.e.at[layer, pl.ds(2 * p, 2)], self.v.e.at[slot], self.sems.e.at[slot]
        )

    def e_drain(self, layer):
        for slot in range(2):
            self.e_store(layer, 0, slot).wait()

    def forward(self, layer, small):
        v, width = self.v, self.width
        vec = v.vec.at[layer]
        again = layer == 1

        def before(*names):
            if again:
                for name in names:
                    self.saving(name).wait()

        def done(*names):
            if not again:
                for name in names:
                    self.saving(name).start()

        self.wait_weight(layer, "win")
        before("qkv")
        for part in range(3):
            shift = [vec[0:1, :], None, vec[1:2, :]][part]
            for j in range(width // TILE):
                at = part * width + j * TILE
                got = mm(v.h[...], v.win[:, at : at + TILE])
                if shift is not None:
                    got = got + shift[:, j * TILE : (j + 1) * TILE]
                got = got.astype(BF16)
                if part == 0:
                    got = got * BF16(HEAD_DIM**-0.5)
                v.qkv[:, at : at + TILE] = got
        done("qkv")
        if again:
            self.e_drain(0)
        else:
            self.start_weight(1, "win", 1)
        before("rinv", "mixed")
        low = lax.broadcasted_iota(jnp.int32, (self.length, 128), 1) < HEAD_DIM
        ones = jnp.ones((self.length, 128), BF16)

        def pair(p, carry):
            slot = lax.rem(p, 2)

            @pl.when(p >= 2)
            def _():
                self.e_store(layer, p, slot).wait()

            q = v.qkv[:, lanes(p * 128, 128)]
            k = v.qkv[:, lanes(width + p * 128, 128)]
            values = jnp.concatenate([v.qkv[:, lanes(2 * width + p * 128, 128)], ones], axis=1)
            outs = []
            for i in range(2):
                qm = jnp.where(low if i == 0 else ~low, q, BF16(0))
                s = mm_right_t(qm, k) + v.bias[...]
                top = jnp.max(s, axis=1, keepdims=True)
                e = jnp.exp(s - top).astype(BF16)
                v.e[slot, i] = e
                outs.append(mm(e, values))
            self.e_store(layer, p, slot).start()
            r0 = 1.0 / outs[0][:, 128:]
            r1 = 1.0 / outs[1][:, 128:]
            m = jnp.where(low, outs[0][:, :128] * r0, outs[1][:, :128] * r1)
            v.mixed[:, lanes(p * 128, 128)] = m.astype(BF16)
            v.rinv[:, lanes(p * 128, 128)] = jnp.where(low, r0, r1)
            return carry

        lax.fori_loop(0, HEADS // 2, pair, 0)
        done("rinv", "mixed")

        self.wait_weight(layer, "wout")
        before("xhat1", "rr", "firstb")

        def mask(b):
            place = lax.broadcasted_iota(jnp.int32, (BLOCK, 1), 0) + b * BLOCK
            return (place < self.valid).astype(F32)

        def norm_first(b, total):
            rows = rows_of(b, BLOCK)
            branch = mm(v.mixed[rows, :], v.wout[...]) + vec[2:3, :]
            u = v.h[rows, :].astype(F32) + branch
            c = u - jnp.mean(u, axis=1, keepdims=True)
            f = lax.rsqrt(jnp.mean(c * c, axis=1, keepdims=True) + EPSILON)
            x = c * f
            v.xhat1[rows, :] = x
            v.rr[0, rows, :] = jnp.broadcast_to(f, (BLOCK, 128))
            y = x * vec[3:4, :] + vec[5:6, :]
            v.first[rows, :] = y
            v.firstb[rows, :] = y.astype(BF16)
            return total + jnp.sum(mask(b) * branch * branch, axis=0, keepdims=True)

        zero = jnp.zeros((1, width), F32)
        blocks = self.length // BLOCK
        branch_sum = lax.fori_loop(0, blocks, norm_first, zero)
        done("xhat1", "firstb")
        if not again:
            self.start_weight(1, "wout", 1)

        before("act", "slope")
        v.feed[...] = jnp.broadcast_to(vec[11:12, :], v.feed.shape)

        def widen(j):
            at = lanes(j * width, width)
            hid = mm(v.firstb[...], v.wid[:, at]) + vec[pl.ds(7 + j, 1), :]
            a, d = gelu_and_slope(hid)
            v.act[:, at] = a.astype(BF16)
            v.slope[:, at] = d.astype(BF16)

        def narrow(j):
            v.feed[...] += mm(v.act[:, lanes(j * width, width)], v.nar[rows_of(j, width), :])

        self.wait_piece(layer, "wid", 0)
        widen(0)

        def ffn(j, carry):
            self.wait_piece(layer, "wid", j)
            self.wait_piece(layer, "nar", j - 1)
            narrow(j - 1)
            widen(j)
            return carry

        parts = self.ff // width
        lax.fori_loop(1, parts, ffn, 0)
        done("act", "slope")
        self.wait_piece(layer, "nar", parts - 1)
        narrow(parts - 1)
        if not again:
            self.start_weight(1, "wid", 1)
            self.start_weight(1, "nar", 1)
        before("xhat2")

        def norm_second(b, totals):
            rows = rows_of(b, BLOCK)
            fd = v.feed[rows, :]
            u = v.first[rows, :] + fd
            c = u - jnp.mean(u, axis=1, keepdims=True)
            f = lax.rsqrt(jnp.mean(c * c, axis=1, keepdims=True) + EPSILON)
            x = c * f
            v.xhat2[rows, :] = x
            v.rr[1, rows, :] = jnp.broadcast_to(f, (BLOCK, 128))
            y = x * vec[4:5, :] + vec[6:7, :]
            v.first[rows, :] = y
            if not again:
                v.h[rows, :] = y.astype(BF16)
            ok = mask(b)
            return (
                totals[0] + jnp.sum(ok * u * u, axis=0, keepdims=True),
                totals[1] + jnp.sum(ok * fd * fd, axis=0, keepdims=True),
            )

        stream_sum, feed_sum = lax.fori_loop(0, blocks, norm_second, (zero, zero))
        done("xhat2", "rr")
        for i in range(8):
            small[i : i + 1, :] = v.first[pl.ds(self.cls_at[i], 1), :]
        small[8:9, :] = stream_sum
        small[9:10, :] = branch_sum
        small[10:11, :] = feed_sum
        small[11:12, :] = jnp.full((1, width), self.valid.astype(F32))
        small[12:16, :] = jnp.zeros((4, width), F32)

    def wait_saved(self, restored, *names):
        if restored:
            for name in names:
                if name in WEIGHTS:
                    self.wait_weight(0, name)
                else:
                    self.restoring(name).wait()

    def restore(self, *names):
        for name in names:
            if name in WEIGHTS:
                self.start_weight(0, name, 2)
            else:
                self.restoring(name).start()

    def send_out(self, stage, shift, n, value, target):
        slot = lax.rem(n, 2)

        @pl.when(n >= 2)
        def _():
            pltpu.make_async_copy(stage.at[slot], target, self.sems.stage.at[shift + slot]).wait()

        stage[slot] = value.astype(BF16)
        pltpu.make_async_copy(stage.at[slot], target, self.sems.stage.at[shift + slot]).start()

    def put_rows(self, n, value, target):
        self.send_out(self.v.row_stage, 0, n, value, target)

    def put_cols(self, n, value, target):
        self.send_out(self.v.col_stage, 2, n, value, target)

    def drain_rows(self, grad):
        for slot in range(2):
            pltpu.make_async_copy(self.v.row_stage.at[slot], grad.at[0, 0:TILE, :], self.sems.stage.at[slot]).wait()

    def drain_cols(self, grad):
        for slot in range(2):
            pltpu.make_async_copy(
                self.v.col_stage.at[slot], grad.at[0, :, 0:TILE], self.sems.stage.at[2 + slot]
            ).wait()

    def norms(self, vec, source, x_ref, f_at, gain, target, target_b, where):
        v = self.v
        zero = jnp.zeros((1, self.width), F32)

        def body(b, total):
            rows = rows_of(b, BLOCK)
            up = source[rows, :].astype(F32)
            x = x_ref[rows, :]
            d = norm_back(up * vec[gain : gain + 1, :], x, v.rr[f_at, rows, 0:1])
            target[rows, :] = d
            db = d.astype(BF16)
            target_b[rows, :] = db
            return (
                total[0] + jnp.sum(up * x, axis=0, keepdims=True),
                total[1] + jnp.sum(up, axis=0, keepdims=True),
                total[2] + jnp.sum(db.astype(F32), axis=0, keepdims=True),
            )

        got = lax.fori_loop(0, self.length // BLOCK, body, (zero, zero, zero))
        for i in range(3):
            v.sums[where + i : where + i + 1, :] = got[i]

    def din_kept(self, source):
        return pltpu.make_async_copy(source, self.a.din_kept, self.sems.h.at[2])

    def din_sent(self, source):
        return pltpu.make_async_remote_copy(
            src_ref=source, dst_ref=self.a.din_got, send_sem=self.sems.din.at[0], recv_sem=self.sems.din.at[1],
            device_id=self.a.other, device_id_type=MESH,
        )

    def backward(self, layer, grad, small):
        v, width, restored = self.v, self.width, layer == 0
        vec = v.vec.at[layer]
        dh, dqkv, dbr, dres, ds = v.slope, v.qkv, v.g, v.feed, v.first

        def second():
            self.wait_saved(restored, "xhat2", "rr")
            self.norms(vec, v.g, v.xhat2, 1, 4, ds, v.dfeed, 0)
            self.wait_saved(restored, "nar", "act", "slope", "firstb")

        def ffn(low, i, carry):
            at = lanes(i * 2 * TILE, 2 * TILE)
            da = mm_right_t(v.dfeed[...], v.nar[at, :])
            d = (v.slope[:, at].astype(F32) * da).astype(BF16)
            dh[:, at] = d
            d_narrow = mm_left_t(v.act[:, at], v.dfeed[...])
            d_widen = mm_left_t(v.firstb[...], d)
            d_bias = jnp.sum(d.astype(F32), axis=0, keepdims=True)
            for half in range(2):
                j, part = 2 * i + half, slice(half * TILE, (half + 1) * TILE)
                place = lanes(lax.rem(j, 3) * TILE, TILE)
                v.wbias[pl.ds(j, 1), :] = d_bias[:, part]
                self.put_rows(j - low, d_narrow[part, :], grad.at[2 * (j // 3), place, :])
                self.put_cols(j - low, d_widen[:, part], grad.at[2 * (j // 3) + 1, :, place])
            return carry

        def tiles(low, high):
            lax.fori_loop(low // 2, high // 2, functools.partial(ffn, low), 0)

        def first_grad():
            self.wait_saved(restored, "wid")

            def body(j, carry):
                at = lanes(j * TILE, TILE)
                ds[:, at] = ds[:, at] + mm_right_t(dh[...], v.wid[at, :])
                return carry

            lax.fori_loop(0, width // TILE, body, 0)

        def first():
            self.wait_saved(restored, "xhat1")
            self.norms(vec, ds, v.xhat1, 0, 3, dres, dbr, 3)

        def out_grad():
            self.wait_saved(restored, "mixed", "wout", "rinv", "qkv")

            def body(j, carry):
                at = lanes(j * TILE, TILE)
                self.put_cols(j, mm_left_t(v.mixed[...], dbr[:, at]), grad.at[OUT, :, at])
                d = mm_right_t(dbr[...], v.wout[at, :]).astype(BF16).astype(F32)
                v.dm[:, at] = (d * v.rinv[:, at]).astype(BF16)
                return carry

            lax.fori_loop(0, width // TILE, body, 0)

        def pair(p, carry):
            low = lax.broadcasted_iota(jnp.int32, (self.length, 128), 1) < HEAD_DIM
            slot = lax.rem(p, 2)

            @pl.when(p + 1 < HEADS // 2)
            def _():
                self.e_load(layer, p + 1, 1 - slot).start()

            at_q, at_k, at_v = lanes(p * 128, 128), lanes(width + p * 128, 128), lanes(2 * width + p * 128, 128)
            q, k, values = v.qkv[:, at_q], v.qkv[:, at_k], v.qkv[:, at_v]
            d = v.dm[:, at_q]
            prod = d.astype(F32) * v.mixed[:, at_q].astype(F32)
            self.e_load(layer, p, slot).wait()
            dq, dk, dv = [], [], []
            for i in range(2):
                mine = low if i == 0 else ~low
                delta = jnp.sum(jnp.where(mine, prod, 0.0), axis=1, keepdims=True)
                dp = mm_right_t(jnp.where(mine, d, BF16(0)), values)
                e = v.e[slot, i]
                s = (e.astype(F32) * (dp - delta)).astype(BF16)
                dq.append(mm(s, k))
                dk.append(mm_left_t(s, q))
                dv.append(mm_left_t(e, d))
            dqkv[:, at_q] = (jnp.where(low, dq[0], dq[1]) * HEAD_DIM**-0.5).astype(BF16)
            dqkv[:, at_k] = jnp.where(low, dk[0], dk[1]).astype(BF16)
            dqkv[:, at_v] = jnp.where(low, dv[0], dv[1]).astype(BF16)
            return carry

        def pairs(low, high):
            lax.fori_loop(low, high, pair, 0)

        def in_grad(low, high):
            if restored:
                pl.when(low == 0)(lambda: self.load_input(self.a.hidden).wait())

            def body(j, carry):
                at = lanes(j * TILE, TILE)
                place = lanes(lax.rem(j, 3) * TILE, TILE)
                self.put_cols(j - low, mm_left_t(v.h[...], dqkv[:, at]), grad.at[IN + j // 3, :, place])
                return carry

            lax.fori_loop(low, high, body, 0)

        def input_grad():
            self.wait_saved(restored, "win")

            def body(j, carry):
                at = lanes(j * TILE, TILE)
                d = dres[:, at] + mm_right_t(dqkv[...], v.win[at, :])
                dres[:, at] = d
                if layer == 1:
                    v.g[:, at] = d.astype(BF16)
                return carry

            lax.fori_loop(0, width // TILE, body, 0)
            pl.when(self.section == layer)(lambda: self.din_kept(dres).start())
            pl.when(self.section != layer)(lambda: self.din_sent(dres).start())
            small[16:17, :] = jnp.sum(dqkv[:, 0:width].astype(F32), axis=0, keepdims=True)
            small[17:18, :] = jnp.sum(dqkv[:, 2 * width :].astype(F32), axis=0, keepdims=True)
            for i, source in enumerate((5, 3, 0, 4, 1)):
                small[18 + i : 19 + i, :] = v.sums[source : source + 1, :]
            for i in range(self.ff // TILE):
                small[23 + i // 3 : 24 + i // 3, (i % 3) * TILE : (i % 3 + 1) * TILE] = v.wbias[i : i + 1, :]
            small[27:28, :] = v.sums[2:3, :]
            small[28:32, :] = jnp.zeros((4, width), F32)

        def input_done():
            pl.when(self.section == layer)(lambda: self.din_kept(dres).wait())
            pl.when(self.section != layer)(lambda: self.din_sent(dres).wait_send())

        def tiles_done():
            self.drain_rows(grad)
            self.drain_cols(grad)

        return Refs(
            second=second, tiles=tiles, first_grad=first_grad, first=first, out_grad=out_grad, pairs=pairs, in_grad=in_grad,
            input_grad=input_grad, input_done=input_done, tiles_done=tiles_done,
            cols_done=lambda: self.drain_cols(grad),
        )


def sum_plan(devices, rows):
    side = round((devices / 2) ** (1 / 3))
    extents = [side, side, devices // (side * side)]
    axes, stride = [], 1
    for extent in extents:
        steps, step = [], 1
        while step < extent:
            steps.append(stride * step)
            step *= 2
        axes.append(steps)
        stride *= extent
    x, y, z = axes
    distances = x + y + z
    swaps = lambda order, active=None: [("swap", distance, active) for distance in order]
    unit = 256 if devices <= 16 else 128
    run = 5 * unit // 2
    count, over = rows // run, rows % run
    return [
        (0, unit, count + (over >= unit), swaps(y + x + z)),
        (unit, unit, count + (over >= 2 * unit), swaps(x + y + z)),
        (2 * unit, unit // 2, count, swaps(z + x + y)),
    ], distances, None


class Stage:
    def __init__(self, kind, rows, cols, send, to, recv, source, sent, got):
        self.kind, self.rows, self.cols = kind, rows, cols
        self.send, self.to, self.recv, self.source, self.sent, self.got = send, to, recv, source, sent, got


def message_shapes(unit, width, spec):
    rows, cols, shapes = unit // 2, width, []
    for i, (kind, arg, _) in enumerate(spec):
        if kind == "chain":
            if arg == 0:
                rows //= 2
        elif kind != "fold":
            if rows >= 32:
                rows //= 2
            elif cols == width:
                cols //= 2
            else:
                kind = "full"
        shapes.append((kind, rows, cols))
    return shapes


def build_stages(unit, width, spec, me, line):
    rows, cols = unit // 2, width
    row = col = me * 0
    if line is not None:
        stride, depth = line
        z = me // stride
    flag = lambda condition: condition.astype(jnp.int32)
    stages = []
    for kind, arg, active in spec:
        if kind == "fold":
            first, third = flag(z == arg), flag(z == arg + 1)
            send, recv = (z == arg) | (z == depth - 1 - arg), (z == arg + 1) | (z == depth - 2 - arg)
            place = (row, col)
            stages.append(Stage(
                kind, rows, cols, send, me + stride * (2 * first - 1), recv, me + stride * (1 - 2 * third), place, place
            ))
        elif kind == "chain":
            if arg == 0:
                rows //= 2
                base = row
            up, came = flag(z == arg), flag(z == arg + 1)
            send, recv = (z == arg) | (z == depth - 1 - arg), (z == arg + 1) | (z == depth - 2 - arg)
            stages.append(Stage(
                kind, rows, cols, send, me + stride * (2 * up - 1), recv, me + stride * (1 - 2 * came),
                (base + up * rows, col), (base + came * rows, col),
            ))
            if arg == depth - 2:
                row = base + flag(z == depth - 1) * rows
        else:
            if kind == "middle":
                bit, distance = flag(z >= depth // 2), stride
                active = "middle"
            else:
                bit, distance = lax.rem(me // arg, 2), arg
            if active == "middle":
                on = (z == depth // 2 - 1) | (z == depth // 2)
            elif active == "ends":
                on = (z == 0) | (z == depth - 1)
            else:
                on = None
            partner = me + distance * (1 - 2 * bit)
            sent = (row, col)
            kind = "swap"
            if rows >= 32:
                rows //= 2
                sent, row = (row + (1 - bit) * rows, col), row + bit * rows
            elif cols == width:
                cols //= 2
                sent, col = (row, col + (1 - bit) * cols), col + bit * cols
            else:
                kind = "full"
            stages.append(Stage(kind, rows, cols, on, partner, on, partner, sent, (row, col)))
    return stages


def when(condition, action):
    if condition is None:
        action()
    else:
        pl.when(condition)(action)


class GradientSum:
    def __init__(self, plan, distances, line, width, grads, out, buffers, sems):
        self.plan, self.distances, self.line, self.width, self.grads, self.out = plan, distances, line, width, grads, out
        self.run = sum(unit for _, unit, _, _ in plan)
        self.section, self.me = lax.axis_index("section"), lax.axis_index("dp")
        self.peer = (1 - self.section, self.me)
        self.parts = [build_stages(unit, width, spec, self.me, line) for _, unit, _, spec in plan]
        self.slots = [slots_of(spec) for _, _, _, spec in plan]
        self.total, self.other, self.recvs, self.fulls = buffers
        self.keep_sems, self.pair_sems, self.trade_sems, self.end_sems, self.send_sems, self.rs_sems, self.ag_sems = sems[:7]
        self.free, self.full_free = sems[7:]
        self.length = max(2 * count + 2 * len(spec) + 2 for _, _, count, spec in plan)

    def partner(self, distance):
        return (self.section, self.me + distance * (1 - 2 * lax.rem(self.me // distance, 2)))

    def barrier(self):
        barrier = pltpu.get_barrier_semaphore()
        for device in [self.peer] + [self.partner(distance) for distance in self.distances]:
            pl.semaphore_signal(barrier, inc=1, device_id=device, device_id_type=MESH)
        neighbours = []
        if self.line is not None:
            stride, depth = self.line
            z = self.me // stride
            neighbours = [(z > 0, -stride), (z < depth - 1, stride)]
        for there, distance in neighbours:

            @pl.when(there)
            def _(distance=distance):
                pl.semaphore_signal(
                    barrier, inc=1, device_id=(self.section, self.me + distance), device_id_type=MESH
                )

        pl.semaphore_wait(barrier, len(self.distances) + 1)
        for there, _ in neighbours:
            pl.when(there)(lambda: pl.semaphore_wait(barrier, 1))

    def slot(self, part, k):
        return lax.rem(k, self.slots[part])

    def stage_slot(self, part, k, s):
        return lax.rem(k, stage_slots_of(self.plan[part][3], s))

    def half_rows(self, ref, part, k, which):
        base, unit, count, _ = self.plan[part]
        row = base + lax.rem(k, count) * self.run + which * (unit // 2)
        return ref.at[row // self.width, pl.ds(pl.multiple_of(lax.rem(row, self.width), 16), unit // 2)]

    def load(self, part, k, source):
        slot = self.slot(part, k)
        return pltpu.make_async_copy(
            self.half_rows(source, part, k, self.section), self.total[part].at[slot], self.keep_sems[part].at[slot]
        )

    def trade(self, part, k, source):
        slot = self.slot(part, k)
        return pltpu.make_async_remote_copy(
            src_ref=self.half_rows(source, part, k, 1 - self.section), dst_ref=self.other[part].at[slot],
            send_sem=self.pair_sems[part].at[slot], recv_sem=self.trade_sems[part].at[slot],
            device_id=self.peer, device_id_type=MESH,
        )

    def keep(self, part, k):
        slot = self.slot(part, k)
        return pltpu.make_async_copy(
            self.other[part].at[slot], self.half_rows(self.out, part, k, self.section), self.keep_sems[part].at[slot]
        )

    def hand_over(self, part, k):
        slot = self.slot(part, k)
        return pltpu.make_async_remote_copy(
            src_ref=self.other[part].at[slot], dst_ref=self.half_rows(self.out, part, k, self.section),
            send_sem=self.pair_sems[part].at[slot], recv_sem=self.end_sems[part].at[slot],
            device_id=self.peer, device_id_type=MESH,
        )

    def view(self, ref, slot, stage, place):
        row, col = place
        at = pl.ds(pl.multiple_of(row, 16), stage.rows)
        if stage.cols == self.width:
            return ref.at[slot, at]
        return ref.at[slot, at, pl.ds(pl.multiple_of(col, 128), stage.cols)]

    def held(self, part, k, s, place):
        stages = self.parts[part]
        fulls = [i for i in range(s + 1) if stages[i].kind == "full"]
        if fulls:
            return self.fulls[part][fulls[-1]].at[self.slot(part, k)]
        return self.view(self.total[part], self.slot(part, k), stages[s], place)

    def reduce_copy(self, part, k, s, device):
        stage = self.parts[part][s]
        at = self.stage_slot(part, k, s)
        if stage.kind == "full":
            source = self.held(part, k, s - 1, self.parts[part][s - 1].got)
        else:
            source = self.view(self.total[part], self.slot(part, k), stage, stage.sent)
        return pltpu.make_async_remote_copy(
            src_ref=source, dst_ref=self.recvs[part][s].at[at],
            send_sem=self.send_sems[part][s].at[self.slot(part, k)], recv_sem=self.rs_sems[part][s].at[at],
            device_id=(self.section, device), device_id_type=MESH,
        )

    def gather_copy(self, part, k, s, device, place):
        stage = self.parts[part][s]
        ref = self.view(self.other[part], self.slot(part, k), stage, place)
        return pltpu.make_async_remote_copy(
            src_ref=ref, dst_ref=ref, send_sem=self.send_sems[part][s].at[self.slot(part, k)],
            recv_sem=self.ag_sems[part][s].at[self.stage_slot(part, k, s)],
            device_id=(self.section, device), device_id_type=MESH,
        )

    def start_reduce(self, part, k, s):
        stage = self.parts[part][s]

        def action():
            if stage.kind == "full":

                @pl.when(k >= stage_slots_of(self.plan[part][3], s))
                def _():
                    pl.semaphore_wait(self.full_free[part][s].at[0], 1)

            self.reduce_copy(part, k, s, stage.to).start()

        when(stage.send, action)

    def end_reduce(self, part, k, s):
        stage = self.parts[part][s]
        slot, at = self.slot(part, k), self.stage_slot(part, k, s)
        last = len(self.parts[part]) - 1

        def action():
            self.reduce_copy(part, k, s, stage.source).wait_recv()
            if stage.kind == "full":
                left = self.held(part, k, s - 1, self.parts[part][s - 1].got)
            else:
                left = self.view(self.total[part], slot, stage, stage.got)
            target = self.view(self.other[part], slot, stage, stage.got) if s == last else self.held(part, k, s, stage.got)
            self.add(target, left, self.recvs[part][s].at[at], stage.rows)
            if stage.kind == "full":

                @pl.when(k + stage_slots_of(self.plan[part][3], s) < 2 * self.plan[part][2])
                def _():
                    pl.semaphore_signal(
                        self.full_free[part][s].at[0], inc=1, device_id=(self.section, stage.source),
                        device_id_type=MESH,
                    )

        when(stage.recv, action)

    def start_gather(self, part, k, s):
        stage = self.parts[part][s]
        if stage.kind == "full":
            return
        when(stage.send, lambda: self.reduce_copy(part, k, s, stage.to).wait_send())
        when(stage.recv, lambda: self.gather_copy(part, k, s, stage.source, stage.got).start())

    def end_gather(self, part, k, s):
        stage = self.parts[part][s]
        if stage.kind != "full":
            when(stage.send, lambda: self.gather_copy(part, k, s, stage.to, stage.sent).wait_recv())

    def owned(self, part, k):
        return (k < self.plan[part][2]) == (self.section == 1)

    def add(self, target, left, right, rows):
        block = min(rows, 64)

        def body(i, carry):
            at = pl.ds(pl.multiple_of(i * block, 16), block)
            target[at, :] = left[at, :] + right[at, :]
            return carry

        lax.fori_loop(0, rows // block, body, 0)

    def retire(self, part, k):
        for s, stage in enumerate(self.parts[part]):
            if stage.kind == "full":
                when(stage.send, lambda s=s, stage=stage: self.reduce_copy(part, k, s, stage.to).wait_send())
            else:
                when(stage.recv, lambda s=s, stage=stage: self.gather_copy(part, k, s, stage.source, stage.got).wait_send())
        mine = self.owned(part, k)
        pl.when(mine)(lambda: self.keep(part, k).wait())
        pl.when(jnp.logical_not(mine))(lambda: self.hand_over(part, k).wait_send())

    def task(self, part, k, s):
        last = len(self.parts[part]) - 1
        slots, count = self.slots[part], self.plan[part][2]
        if s == 0:

            @pl.when(k >= slots)
            def _():
                self.retire(part, k - slots)
                pl.semaphore_signal(self.free.at[part], inc=1, device_id=self.peer, device_id_type=MESH)
                pl.semaphore_wait(self.free.at[part], 1)

            first = k < count

            @pl.when(first)
            def _():
                self.load(part, k, self.grads[1]).start()
                self.trade(part, k, self.grads[1]).start()

            @pl.when(jnp.logical_not(first))
            def _():
                self.load(part, k, self.grads[0]).start()
                self.trade(part, k, self.grads[0]).start()

        elif s == 1:
            self.load(part, k, self.grads[0]).wait()
            self.trade(part, k, self.grads[0]).wait_recv()
            total = self.total[part].at[self.slot(part, k)]
            self.add(total, total, self.other[part].at[self.slot(part, k)], self.plan[part][1] // 2)
            self.start_reduce(part, k, 0)
        elif s <= last + 2:
            self.end_reduce(part, k, s - 2)
            if s - 1 <= last:
                self.start_reduce(part, k, s - 1)
            else:
                self.start_gather(part, k, last)
        elif s <= 2 * last + 3:
            j = 2 * last + 3 - s
            self.end_gather(part, k, j)
            if j > 0:
                self.start_gather(part, k, j - 1)
            else:
                self.trade(part, k, self.grads[0]).wait_send()
                mine = self.owned(part, k)
                pl.when(mine)(lambda: self.keep(part, k).start())
                pl.when(jnp.logical_not(mine))(lambda: self.hand_over(part, k).start())
        else:
            pl.when(self.owned(part, k))(lambda: self.hand_over(part, k).wait_recv())

    def step(self, t):
        most = max(len(stages) for stages in self.parts)
        for s in range(2 * most + 3):
            for part, (_, _, count, spec) in enumerate(self.plan):
                if s < 2 * len(spec) + 3:
                    k = t - s
                    pl.when((k >= 0) & (k < 2 * count))(lambda part=part, s=s, k=k: self.task(part, k, s))

    def finish(self):
        for part, (_, _, count, _) in enumerate(self.plan):

            def body(k, carry, part=part):
                self.retire(part, k)
                return carry

            lax.fori_loop(max(2 * count - self.slots[part], 0), 2 * count, body, 0)


def slots_of(spec):
    return 2 * len(spec) + 3


def stage_slots_of(spec, s):
    return 2 * (len(spec) - s) + 1


def sum_scratch(plan, width):
    shapes, names = [], []

    def need(name, part, s, shape):
        names.append((name, part, s))
        shapes.append(shape)

    for part, (_, unit, _, spec) in enumerate(plan):
        slots = slots_of(spec)
        steps = message_shapes(unit, width, spec)
        for name in ("total", "other"):
            need(name, part, 0, pltpu.VMEM((slots, unit // 2, width), BF16))
        for name in ("keep", "pair", "trade", "end"):
            need(name, part, 0, pltpu.SemaphoreType.DMA((slots,)))
        for s, (kind, rows, cols) in enumerate(steps):
            at = stage_slots_of(spec, s)
            need("recv", part, s, pltpu.VMEM((at, rows, cols), BF16))
            need("send", part, s, pltpu.SemaphoreType.DMA((slots,)))
            need("rs", part, s, pltpu.SemaphoreType.DMA((at,)))
            if kind == "full":
                need("full_free", part, s, pltpu.SemaphoreType.REGULAR((1,)))
                if s < len(steps) - 1:
                    need("full", part, s, pltpu.VMEM((slots, rows, cols), BF16))
            else:
                need("ag", part, s, pltpu.SemaphoreType.DMA((at,)))
    need("free", 0, 0, pltpu.SemaphoreType.REGULAR((len(plan),)))

    def split(refs):
        by_name = {}
        for (name, part, s), ref in zip(names, refs):
            by_name.setdefault(name, {}).setdefault(part, {})[s] = ref
        one = lambda name: [by_name[name][part][0] for part in range(len(plan))]
        many = lambda name: [by_name.get(name, {}).get(part, {}) for part in range(len(plan))]
        buffers = (one("total"), one("other"), many("recv"), many("full"))
        sems = (
            one("keep"), one("pair"), one("trade"), one("end"), many("send"), many("rs"), many("ag"),
            by_name["free"][0][0], many("full_free"),
        )
        return buffers, sems

    return shapes, split


def layers_kernel(plan, distances, line, split, *refs):
    refs = list(refs)
    take = lambda n: [refs.pop(0) for _ in range(n)]
    valid_ref, cls_ref, seg_ref, proj_bias, out_shift, gains, shifts, widen_bias, narrow_bias = take(9)
    hidden, cotangent = take(2)
    own = take(4)
    out, din_kept, din_got, small_got, small_sum, small_mine = take(6)
    grad0, grad1, e_hbm = take(3)
    saved = take(9)
    v = Refs(**dict(zip(VMEM_NAMES, take(len(VMEM_NAMES)))))
    small_send, small_acc, small_recv = take(3)
    weight_sems, sent_sems, arrived_sems, free_sems, saved_sems, e_sems, h_sems, stage_sems, vec_sems, small_sems = take(10)
    din_sems, = take(1)
    section = lax.axis_index("section")
    width = v.h.shape[1]
    total = GradientSum(plan, distances, line, width, (grad0, grad1), out, *split(refs))
    compute = Compute(
        v,
        Refs(own=own, other=total.peer, saved=saved, e=e_hbm, hidden=hidden, din_kept=din_kept, din_got=din_got),
        Refs(
            weights=weight_sems, sent=sent_sems, arrived=arrived_sems, free=free_sems, saved=saved_sems, e=e_sems, h=h_sems,
            stage=stage_sems, din=din_sems,
        ),
        section, valid_ref[section], [cls_ref[section, i] for i in range(8)],
    )

    def vec_sent():
        return pltpu.make_async_remote_copy(
            src_ref=v.vec_own, dst_ref=v.vec_peer, send_sem=vec_sems.at[0], recv_sem=vec_sems.at[1],
            device_id=total.peer, device_id_type=MESH,
        )

    compute.load_input(hidden).start()
    v.vec_own[0:2, :] = proj_bias[0]
    v.vec_own[2:3, :] = out_shift[...]
    v.vec_own[3:5, :] = gains[0]
    v.vec_own[5:7, :] = shifts[0]
    for i in range(4):
        v.vec_own[7 + i : 8 + i, :] = widen_bias[:, i * width : (i + 1) * width]
    v.vec_own[11:12, :] = narrow_bias[...]
    v.vec_own[12:16, :] = jnp.zeros((4, width), F32)
    total.barrier()
    vec_sent().start()
    compute.start_weight(0, "win", 0)
    compute.start_weight(0, "wout", 0)
    for q in range(compute.pieces("wid")):
        compute.start_weight(0, "wid", 0, q)
        compute.start_weight(0, "nar", 0, q)
    segments = seg_ref[pl.ds(section, 1), :]
    columns = jnp.broadcast_to(segments.astype(F32), (128, compute.length)).T[:, :1]
    v.bias[...] = jnp.where(columns == segments.astype(F32), 0.0, MASKED)
    compute.load_cotangent(cotangent).start()
    vec_sent().wait_recv()
    for layer in range(2):
        v.vec[layer] = jnp.where(section == layer, v.vec_own[...], v.vec_peer[...])
    compute.load_input(hidden).wait()

    small0, small1 = v.small.at[0], v.small.at[1]
    compute.forward(0, small0)
    compute.forward(1, small1)
    compute.e_drain(1)
    compute.e_load(1, 0, 0).start()
    compute.load_cotangent(cotangent).wait()

    rounds = len(distances)

    def small_trade():
        return pltpu.make_async_remote_copy(
            src_ref=small_send, dst_ref=small_got, send_sem=small_sems.at[0, rounds], recv_sem=small_sems.at[1, rounds],
            device_id=total.peer, device_id_type=MESH,
        )

    def small_copy(i):
        return pltpu.make_async_remote_copy(
            src_ref=small_acc.at[i], dst_ref=small_recv.at[i], send_sem=small_sems.at[0, i],
            recv_sem=small_sems.at[1, i], device_id=total.partner(distances[i]), device_id_type=MESH,
        )

    def small_start():
        small_mine[...] = jnp.where(section == 0, small0[...], small1[...])
        small_send[...] = jnp.where(section == 0, small1[...], small0[...])
        small_trade().start()

    def small_step(stage):
        if stage == 0:
            small_trade().wait_recv()
            small_acc[0] = small_mine[8:, :] + small_got[8:, :]
        else:
            small_copy(stage - 1).wait_recv()
            small_acc[stage] = small_acc[stage - 1] + small_recv[stage - 1]
        if stage < rounds:
            small_copy(stage).start()
        else:
            small_sum[...] = small_acc[stage]

    one = compute.backward(1, grad1, small1)
    zero = compute.backward(0, grad0, small0)
    restore = compute.restore
    def tiles_of(layer, first):
        def action(t):
            begin = t == first
            pl.when(t > first)(layer.tiles_done)
            number = jnp.clip(t - first, 0, 4)
            layer.tiles(jnp.where(begin, 0, 2 + 2 * number), 4 + 2 * number)

        return first, first + 4, action

    def pairs_of(layer, first):
        def action(t):
            pl.when(t == first)(layer.cols_done)
            number = jnp.clip(t - first, 0, 2)
            layer.pairs(2 * number, 2 * number + 2)

        return first, first + 2, action

    def in_grad_of(layer, first, drained=0):
        def action(t):
            begin = t == first
            pl.when(t > first + drained)(layer.cols_done)
            layer.in_grad(jnp.where(begin, 0, 5), jnp.where(begin, 5, 9))

        return first, first + 1, action

    def at(t, *actions):
        def action(_):
            for act in actions:
                act()

        return t, t, action

    def later_tiles(t):
        pl.when(t > 0)(one.tiles_done)
        number = jnp.clip(t, 0, 3)
        one.tiles(4 + 2 * number, 6 + 2 * number)

    do = functools.partial
    one.second()
    one.tiles(0, 4)
    one.tiles_done()
    events = [
        (0, 3, later_tiles),
        at(3, do(restore, "nar", "act", "firstb", "xhat2")),
        at(4, one.tiles_done, one.first_grad, do(restore, "slope", "wid")),
        at(5, one.first, do(restore, "xhat1", "rr"), one.out_grad, do(restore, "wout", "rinv")),
        pairs_of(one, 6),
        at(8, do(restore, "mixed"), lambda: compute.e_load(0, 0, 0).start()),
        in_grad_of(one, 9, 1),
        at(9, one.cols_done),
        at(10, lambda: compute.load_input(hidden).start()),
        at(11, one.cols_done, one.input_grad, do(restore, "qkv", "win"), zero.second),
        at(12, one.input_done),
        tiles_of(zero, 12),
        at(17, zero.tiles_done, zero.first_grad),
        at(18, zero.first, zero.out_grad),
        pairs_of(zero, 19),
        in_grad_of(zero, 22),
        at(24, zero.cols_done, zero.input_grad, small_start),
    ] + [at(25 + s, do(small_step, s)) for s in range(rounds + 1)]

    def body(t, carry):
        total.step(t)
        for first, last, action in events:
            pl.when((t >= first) & (t <= last))(lambda action=action: action(t))
        return carry

    lax.fori_loop(0, total.length, body, 0)
    total.finish()
    zero.input_done()
    vec_sent().wait_send()
    for name in WEIGHTS:
        for q in range(compute.pieces(name)):
            compute.weight_sent(name, q).wait_send()
    small_trade().wait_send()
    for i in range(rounds):
        small_copy(i).wait_send()
    compute.din_sent(v.feed).wait_recv()


VMEM_NAMES = (
    "h", "g", "win", "wout", "wid", "nar", "qkv", "e", "rinv", "mixed", "xhat1", "rr", "first", "firstb", "act", "slope",
    "xhat2", "feed", "bias", "dfeed", "dm", "row_stage", "col_stage", "wbias", "sums", "vec", "vec_own", "vec_peer", "small",
)


def layers(valid_counts, cls_positions, segment_ids, vectors, hidden, cotangent, own):
    rows, length = segment_ids.shape
    width, ff = hidden.shape[1], own[2].shape[2]
    devices = lax.axis_size("dp")
    plan, distances, line = sum_plan(devices, 12 * width)
    stages = len(distances)
    shapes, split = sum_scratch(plan, width)
    row_b, row_f = ((length, width), BF16), ((length, width), F32)
    saved = [
        ((length, 3 * width), BF16), row_f, row_b, row_f, ((2, length, 128), F32), row_b, ((length, ff), BF16),
        ((length, ff), BF16), row_f,
    ]
    grad = ((12, width, width), BF16)
    small = ((32, width), F32)
    sums = (24, width)
    outs = [grad, row_f, row_f, small, (sums, F32), small, grad, grad, ((2, HEADS, length, length), BF16), *saved]
    scratch = dict(
        h=row_b, g=row_b, win=(own[0].shape[1:], BF16), wout=(own[1].shape[1:], BF16), wid=(own[2].shape[1:], BF16),
        nar=(own[3].shape[1:], BF16), qkv=saved[0], e=((2, 2, length, length), BF16), rinv=row_f, mixed=row_b, xhat1=row_f,
        rr=saved[4], first=row_f, firstb=row_b, act=saved[6], slope=saved[7], xhat2=row_f, feed=row_f,
        bias=((length, length), F32), dfeed=row_b, dm=row_b, row_stage=((2, TILE, width), BF16),
        col_stage=((2, width, TILE), BF16), wbias=((16, TILE), F32), sums=((8, width), F32), vec=((2, 16, width), F32),
        vec_own=((16, width), F32), vec_peer=((16, width), F32), small=((2, 32, width), F32),
    )
    in_vmem = (3, 4, 5)
    got = pl.pallas_call(
        functools.partial(layers_kernel, plan, distances, line, split),
        out_shape=[jax.ShapeDtypeStruct(s, d) for s, d in outs],
        in_specs=[SMEM, SMEM] + [VMEM] * 7 + [ANY] * 6,
        out_specs=[VMEM if i in in_vmem else ANY for i in range(len(outs))],
        scratch_shapes=[
            *[pltpu.VMEM(*scratch[name]) for name in VMEM_NAMES],
            pltpu.VMEM(*small),
            pltpu.VMEM((stages + 1, *sums), F32),
            pltpu.VMEM((stages, *sums), F32),
            pltpu.SemaphoreType.DMA((10,)),
            pltpu.SemaphoreType.DMA((10,)),
            pltpu.SemaphoreType.DMA((10,)),
            pltpu.SemaphoreType.REGULAR((4,)),
            pltpu.SemaphoreType.DMA((9,)),
            pltpu.SemaphoreType.DMA((2,)),
            pltpu.SemaphoreType.DMA((3,)),
            pltpu.SemaphoreType.DMA((4,)),
            pltpu.SemaphoreType.DMA((2,)),
            pltpu.SemaphoreType.DMA((2, stages + 1)),
            pltpu.SemaphoreType.DMA((2,)),
            *shapes,
        ],
        compiler_params=pltpu.CompilerParams(collective_id=0, has_side_effects=True, vmem_limit_bytes=63 * MIB),
        cost_estimate=pl.CostEstimate(flops=54 * 10**9, bytes_accessed=200 * 10**6, transcendentals=10**7),
        name="layers_and_sum",
    )(valid_counts, cls_positions, segment_ids, *vectors, hidden, cotangent, *own)
    return got[:6]


def finish_kernel(
    flags, blocks, din_kept, din_got, small_mine, small_got, small_sum,
    cls_o, input_o, in_o, bias_o, out_o, out_shift_o, gain_o, shift_o, widen_o, widen_bias_o, narrow_o, narrow_bias_o, rms_o,
    dins, halves, wide, block_sems, din_sems, wide_sems,
):
    section = flags[0]
    got_row = 1 - section
    length, width = din_got.shape
    slots = wide.shape[0]

    def rows(row):
        return input_o.at[0, pl.ds(pl.multiple_of(row * length, 16), length)]

    def target(index):
        part = slice(index // 2 * width, (index // 2 + 1) * width)
        if index >= IN:
            return in_o.at[0, :, (index - IN) * width : (index - IN + 1) * width]
        if index == OUT:
            return out_o.at[0]
        return narrow_o.at[0, part, :] if index % 2 == 0 else widen_o.at[0, :, part]

    loads = [pltpu.make_async_copy(blocks.at[i], halves.at[i], block_sems.at[i]) for i in range(12)]
    stores = [pltpu.make_async_copy(wide.at[i % slots], target(i), wide_sems.at[i % slots]) for i in range(12)]
    din_loads = [pltpu.make_async_copy(din, dins.at[i], din_sems.at[i]) for i, din in enumerate((din_kept, din_got))]
    din_stores = [
        pltpu.make_async_copy(dins.at[i], rows(row), din_sems.at[i]) for i, row in enumerate((section, got_row))
    ]
    for copy in loads[:2] + din_loads + loads[2:]:
        copy.start()
    cls_o[0, section] = small_mine[0:8, :]
    cls_o[0, got_row] = small_got[0:8, :]
    bias_o[0] = small_sum[8:10, :]
    out_shift_o[...] = small_sum[10:11, :]
    gain_o[0] = small_sum[11:13, :]
    shift_o[0] = small_sum[13:15, :]
    for i in range(4):
        widen_bias_o[0:1, i * width : (i + 1) * width] = small_sum[15 + i : 16 + i, :]
    narrow_bias_o[...] = small_sum[19:20, :]
    for i in range(3):
        squares = jnp.sum(small_sum[i : i + 1, :], axis=1, keepdims=True)
        rms_o[0:1, i : i + 1] = jnp.sqrt(squares / (small_sum[3:4, 0:1] * width))

    for i in range(12):
        loads[i].wait()
        if i >= slots:
            stores[i - slots].wait()

        def widen_rows(b, carry, i=i):
            at = rows_of(b, 64)
            wide[i % slots, at, :] = halves[i, at, :].astype(F32)
            return carry

        lax.fori_loop(0, width // 64, widen_rows, 0)
        stores[i].start()
        if i == 1:
            for load, store in zip(din_loads, din_stores):
                load.wait()
                store.start()
    for copy in stores[12 - slots :] + din_stores:
        copy.wait()


def finish(section, blocks, din_kept, din_got, small_mine, small_got, small_sum):
    length, width = din_got.shape
    shapes = [
        (1, 2, 8, width), (1, 2 * length, width), (1, width, 3 * width), (1, 2, width), (1, width, width), (1, width),
        (1, 2, width), (1, 2, width), (1, width, 4 * width), (1, 4 * width), (1, 4 * width, width), (1, width), (1, 3),
    ]
    big = (1, 2, 4, 8, 10)
    return pl.pallas_call(
        finish_kernel,
        out_shape=[jax.ShapeDtypeStruct(s, F32) for s in shapes],
        in_specs=[SMEM] + [ANY] * 3 + [VMEM] * 3,
        out_specs=[ANY if i in big else VMEM for i in range(len(shapes))],
        scratch_shapes=[
            pltpu.VMEM((2, length, width), F32),
            pltpu.VMEM(blocks.shape, BF16),
            pltpu.VMEM((6, width, width), F32),
            pltpu.SemaphoreType.DMA((12,)),
            pltpu.SemaphoreType.DMA((2,)),
            pltpu.SemaphoreType.DMA((6,)),
        ],
        compiler_params=pltpu.CompilerParams(vmem_limit_bytes=63 * MIB),
        cost_estimate=pl.CostEstimate(flops=10**7, bytes_accessed=46 * 10**6, transcendentals=0),
        name="finish",
    )(section[None], blocks, din_kept, din_got, small_mine, small_got, small_sum)


def local(
    hidden_in, segment_ids, cls_positions, valid_counts, proj_in, proj_bias, proj_out, out_shift, norm_gains,
    norm_shifts, widen, widen_bias, narrow, narrow_bias, cotangent,
):
    section = lax.axis_index("section")
    vectors = (proj_bias, out_shift, norm_gains, norm_shifts, widen_bias, narrow_bias)
    blocks, din_kept, din_got, small_got, small_sum, small_mine = layers(
        valid_counts, cls_positions, segment_ids, vectors, hidden_in, cotangent, (proj_in, proj_out, widen, narrow)
    )
    return finish(section, blocks, din_kept, din_got, small_mine, small_got, small_sum)


def solution(mesh):
    placed = (
        P("dp", None),
        P("dp", None),
        P("dp", None),
        P("dp"),
        P("section", None, None),
        P("section", None, None),
        P("section", None, None),
        P("section", None),
        P("section", None, None),
        P("section", None, None),
        P("section", None, None),
        P("section", None),
        P("section", None, None),
        P("section", None),
        P("dp", None),
    )
    return jax.shard_map(
        local,
        mesh=mesh,
        in_specs=placed,
        out_specs=(
            P("section", "dp", None, None),
            P("section", "dp", None),
            P("section", None, None),
            P("section", None, None),
            P("section", None, None),
            P("section", None),
            P("section", None, None),
            P("section", None, None),
            P("section", None, None),
            P("section", None),
            P("section", None, None),
            P("section", None),
            P("section", None),
        ),
        check_vma=False,
    )
```
